32 devices in a mesh: batch: 8 (over z, core), exp: 4 (over y, x).
Axes of the slice: x: 2, y: 2, z: 4, core: 2. Of those that a mesh axis runs over, the one named last changes fastest.
Arguments:
- layer_input: bfloat16 [32, 1024, 512], P(('batch', 'exp')), may hold values from -6 to 6
- memory: bfloat16 [32, 1024, 512], P(('batch', 'exp')), may hold values from -6 to 6
- routes: int32 [32, 8, 1], P(('batch', 'exp')), may hold values from 0 to 3; in each aligned block of 8 rows (0 to 7, 8 to 15, ..., all dimensions but the last counted through in order) at most 4 rows name the same one
- out_grad: bfloat16 [32, 1024, 512], P(('batch', 'exp')), may hold values from -6 to 6
- self_gain: float32 [512], replicated, may hold values from 0.25 to 1.75
- self_shift: float32 [512], replicated, may hold values from -3 to 3
- self_project: bfloat16 [512, 1536], replicated, may hold values from -0.375 to 0.375
- self_output: bfloat16 [512, 512], replicated, may hold values from -1.5 to 1.5
- cross_gain: float32 [512], replicated, may hold values from 0.25 to 1.75
- cross_shift: float32 [512], replicated, may hold values from -3 to 3
- cross_query: bfloat16 [512, 512], replicated, may hold values from -0.375 to 0.375
- cross_memory: bfloat16 [512, 1024], replicated, may hold values from -0.375 to 0.375
- cross_output: bfloat16 [512, 512], replicated, may hold values from -0.75 to 0.75
- moe_gain: float32 [512], replicated, may hold values from 0.25 to 1.75
- moe_shift: float32 [512], replicated, may hold values from -3 to 3
- expert_up: bfloat16 [4, 512, 2048], P('exp'), may hold values from -0.25 to 0.25
- up_bias: float32 [4, 2048], P('exp'), may hold values from -3 to 3
- expert_down: bfloat16 [4, 2048, 512], P('exp'), may hold values from -0.125 to 0.125
- down_bias: float32 [4, 512], P('exp'), may hold values from -2 to 2
Outputs:
- layer_output: bfloat16 [32, 1024, 512], P(('batch', 'exp'))
- grad_input: float32 [32, 1024, 512], P(('batch', 'exp'))
- grad_memory: float32 [32, 1024, 512], P(('batch', 'exp'))
- grad_self_gain: float32 [512], replicated
- grad_self_shift: float32 [512], replicated
- grad_self_project: float32 [512, 1536], replicated
- grad_self_output: float32 [512, 512], replicated
- grad_cross_gain: float32 [512], replicated
- grad_cross_shift: float32 [512], replicated
- grad_cross_query: float32 [512, 512], replicated
- grad_cross_memory: float32 [512, 1024], replicated
- grad_cross_output: float32 [512, 512], replicated
- grad_moe_gain: float32 [512], replicated
- grad_moe_shift: float32 [512], replicated
- grad_expert_up: float32 [4, 512, 2048], P('exp', 'batch')
- grad_up_bias: float32 [4, 2048], P('exp', 'batch')
- grad_expert_down: float32 [4, 2048, 512], P('exp', 'batch')
- grad_down_bias: float32 [4, 512], P('exp', 'batch')
The draws below stay inside these ranges and needn't reach their ends.
Inputs may be any that keep to these rules, and one draw needn't show every extreme that they name: `routes`: the 128 tokens of a group all go to the expert that the group's entry names; the 8 entries of one sequence name no expert more than 4 times.
All inputs are finite; a program needn't handle non-finite values.
Results may differ from the reference program's by a relative error of at most 0.02.
The reference program's roundings to bfloat16 on the way count: a program that leaves them out, or rounds other values in their place, can miss the bound.
Values may be sent and summed in bfloat16 or wider, within the bound.
A program may use at most 192 MiB of HBM per device.

```python
import math
import jax
import jax.numpy as jnp
import numpy as np
from jax import lax

D = 512
HEADS = 8
HEAD_DIM = 64
FF = 2048
SEQ = 1024
MEM = 1024
CAPACITY = 4
SEQS = 32
EXPERTS = 4
GROUPS = 8
GROUP_ROWS = 128


def levels(key, shape, shards, least, largest):
    level, own = 1.0, jax.random.fold_in(key, 6)
    for dim, parts in shards:
        steps = jnp.exp(jax.random.uniform(jax.random.fold_in(own, dim), (parts,), jnp.float32, least / len(shards), largest / len(shards)))
        level = level * jnp.repeat(steps, shape[dim] // parts).reshape([-1 if axis == dim else 1 for axis in range(len(shape))])
    return level


def deal_out(rng, own, number, rows, number_of, top, reach, slope):
    sequence = jax.random.permutation(rng, number_of)
    heavy_load, common = portions_of(number_of, rows * top, reach, slope, True), portions_of(number_of, rows * top, reach, slope, False)
    places = jnp.arange(number_of)

    def named(sizes, turn):
        used = int((sizes > 0).sum())
        fixed = max(1, used // 4)
        shifted = fixed + (places - fixed + turn * (used - fixed)) % max(1, number_of - fixed)
        return jnp.zeros((number_of,), jnp.int32).at[sequence[jnp.where(places < fixed, places, shifted)]].set(jnp.asarray(sizes, jnp.int32))

    sizes = jnp.where(number % 4 == 0, named(heavy_load, number // 4), named(common, number - number // 4 - 1))
    mixed = jax.random.permutation(jax.random.fold_in(own, 3), number_of)
    donor, sink = mixed[0:number_of // 2 * 2:2], mixed[1:number_of // 2 * 2:2]
    margin = jnp.minimum(sizes[donor] - 1, reach - sizes[sink]) // 2
    margin = jnp.where((donor == sequence[0]) | (sink == sequence[0]) | (sizes[sink] == 0), 0, jnp.maximum(margin, 0))
    shifted = jax.random.randint(jax.random.fold_in(own, 4), (number_of // 2,), 0, 1 << 20) % (margin + 1)
    sizes = sizes.at[donor].add(-shifted).at[sink].add(shifted)
    items = jnp.searchsorted(jnp.cumsum(sizes), jnp.arange(rows * top), side="right").astype(jnp.int32)
    grid = items.reshape(top, rows).T
    grid = grid[jax.random.permutation(jax.random.fold_in(own, 1), rows)]
    turn = jax.random.randint(jax.random.fold_in(own, 2), (rows, 1), 0, top)
    return jnp.take_along_axis(grid, (jnp.arange(top)[None, :] + turn) % top, axis=1)


def portions_of(amount, total, bound, skew, full):
    loads = [(1 << 20) // math.isqrt(grade ** skew) + 1 for grade in range(1, amount + 1)]
    largest = bound if full else min(bound, max(-(-total // amount), total * loads[0] // sum(loads)))
    least = 1 if total - largest >= amount - 1 else 0
    given, spare = [largest] + [least] * (amount - 1), total - largest - least * (amount - 1)
    while spare > 0:
        movable = [i for i in range(1, amount) if given[i] < largest] or [i for i in range(1, amount) if given[i] < bound]
        mass, left = sum([loads[i] for i in movable]), spare
        for i in movable:
            more = min(bound - given[i], max(1, left * loads[i] // mass), spare)
            given[i] = given[i] + more
            spare = spare - more
    return np.array(given)


def gaussian(key, shape, scale, limit, pieces=(), held_as=jnp.bfloat16):
    values = jax.random.normal(key, shape, jnp.float32) * scale
    if len(pieces) > 0:
        values = levels(key, shape, pieces, -0.22, 0.18) * values
    return jnp.clip(values, min=-limit, max=limit).astype(held_as)


def setup_inputs(seed: int = 0) -> dict:
    streams_of = jax.random.split(jax.random.key(seed), 20)
    layer_input = gaussian(streams_of[0], (SEQS, SEQ, D), 1.0, 6.0, ((0, 32),))
    memory = gaussian(streams_of[1], (SEQS, MEM, D), 1.0, 6.0, ((0, 32),))
    routes_keys = jax.random.split(jax.random.fold_in(streams_of[2], 1), SEQS * GROUPS // GROUPS)
    routes_turns = jax.random.permutation(jax.random.fold_in(streams_of[2], 3), SEQS * GROUPS // GROUPS)
    routes = jax.vmap(lambda own, number: deal_out(jax.random.fold_in(streams_of[2], 2), own, number, GROUPS, EXPERTS, 1, CAPACITY, 2))(routes_keys, routes_turns).reshape((SEQS, GROUPS, 1))
    out_grad = gaussian(streams_of[3], (SEQS, SEQ, D), 1.0, 6.0, ((0, 32),))
    self_gain = jnp.clip(1.0 + 0.15 * jax.random.normal(streams_of[4], (D,), jnp.float32), 0.25, 1.75)
    self_shift = gaussian(streams_of[5], (D,), 0.5, 3.0, (), jnp.float32)
    self_project = gaussian(streams_of[6], (D, 3 * D), (D // 2) ** -0.5, 0.375)
    self_output = gaussian(streams_of[7], (D, D), (D // 32) ** -0.5, 1.5)
    cross_gain = jnp.clip(1.0 + 0.15 * jax.random.normal(streams_of[8], (D,), jnp.float32), 0.25, 1.75)
    cross_shift = gaussian(streams_of[9], (D,), 0.5, 3.0, (), jnp.float32)
    cross_query = gaussian(streams_of[10], (D, D), (D // 2) ** -0.5, 0.375)
    cross_memory = gaussian(streams_of[11], (D, 2 * D), (D // 2) ** -0.5, 0.375)
    cross_output = gaussian(streams_of[12], (D, D), (D // 8) ** -0.5, 0.75)
    moe_gain = jnp.clip(1.0 + 0.15 * jax.random.normal(streams_of[13], (D,), jnp.float32), 0.25, 1.75)
    moe_shift = gaussian(streams_of[14], (D,), 0.5, 3.0, (), jnp.float32)
    expert_up = gaussian(streams_of[15], (EXPERTS, D, FF), D ** -0.5, 0.25, ((0, 4),))
    up_bias = gaussian(streams_of[16], (EXPERTS, FF), 0.5, 3.0, ((0, 4),), jnp.float32)
    expert_down = gaussian(streams_of[17], (EXPERTS, FF, D), FF ** -0.5, 0.125, ((0, 4),))
    down_bias = gaussian(streams_of[18], (EXPERTS, D), 0.3, 2.0, ((0, 4),), jnp.float32)
    return {"layer_input": layer_input, "memory": memory, "routes": routes, "out_grad": out_grad, "self_gain": self_gain, "self_shift": self_shift, "self_project": self_project, "self_output": self_output, "cross_gain": cross_gain, "cross_shift": cross_shift, "cross_query": cross_query, "cross_memory": cross_memory, "cross_output": cross_output, "moe_gain": moe_gain, "moe_shift": moe_shift, "expert_up": expert_up, "up_bias": up_bias, "expert_down": expert_down, "down_bias": down_bias}


HIGH = lax.Precision.HIGHEST
EPSILON = 1e-05
NEGATIVE = -1e+30

@jax.custom_vjp
def low(v):
    return lax.optimization_barrier(v.astype(jnp.bfloat16)).astype(jnp.float32)

@jax.custom_vjp
def low_back(v):
    return v

def low_keep(v):
    return (low(v), None)

def low_pass(kept, grad):
    return (grad,)

def back_keep(v):
    return (v, None)

def back_low(kept, grad):
    return (low(grad),)
low.defvjp(low_keep, low_pass)
low_back.defvjp(back_keep, back_low)

def rounded_both(values):
    return low(low_back(values))

def layer_norm(values, gain, shift):
    center = values - lax.optimization_barrier(jnp.mean(values, -1, keepdims=True))
    return center * lax.rsqrt(lax.optimization_barrier(jnp.mean(center * center, -1, keepdims=True)) + EPSILON) * gain + shift

def product(left, right):
    return jnp.dot(left, right, precision=HIGH)

def attention(query, keys, values, causal):
    length = query.shape[0]
    block = min(512, length)
    scale = HEAD_DIM ** (-0.5)
    key_heads = keys.reshape(keys.shape[0], HEADS, HEAD_DIM)
    value_heads = values.reshape(values.shape[0], HEADS, HEAD_DIM)
    key_place = jnp.arange(keys.shape[0], dtype=jnp.int32)

    def one_block(operands):
        rows, start = operands
        query_heads = rows.reshape(block, HEADS, HEAD_DIM)
        scores = low_back(jnp.einsum('qhd,khd->hqk', query_heads, key_heads, precision=HIGH) * scale)
        if causal:
            query_place = start + jnp.arange(block, dtype=jnp.int32)
            scores = jnp.where((query_place[:, None] >= key_place[None, :])[None], scores, NEGATIVE)
        highest = lax.optimization_barrier(jnp.max(scores, -1, keepdims=True))
        weights = jnp.exp(scores - highest)
        probs = weights / lax.optimization_barrier(jnp.sum(weights, -1, keepdims=True))
        result = jnp.einsum('hqk,khd->qhd', low(probs), value_heads, precision=HIGH)
        return result.reshape(block, HEADS * HEAD_DIM)
    count = length // block
    starts = jnp.arange(count, dtype=jnp.int32) * block
    blocks = lax.map(jax.checkpoint(one_block), (query.reshape(count, block, query.shape[1]), starts))
    return blocks.reshape(length, HEADS * HEAD_DIM)

def layer_seq(inputs, memory, route, params):
    self_gain, self_shift, self_project, self_output, cross_gain, cross_shift, cross_query, cross_memory, cross_output, moe_gain, moe_shift, expert_up, up_bias, expert_down, down_bias = params
    width = inputs.shape[1]
    normed1 = low(layer_norm(inputs, self_gain, self_shift))
    project = rounded_both(product(normed1, self_project))
    attn = rounded_both(attention(project[:, :width], project[:, width:2 * width], project[:, 2 * width:], True))
    hidden1 = inputs + low_back(product(attn, self_output))
    normed2 = low(layer_norm(hidden1, cross_gain, cross_shift))
    cross_q = rounded_both(product(normed2, cross_query))
    memory_kv = rounded_both(product(memory, cross_memory))
    cross = rounded_both(attention(cross_q, memory_kv[:, :width], memory_kv[:, width:], False))
    hidden2 = hidden1 + low_back(product(cross, cross_output))
    normed3 = rounded_both(layer_norm(hidden2, moe_gain, moe_shift))
    owner = jnp.repeat(route, GROUP_ROWS, total_repeat_length=SEQ)

    def one_expert(total, expert):
        pre = low_back(product(normed3, expert_up[expert]) + up_bias[expert])
        hidden = low(jax.nn.gelu(pre))
        rows_out = rounded_both(product(hidden, expert_down[expert]) + down_bias[expert])
        return (total + jnp.where((owner == expert)[:, None], rows_out, jnp.zeros_like(rows_out)), None)
    mixture, _ = lax.scan(jax.checkpoint(one_expert), jnp.zeros_like(hidden2), jnp.arange(EXPERTS, dtype=jnp.int32))
    return hidden2 + mixture

def reference(layer_input, memory, routes, out_grad, self_gain, self_shift, self_project, self_output, cross_gain, cross_shift, cross_query, cross_memory, cross_output, moe_gain, moe_shift, expert_up, up_bias, expert_down, down_bias):
    params = tuple((value.astype(jnp.float32) for value in (self_gain, self_shift, self_project, self_output, cross_gain, cross_shift, cross_query, cross_memory, cross_output, moe_gain, moe_shift, expert_up, up_bias, expert_down, down_bias)))
    route_rows = routes[:, :, 0]

    def forward(inputs, memories, weights):

        def one_seq(operands):
            seq_input, seq_memory, seq_route = operands
            return layer_seq(seq_input, seq_memory, seq_route, weights)
        return lax.map(jax.checkpoint(one_seq), (inputs, memories, route_rows))
    output, pull = jax.vjp(forward, layer_input.astype(jnp.float32), memory.astype(jnp.float32), params)
    grad_input, grad_memory, grads = pull(out_grad.astype(jnp.float32))
    return (output.astype(jnp.bfloat16), grad_input, grad_memory, grads[0], grads[1], grads[2], grads[3], grads[4], grads[5], grads[6], grads[7], grads[8], grads[9], grads[10], grads[11], grads[12], grads[13], grads[14])
```

```python
import functools
import math

import jax
import jax.numpy as jnp
from jax import lax
from jax.experimental import pallas as pl
from jax.experimental.pallas import tpu as pltpu
from jax.sharding import PartitionSpec as P

HEADS = 8
HEAD_DIM = 64
CAPACITY = 4
PAIR = 2 * HEAD_DIM
PAIRS = HEADS // 2
EPSILON = 1e-05
NEGATIVE = -1e30
SCALE = HEAD_DIM ** (-0.5)
SCALE2 = SCALE * math.log2(math.e)
BF = jnp.bfloat16
F32 = jnp.float32


def nn(left, right):
    return lax.dot_general(left, right, (((1,), (0,)), ((), ())), preferred_element_type=F32)


def nt(left, right):
    return lax.dot_general(left, right, (((1,), (1,)), ((), ())), preferred_element_type=F32)


def tn(left, right):
    return lax.dot_general(left, right, (((0,), (0,)), ((), ())), preferred_element_type=F32)


def span(index, size):
    return pl.ds(pl.multiple_of(index * size, size), size)


def normalize(values):
    center = values - jnp.mean(values, -1, keepdims=True)
    scale = lax.rsqrt(jnp.mean(center * center, -1, keepdims=True) + EPSILON)
    return center * scale, scale


def normalize_back(hat, scale, grad, gain):
    gained = grad * gain
    first = jnp.mean(gained, -1, keepdims=True)
    second = jnp.mean(gained * hat, -1, keepdims=True)
    return scale * (gained - first - hat * second)


def causal_mask(scores, block, causal):
    length = scores.shape[0]
    if not causal:
        return scores
    key = lax.broadcasted_iota(jnp.int32, (block, block), 0)
    row = lax.broadcasted_iota(jnp.int32, (block, block), 1)
    last = jnp.where(row >= key, scores[length - block :], NEGATIVE)
    if length == block:
        return last
    return jnp.concatenate([scores[: length - block], last], 0)


def own_head(values, head):
    lane = lax.broadcasted_iota(jnp.int32, values.shape, 1) < HEAD_DIM
    return jnp.where(lane if head == 0 else ~lane, values, jnp.zeros_like(values))


def attend(query, keys, values, out, out_t, total, causal, block=512):
    rows = out.shape[0]
    count = rows // block

    def pair(hp, _):
        def columns(column):
            return pl.ds(pl.multiple_of(column + hp * PAIR, PAIR), PAIR)

        two_keys = keys[0][:, columns(keys[1])]
        values_t = values[0][:, columns(values[1])].T
        results = {}

        def first(i, head):
            length = (i + 1) * block if causal else two_keys.shape[0]
            own = own_head(query[0][i * block : (i + 1) * block, columns(query[1])], head)
            return causal_mask(nt(two_keys[:length], own), block, causal)

        def second(i, head, scores):
            length = scores.shape[0]
            place = pl.ds(i * block, block)
            highest = jnp.max(scores, 0, keepdims=True)
            weights = jnp.exp2(scores * SCALE2 - highest * SCALE2).astype(BF)
            extended = jnp.concatenate(
                [
                    values_t[head * HEAD_DIM : (head + 1) * HEAD_DIM, :length],
                    jnp.ones((16, length), BF),
                ],
                0,
            )
            summed = nn(extended, weights)
            sums = summed[HEAD_DIM : HEAD_DIM + 1]
            total[hp, head : head + 1, place] = highest * SCALE2 + jnp.log2(sums)
            results[head] = summed[:HEAD_DIM] / sums
            if head == 1:
                both = jnp.concatenate([results[0], results[1]], 0).astype(BF)
                out_t[span(hp, PAIR), place] = both
                out[place, span(hp, PAIR)] = both.T

        before = None
        for i in range(count):
            for head in range(2):
                scores = first(i, head)
                if before is not None:
                    second(*before)
                before = (i, head, scores)
        second(*before)
        return 0

    lax.fori_loop(0, PAIRS, pair, 0)


def attend_back(
    query, keys, values, grad_out, out, total, grad_query, grad_keys, grad_values, sums, causal, block
):
    rows = grad_out.shape[0]
    count = rows // block

    def pair(hp, _):
        def columns(column):
            return pl.ds(pl.multiple_of(column + hp * PAIR, PAIR), PAIR)

        two_keys = keys[0][:, columns(keys[1])]
        two_values = values[0][:, columns(values[1])]
        keys_t = two_keys.T
        here = span(hp, PAIR)
        product = grad_out[:, here].astype(F32) * out[:, here].astype(F32)
        high = product.astype(BF)
        low = (product - high.astype(F32)).astype(BF)
        pick = (
            lax.broadcasted_iota(jnp.int32, (8, PAIR), 1) // HEAD_DIM
            == lax.broadcasted_iota(jnp.int32, (8, PAIR), 0)
        ).astype(F32).astype(BF)
        dots = nt(pick, high) + nt(pick, low)
        kept = {}

        def first(i, head):
            length = (i + 1) * block if causal else two_keys.shape[0]
            place = pl.ds(i * block, block)
            own_query = own_head(query[0][place, columns(query[1])], head)
            own_grad = own_head(grad_out[place, here], head)
            return (
                nt(two_keys[:length], own_query),
                nt(two_values[:length], own_grad),
                own_query,
                own_grad,
            )

        def second(i, head, state):
            scores, grad_probs, own_query, own_grad = state
            length = scores.shape[0]
            place = pl.ds(i * block, block)
            shifted = scores * SCALE2 - total[hp, head : head + 1, place]
            probs = jnp.exp2(causal_mask(shifted, block, causal))
            dot = dots[head : head + 1, i * block : (i + 1) * block]
            grad_scores = (probs * (grad_probs - dot)).astype(BF)
            back = nn(keys_t[head * HEAD_DIM : (head + 1) * HEAD_DIM, :length], grad_scores)
            kept[head] = (probs.astype(BF), grad_scores, own_query, own_grad, back)
            if head == 1:
                probs2, scores2 = [
                    jnp.concatenate([kept[0][n], kept[1][n]], 1) for n in range(2)
                ]
                query2, grad2 = [
                    jnp.concatenate([kept[0][n], kept[1][n]], 0) for n in range(2, 4)
                ]
                new_values = nn(probs2, grad2)
                new_keys = nn(scores2, query2)
                if i == count - 1:
                    sums[0][...] = new_keys
                    sums[1][...] = new_values
                else:
                    sums[0][:length] += new_keys
                    sums[1][:length] += new_values
                grad_query[0][place, columns(grad_query[1])] = (
                    jnp.concatenate([kept[0][4], kept[1][4]], 0).T * SCALE
                ).astype(BF)

        before = None
        for i in reversed(range(count)):
            for head in range(2):
                state = first(i, head)
                if before is not None:
                    second(*before)
                before = (i, head, state)
        second(*before)
        grad_keys[0][:, columns(grad_keys[1])] = (sums[0][...] * SCALE).astype(BF)
        grad_values[0][:, columns(grad_values[1])] = sums[1][...].astype(BF)
        return 0

    lax.fori_loop(0, PAIRS, pair, 0)


def slot_of(routes, group):
    own = routes[group]
    rank = lax.fori_loop(
        0, group, lambda j, c: c + jnp.where(routes[j] == own, 1, 0).astype(jnp.int32), jnp.int32(0)
    )
    return own * CAPACITY + rank


ROWS = 256


def front_kernel(
    group_rows,
    routes,
    x,
    memory,
    grad,
    self_gain,
    self_shift,
    self_project,
    self_output,
    cross_gain,
    cross_shift,
    cross_query,
    cross_memory,
    cross_output,
    moe_gain,
    moe_shift,
    project,
    attn,
    attn_t,
    total1,
    hidden1,
    cross_q,
    memory_kv,
    cross,
    cross_t,
    total2,
    hidden2,
    send,
    send_grad,
):
    rows, width = x.shape
    blocks = rows // ROWS
    send[...] = jnp.zeros_like(send)
    send_grad[...] = jnp.zeros_like(send_grad)

    def block1(i, _):
        here = span(i, ROWS)
        hat, _s = normalize(x[here].astype(F32))
        normed = (hat * self_gain[...] + self_shift[...]).astype(BF)
        project[here] = nn(normed, self_project[...]).astype(BF)
        memory_kv[here] = nn(memory[here], cross_memory[...]).astype(BF)
        return 0

    lax.fori_loop(0, blocks, block1, 0)
    attend((project, 0), (project, width), (project, 2 * width), attn, attn_t, total1, True)

    def block2(i, _):
        here = span(i, ROWS)
        hidden = x[here].astype(F32) + nn(attn[here], self_output[...])
        hidden1[here] = hidden
        hat, _s = normalize(hidden)
        normed = (hat * cross_gain[...] + cross_shift[...]).astype(BF)
        cross_q[here] = nn(normed, cross_query[...]).astype(BF)
        return 0

    lax.fori_loop(0, blocks, block2, 0)
    attend((cross_q, 0), (memory_kv, 0), (memory_kv, width), cross, cross_t, total2, False)

    def block3(i, _):
        here = span(i, ROWS)
        hidden = hidden1[here] + nn(cross[here], cross_output[...])
        hidden2[here] = hidden
        hat, _s = normalize(hidden)
        normed = (hat * moe_gain[...] + moe_shift[...]).astype(BF)
        for part in range(ROWS // group_rows):
            group = i * (ROWS // group_rows) + part
            slot = span(slot_of(routes, group), group_rows)
            send[slot] = normed[part * group_rows : (part + 1) * group_rows]
            send_grad[slot] = grad[span(group, group_rows)]
        return 0

    lax.fori_loop(0, blocks, block3, 0)


EXPERT_ROWS = 512


def experts_kernel(
    received,
    received_grad,
    up,
    up_bias,
    down,
    down_bias,
    rows_out,
    grad_rows,
    grad_up,
    grad_up_bias,
    grad_down,
    grad_down_bias,
    hidden,
    grad_pre,
    flat_t,
    grad_t,
):
    rows, width = received.shape
    wide = up.shape[1]
    chunk = 512
    first, third = math.sqrt(2.0 / math.pi), math.sqrt(2.0 / math.pi) * 0.044715
    flat_t[width:] = jnp.ones((flat_t.shape[0] - width, rows), BF)

    def block(i, _):
        here = span(i, EXPERT_ROWS)
        flat = received[here]
        grad = received_grad[here]
        flat_t[:width, here] = flat.T
        grad_t[:, here] = grad.T
        out = jnp.zeros((EXPERT_ROWS, width), F32)
        back = jnp.zeros((EXPERT_ROWS, width), F32)
        for c in range(wide // chunk):
            cols = pl.ds(c * chunk, chunk)
            pre = nn(flat, up[:, cols]) + up_bias[:, cols]
            square = pre * pre
            half = 0.5 + 0.5 * jnp.tanh(pre * (first + third * square))
            value = pre * half
            low = value.astype(BF)
            slope = half + value * (1.0 - half) * (2.0 * first + (6.0 * third) * square)
            gpre = (nt(grad, down[cols]) * slope).astype(BF)
            hidden[here, cols] = low
            grad_pre[here, cols] = gpre
            out += nn(low, down[cols])
            back += nt(gpre, up[:, cols])
        rows_out[here] = (out + down_bias[...]).astype(BF)
        grad_rows[here] = back.astype(BF)
        return 0

    lax.fori_loop(0, rows // EXPERT_ROWS, block, 0)

    def weights(c, _):
        cols = span(c, chunk)
        both = nn(flat_t[...], grad_pre[:, cols])
        grad_up[:, cols] = both[:width].astype(BF)
        grad_up_bias[:, cols] = both[width : width + 1].astype(BF)
        grad_down[cols] = nn(grad_t[...], hidden[:, cols]).T.astype(BF)
        return 0

    lax.fori_loop(0, wide // chunk, weights, 0)
    grad_down_bias[...] = jnp.sum(received_grad[...].astype(F32), 0, keepdims=True).astype(BF)


def back_kernel(
    group_rows,
    routes,
    x,
    memory,
    grad,
    self_gain,
    self_shift,
    self_project,
    self_output,
    cross_gain,
    cross_shift,
    cross_query,
    cross_memory,
    cross_output,
    moe_gain,
    moe_shift,
    project,
    attn,
    attn_t,
    total1,
    hidden1,
    cross_q,
    memory_kv,
    cross,
    cross_t,
    total2,
    hidden2,
    returned_grad,
    grad_input,
    grad_memory,
    grads,
    carried,
    carried_low,
    back_low,
    grad_q,
    grad_kv,
    grad_project,
    normed,
    sum_a,
    sum_b,
):
    rows, width = x.shape
    blocks = rows // ROWS
    zero = jnp.zeros((1, width), F32)
    per = ROWS // group_rows
    tail = grads.shape[0] - 16
    gains = []

    def block3(i, carry):
        here = span(i, ROWS)
        hat, scale = normalize(hidden2[here])
        gy = jnp.concatenate(
            [
                returned_grad[span(slot_of(routes, i * per + part), group_rows)]
                for part in range(per)
            ],
            0,
        ).astype(F32)
        total = grad[here].astype(F32) + normalize_back(hat, scale, gy, moe_gain[...])
        carried[here] = total
        low = total.astype(BF)
        carried_low[here] = low
        back_low[here] = nt(low, cross_output[...]).astype(BF)
        return (
            carry[0] + jnp.sum(gy * hat, 0, keepdims=True),
            carry[1] + jnp.sum(gy, 0, keepdims=True),
        )

    gains.append(lax.fori_loop(0, blocks, block3, (zero, zero)))
    grads[span(7, width)] = nn(cross_t[...], carried_low[...]).astype(BF)
    attend_back(
        (cross_q, 0),
        (memory_kv, 0),
        (memory_kv, width),
        back_low,
        cross,
        total2,
        (grad_q, 0),
        (grad_kv, 0),
        (grad_kv, width),
        (sum_a, sum_b),
        False,
        256,
    )

    def block2(i, carry):
        here = span(i, ROWS)
        hat, scale = normalize(hidden1[here])
        normed[here] = (hat * cross_gain[...] + cross_shift[...]).astype(BF)
        gy = nt(grad_q[here], cross_query[...])
        total = carried[here] + normalize_back(hat, scale, gy, cross_gain[...])
        carried[here] = total
        low = total.astype(BF)
        carried_low[here] = low
        back_low[here] = nt(low, self_output[...]).astype(BF)
        grad_memory[here] = nt(grad_kv[here], cross_memory[...])
        return (
            carry[0] + jnp.sum(gy * hat, 0, keepdims=True),
            carry[1] + jnp.sum(gy, 0, keepdims=True),
        )

    gains.append(lax.fori_loop(0, blocks, block2, (zero, zero)))
    grads[span(4, width)] = tn(normed[...], grad_q[...]).astype(BF)
    grads[span(5, width)] = tn(memory[...], grad_kv[:, :width]).astype(BF)
    grads[span(6, width)] = tn(memory[...], grad_kv[:, width:]).astype(BF)
    grads[span(3, width)] = nn(attn_t[...], carried_low[...]).astype(BF)
    attend_back(
        (project, 0),
        (project, width),
        (project, 2 * width),
        back_low,
        attn,
        total1,
        (grad_project, 0),
        (grad_project, width),
        (grad_project, 2 * width),
        (sum_a, sum_b),
        True,
        256,
    )

    def block1(i, carry):
        here = span(i, ROWS)
        hat, scale = normalize(x[here].astype(F32))
        normed[here] = (hat * self_gain[...] + self_shift[...]).astype(BF)
        gy = nt(grad_project[here], self_project[...])
        grad_input[here] = carried[here] + normalize_back(hat, scale, gy, self_gain[...])
        return (
            carry[0] + jnp.sum(gy * hat, 0, keepdims=True),
            carry[1] + jnp.sum(gy, 0, keepdims=True),
        )

    gains.append(lax.fori_loop(0, blocks, block1, (zero, zero)))
    for part in range(3):
        grads[span(part, width)] = tn(
            normed[...], grad_project[:, part * width : (part + 1) * width]
        ).astype(BF)
    small = [gains[2][0], gains[2][1], gains[1][0], gains[1][1], gains[0][0], gains[0][1]]
    grads[tail:] = jnp.concatenate(small + [jnp.zeros((10, width), F32)], 0).astype(BF)


def output_kernel(group_rows, routes, hidden2, returned, out):
    groups = out.shape[0] // group_rows

    def block(i, _):
        here = span(i, group_rows)
        moved = returned[span(slot_of(routes, i), group_rows)]
        out[here] = (hidden2[here] + moved.astype(F32)).astype(BF)
        return 0

    lax.fori_loop(0, groups, block, 0)


def call(kernel, inputs, outputs, scratch=(), scalars=0, flops=0):
    vmem = pl.BlockSpec(memory_space=pltpu.VMEM)
    smem = pl.BlockSpec(memory_space=pltpu.SMEM)
    return pl.pallas_call(
        kernel,
        out_shape=tuple(jax.ShapeDtypeStruct(shape, dtype) for shape, dtype in outputs),
        in_specs=[smem] * scalars + [vmem] * (len(inputs) - scalars),
        out_specs=tuple(vmem for _ in outputs),
        scratch_shapes=[pltpu.VMEM(shape, dtype) for shape, dtype in scratch],
        compiler_params=pltpu.CompilerParams(vmem_limit_bytes=60 << 20),
        cost_estimate=pl.CostEstimate(flops=flops, bytes_accessed=20 << 20, transcendentals=0),
    )(*inputs)


def body(
    layer_input,
    memory,
    routes,
    out_grad,
    self_gain,
    self_shift,
    self_project,
    self_output,
    cross_gain,
    cross_shift,
    cross_query,
    cross_memory,
    cross_output,
    moe_gain,
    moe_shift,
    expert_up,
    up_bias,
    expert_down,
    down_bias,
):
    x = layer_input[0]
    memory = memory[0]
    grad = out_grad[0]
    rows, width = x.shape
    wide = expert_up.shape[2]
    size = lax.axis_size("exp")
    groups = routes.shape[1]
    group_rows = rows // groups
    slot_rows = size * CAPACITY * group_rows
    route = routes.reshape(groups)
    gains = [v.reshape(1, width) for v in (self_gain, self_shift, cross_gain, cross_shift, moe_gain, moe_shift)]
    shared_in = [
        route, x, memory, grad,
        gains[0], gains[1], self_project, self_output,
        gains[2], gains[3], cross_query, cross_memory, cross_output,
        gains[4], gains[5],
    ]
    saved = call(
        functools.partial(front_kernel, group_rows),
        shared_in,
        [
            ((rows, 3 * width), BF),
            ((rows, width), BF),
            ((width, rows), BF),
            ((PAIRS, 8, rows), F32),
            ((rows, width), F32),
            ((rows, width), BF),
            ((memory.shape[0], 2 * width), BF),
            ((rows, width), BF),
            ((width, rows), BF),
            ((PAIRS, 8, rows), F32),
            ((rows, width), F32),
            ((slot_rows, width), BF),
            ((slot_rows, width), BF),
        ],
        scalars=1,
        flops=30 * 10**9,
    )
    send, send_grad = saved[-2:]
    saved = list(saved[:-2])
    hidden2 = saved[-1]

    def exchange(values):
        return lax.all_to_all(
            values.reshape(size, slot_rows // size, width), "exp", split_axis=0, concat_axis=0, tiled=True
        ).reshape(slot_rows, width)

    received_grad = exchange(send_grad)
    received = exchange(send)
    rows_out, grad_rows, grad_up, grad_up_bias, grad_down, grad_down_bias = call(
        experts_kernel,
        [received, received_grad, expert_up[0], up_bias, expert_down[0], down_bias],
        [
            ((slot_rows, width), BF),
            ((slot_rows, width), BF),
            ((width, wide), BF),
            ((1, wide), BF),
            ((wide, width), BF),
            ((1, width), BF),
        ],
        [
            ((slot_rows, wide), BF),
            ((slot_rows, wide), BF),
            ((width + 16, slot_rows), BF),
            ((width, slot_rows), BF),
        ],
        flops=26 * 10**9,
    )
    returned_grad = exchange(grad_rows)
    returned = exchange(rows_out)
    expert_sums = (
        lax.psum_scatter(grad_up, "batch", scatter_dimension=0, tiled=True).astype(F32),
        lax.psum_scatter(grad_up_bias, "batch", scatter_dimension=1, tiled=True).astype(F32),
        lax.psum_scatter(grad_down, "batch", scatter_dimension=0, tiled=True).astype(F32),
        lax.psum_scatter(grad_down_bias, "batch", scatter_dimension=1, tiled=True).astype(F32),
    )
    mats = 8
    grad_input, grad_memory, grads = call(
        functools.partial(back_kernel, group_rows),
        shared_in + saved + [returned_grad],
        [
            ((rows, width), F32),
            ((memory.shape[0], width), F32),
            ((mats * width + 16, width), BF),
        ],
        [
            ((rows, width), F32),
            ((rows, width), BF),
            ((rows, width), BF),
            ((rows, width), BF),
            ((memory.shape[0], 2 * width), BF),
            ((rows, 3 * width), BF),
            ((rows, width), BF),
            ((max(rows, memory.shape[0]), PAIR), F32),
            ((max(rows, memory.shape[0]), PAIR), F32),
        ],
        scalars=1,
        flops=60 * 10**9,
    )
    layer_output = call(
        functools.partial(output_kernel, group_rows),
        [route, hidden2, returned],
        [((rows, width), BF)],
        scalars=1,
        flops=10**6,
    )[0]
    grads = lax.psum(grads, ("batch", "exp")).astype(F32)
    mat = [grads[i * width : (i + 1) * width] for i in range(mats)]
    small = grads[mats * width :]
    return (
        layer_output[None],
        grad_input[None],
        grad_memory[None],
        small[0],
        small[1],
        jnp.concatenate(mat[0:3], 1),
        mat[3],
        small[2],
        small[3],
        mat[4],
        jnp.concatenate(mat[5:7], 1),
        mat[7],
        small[4],
        small[5],
        expert_sums[0][None],
        expert_sums[1],
        expert_sums[2][None],
        expert_sums[3],
    )


def solution(mesh):
    return jax.shard_map(
        body,
        mesh=mesh,
        in_specs=(
            P(("batch", "exp"), None, None),
            P(("batch", "exp"), None, None),
            P(("batch", "exp"), None, None),
            P(("batch", "exp"), None, None),
            P(),
            P(),
            P(),
            P(),
            P(),
            P(),
            P(),
            P(),
            P(),
            P(),
            P(),
            P("exp", None, None),
            P("exp", None),
            P("exp", None, None),
            P("exp", None),
        ),
        out_specs=(
            P(("batch", "exp"), None, None),
            P(("batch", "exp"), None, None),
            P(("batch", "exp"), None, None),
            P(),
            P(),
            P(),
            P(),
            P(),
            P(),
            P(),
            P(),
            P(),
            P(),
            P(),
            P("exp", "batch", None),
            P("exp", "batch"),
            P("exp", "batch", None),
            P("exp", "batch"),
        ),
        check_vma=False,
    )
```

```python
import functools
import math

import jax
import jax.numpy as jnp
from jax import lax
from jax.experimental import pallas as pl
from jax.experimental.pallas import tpu as pltpu
from jax.sharding import PartitionSpec as P

HEADS = 8
HEAD_DIM = 64
CAPACITY = 4
PAIR = 2 * HEAD_DIM
PAIRS = HEADS // 2
EPSILON = 1e-05
NEGATIVE = -1e30
SCALE = HEAD_DIM ** (-0.5)
SCALE2 = SCALE * math.log2(math.e)
BF = jnp.bfloat16
F32 = jnp.float32


def nn(left, right):
    return lax.dot_general(left, right, (((1,), (0,)), ((), ())), preferred_element_type=F32)


def nt(left, right):
    return lax.dot_general(left, right, (((1,), (1,)), ((), ())), preferred_element_type=F32)


def tn(left, right):
    return lax.dot_general(left, right, (((0,), (0,)), ((), ())), preferred_element_type=F32)


def span(index, size):
    return pl.ds(pl.multiple_of(index * size, size), size)


def normalize(values):
    center = values - jnp.mean(values, -1, keepdims=True)
    scale = lax.rsqrt(jnp.mean(center * center, -1, keepdims=True) + EPSILON)
    return center * scale, scale


def normalize_back(hat, scale, grad, gain):
    gained = grad * gain
    first = jnp.mean(gained, -1, keepdims=True)
    second = jnp.mean(gained * hat, -1, keepdims=True)
    return scale * (gained - first - hat * second)


def causal_mask(scores, block, causal):
    length = scores.shape[0]
    if not causal:
        return scores
    key = lax.broadcasted_iota(jnp.int32, (block, block), 0)
    row = lax.broadcasted_iota(jnp.int32, (block, block), 1)
    last = jnp.where(row >= key, scores[length - block :], NEGATIVE)
    if length == block:
        return last
    return jnp.concatenate([scores[: length - block], last], 0)


def own_head(values, head):
    lane = lax.broadcasted_iota(jnp.int32, values.shape, 1) < HEAD_DIM
    return jnp.where(lane if head == 0 else ~lane, values, jnp.zeros_like(values))


def attend(query, keys, values, out, out_t, total, causal, block=512):
    rows = out.shape[0]
    count = rows // block

    def pair(hp, _):
        def columns(column):
            return pl.ds(pl.multiple_of(column + hp * PAIR, PAIR), PAIR)

        two_keys = keys[0][:, columns(keys[1])]
        values_t = values[0][:, columns(values[1])].T
        results = {}

        def first(i, head):
            length = (i + 1) * block if causal else two_keys.shape[0]
            own = own_head(query[0][i * block : (i + 1) * block, columns(query[1])], head)
            return causal_mask(nt(two_keys[:length], own), block, causal)

        def second(i, head, scores):
            length = scores.shape[0]
            place = pl.ds(i * block, block)
            highest = jnp.max(scores, 0, keepdims=True)
            weights = jnp.exp2(scores * SCALE2 - highest * SCALE2).astype(BF)
            extended = jnp.concatenate(
                [
                    values_t[head * HEAD_DIM : (head + 1) * HEAD_DIM, :length],
                    jnp.ones((16, length), BF),
                ],
                0,
            )
            summed = nn(extended, weights)
            sums = summed[HEAD_DIM : HEAD_DIM + 1]
            total[hp, head : head + 1, place] = highest * SCALE2 + jnp.log2(sums)
            results[head] = summed[:HEAD_DIM] / sums
            if head == 1:
                both = jnp.concatenate([results[0], results[1]], 0).astype(BF)
                out_t[pl.ds(pl.multiple_of(i * HEADS * HEAD_DIM + hp * PAIR, PAIR), PAIR)] = both
                out[place, span(hp, PAIR)] = both.T

        before = None
        for i in range(count):
            for head in range(2):
                scores = first(i, head)
                if before is not None:
                    second(*before)
                before = (i, head, scores)
        second(*before)
        return 0

    lax.fori_loop(0, PAIRS, pair, 0)


def attend_back(
    query, keys, values, grad_out, out, total, grad_query, grad_keys, grad_values, sums, causal, block
):
    rows = grad_out.shape[0]
    count = rows // block

    def pair(hp, _):
        def columns(column):
            return pl.ds(pl.multiple_of(column + hp * PAIR, PAIR), PAIR)

        two_keys = keys[0][:, columns(keys[1])]
        two_values = values[0][:, columns(values[1])]
        keys_t = two_keys.T
        here = span(hp, PAIR)
        product = grad_out[:, here].astype(F32) * out[:, here].astype(F32)
        high = product.astype(BF)
        low = (product - high.astype(F32)).astype(BF)
        pick = (
            lax.broadcasted_iota(jnp.int32, (8, PAIR), 1) // HEAD_DIM
            == lax.broadcasted_iota(jnp.int32, (8, PAIR), 0)
        ).astype(F32).astype(BF)
        dots = nt(pick, high) + nt(pick, low)
        kept = {}

        def first(i, head):
            length = (i + 1) * block if causal else two_keys.shape[0]
            place = pl.ds(i * block, block)
            own_query = own_head(query[0][place, columns(query[1])], head)
            own_grad = own_head(grad_out[place, here], head)
            return (
                nt(two_keys[:length], own_query),
                nt(two_values[:length], own_grad),
                own_query,
                own_grad,
            )

        def second(i, head, state):
            scores, grad_probs, own_query, own_grad = state
            length = scores.shape[0]
            place = pl.ds(i * block, block)
            shifted = scores * SCALE2 - total[hp, head : head + 1, place]
            probs = jnp.exp2(causal_mask(shifted, block, causal))
            dot = dots[head : head + 1, i * block : (i + 1) * block]
            grad_scores = (probs * (grad_probs - dot)).astype(BF)
            back = nn(keys_t[head * HEAD_DIM : (head + 1) * HEAD_DIM, :length], grad_scores)
            kept[head] = (probs.astype(BF), grad_scores, own_query, own_grad, back)
            if head == 1:
                probs2, scores2 = [
                    jnp.concatenate([kept[0][n], kept[1][n]], 1) for n in range(2)
                ]
                query2, grad2 = [
                    jnp.concatenate([kept[0][n], kept[1][n]], 0) for n in range(2, 4)
                ]
                new_values = nn(probs2, grad2)
                new_keys = nn(scores2, query2)
                if i == count - 1:
                    sums[0][...] = new_keys
                    sums[1][...] = new_values
                else:
                    sums[0][:length] += new_keys
                    sums[1][:length] += new_values
                grad_query[0][place, columns(grad_query[1])] = (
                    jnp.concatenate([kept[0][4], kept[1][4]], 0).T * SCALE
                ).astype(BF)

        before = None
        for i in reversed(range(count)):
            for head in range(2):
                state = first(i, head)
                if before is not None:
                    second(*before)
                before = (i, head, state)
        second(*before)
        grad_keys[0][:, columns(grad_keys[1])] = (sums[0][...] * SCALE).astype(BF)
        grad_values[0][:, columns(grad_values[1])] = sums[1][...].astype(BF)
        return 0

    lax.fori_loop(0, PAIRS, pair, 0)


def slot_of(routes, group, device, size):
    own = routes[group]
    rank = lax.fori_loop(
        0, group, lambda j, c: c + jnp.where(routes[j] == own, 1, 0).astype(jnp.int32), jnp.int32(0)
    )
    return partner_of(device, own, size) * CAPACITY + rank


def weigh(values, weight):
    return values * jnp.full(values.shape, weight.astype(F32), F32).astype(BF)


def pick_group(routes, source, group_rows, expert, rank):
    count = jnp.int32(0)
    total = None
    for group in range(source.shape[0] // group_rows):
        same = jnp.where(routes[group] == expert, 1, 0).astype(jnp.int32)
        hit = same * jnp.where(count == rank, 1, 0).astype(jnp.int32)
        count = count + same
        term = weigh(source[group * group_rows : (group + 1) * group_rows], hit)
        total = term if total is None else total + term
    return total


def partner_of(own, offset, size):
    result, bit = 0, 1
    while bit < size:
        result = result + lax.rem(own // bit + offset // bit, 2) * bit
        bit *= 2
    return result


ROWS = 256
MESH = pl.DeviceIdType.MESH
Q, K, V, ATTN, CQ, MK, MV, CROSS, ATTN_T, CROSS_T = range(10)
SAVED = 10


def forward_kernel(
    size,
    group_rows,
    routes,
    self_gain,
    self_shift,
    cross_gain,
    cross_shift,
    moe_gain,
    moe_shift,
    up_bias,
    down_bias,
    *refs,
):
    (
        x_h, memory_h, grad_h, project_h, output_h, query_h, memory_w_h, cross_w_h, up_h, down_h,
        saved_o, hidden1_o, hidden2_o, rows_out_o, returned_o, grad_up_o, grad_down_o,
        total1, total2, grad_up_bias, grad_down_bias,
        x, memory, grad, self_project, self_output, cross_query, cross_memory, cross_output, up, down,
        arena, hidden1, hidden2, normed3, outbound, received, received_grad, flat_t, grad_t, grad_up, grad_down,
        in_sems, out_sems, grad_send, grad_recv, row_send, row_recv, back_send, back_recv,
    ) = refs
    rows, width = x.shape
    wide = up.shape[1]
    blocks = rows // ROWS
    part_rows = CAPACITY * group_rows
    slot_rows = size * part_rows
    batch, own = lax.axis_index("batch"), lax.axis_index("exp")

    def partner(offset):
        return (batch, partner_of(own, offset, size))

    loads = [
        pltpu.make_async_copy(source, target, in_sems.at[n])
        for n, (source, target) in enumerate(
            [
                (grad_h, grad), (x_h, x), (project_h, self_project), (memory_h, memory),
                (memory_w_h, cross_memory), (output_h, self_output), (query_h, cross_query),
                (cross_w_h, cross_output), (up_h, up), (down_h, down),
            ]
        )
    ]
    for load in loads:
        load.start()
    barrier = pltpu.get_barrier_semaphore()
    for offset in range(1, size):
        pl.semaphore_signal(barrier, inc=1, device_id=partner(offset), device_id_type=MESH)
    pl.semaphore_wait(barrier, size - 1)

    def part(ref, offset):
        return ref.at[pl.ds(pl.multiple_of(offset * part_rows, part_rows), part_rows)]

    def send(source, target, offset, send_sems, recv_sems):
        return pltpu.make_async_remote_copy(
            src_ref=part(source, offset),
            dst_ref=part(target, offset),
            send_sem=send_sems.at[offset],
            recv_sem=recv_sems.at[offset],
            device_id=partner(offset),
            device_id_type=MESH,
        )

    def dispatch(source, target, offset):
        expert = partner_of(own, offset, size)

        def one(rank, _):
            values = pick_group(routes, source, group_rows, expert, rank)
            target[pl.ds(pl.multiple_of(offset * part_rows + rank * group_rows, group_rows), group_rows)] = values
            return 0

        lax.fori_loop(0, CAPACITY, one, 0)

    def to_all(source, target, send_sems, recv_sems):
        dispatch(source, target, 0)

        def one(offset, _):
            dispatch(source, outbound, offset)
            send(outbound, target, offset, send_sems, recv_sems).start()
            return 0

        lax.fori_loop(1, size, one, 0)

    loads[0].wait()
    to_all(grad, received_grad, grad_send, grad_recv)
    for load in loads[1:5]:
        load.wait()

    def place(which):
        return arena.at[pl.ds(which * rows, rows)]

    q, k, v, attn, cq, mk, mv, cross, attn_t, cross_t = [place(n) for n in range(SAVED)]

    def block1(i, _):
        here = span(i, ROWS)
        hat, _s = normalize(x[here].astype(F32))
        normed = (hat * self_gain[...] + self_shift[...]).astype(BF)
        for n, target in enumerate((q, k, v)):
            target[here] = nn(normed, self_project[:, n * width : (n + 1) * width]).astype(BF)
        for n, target in enumerate((mk, mv)):
            target[here] = nn(memory[here], cross_memory[:, n * width : (n + 1) * width]).astype(BF)
        return 0

    lax.fori_loop(0, blocks, block1, 0)
    attend((q, 0), (k, 0), (v, 0), attn, attn_t, total1, True)
    for load in loads[5:]:
        load.wait()

    def block2(i, _):
        here = span(i, ROWS)
        hidden = x[here].astype(F32) + nn(attn[here], self_output[...])
        hidden1[here] = hidden
        hat, _s = normalize(hidden)
        normed = (hat * cross_gain[...] + cross_shift[...]).astype(BF)
        cq[here] = nn(normed, cross_query[...]).astype(BF)
        return 0

    lax.fori_loop(0, blocks, block2, 0)
    attend((cq, 0), (mk, 0), (mv, 0), cross, cross_t, total2, False)
    stores = [
        pltpu.make_async_copy(arena.at[pl.ds(0, SAVED * rows)], saved_o, out_sems.at[0]),
        pltpu.make_async_copy(hidden1, hidden1_o, out_sems.at[1]),
        pltpu.make_async_copy(hidden2, hidden2_o, out_sems.at[2]),
    ]
    stores[0].start()
    stores[1].start()

    def block3(i, _):
        here = span(i, ROWS)
        hidden = hidden1[here] + nn(cross[here], cross_output[...])
        hidden2[here] = hidden
        hat, _s = normalize(hidden)
        normed3[here] = (hat * moe_gain[...] + moe_shift[...]).astype(BF)
        return 0

    lax.fori_loop(0, blocks, block3, 0)
    stores[2].start()

    def sent(source, target, send_sems, recv_sems):
        def one(offset, _):
            send(source, target, offset, send_sems, recv_sems).wait_send()
            return 0

        lax.fori_loop(1, size, one, 0)

    sent(outbound, received_grad, grad_send, grad_recv)
    to_all(normed3, received, row_send, row_recv)
    stores[0].wait()

    block_rows = max(512, part_rows)
    per = block_rows // part_rows
    chunk = 512
    first, third = math.sqrt(2.0 / math.pi), math.sqrt(2.0 / math.pi) * 0.044715
    flat_t[width:] = jnp.ones((flat_t.shape[0] - width, slot_rows), BF)

    def hidden_at(c, start, length):
        return arena.at[pl.ds(pl.multiple_of(c * slot_rows + start, block_rows), length)]

    def pre_at(c, start, length):
        return arena.at[
            pl.ds(pl.multiple_of((wide // chunk + c) * slot_rows + start, block_rows), length)
        ]

    def block(i, bias):
        for n in range(per):
            offset = i * per + n

            @pl.when(offset > 0)
            def _():
                send(outbound, received_grad, offset, grad_send, grad_recv).wait_recv()
                send(outbound, received, offset, row_send, row_recv).wait_recv()

        here = span(i, block_rows)
        flat = received[here]
        grads = received_grad[here]
        flat_t[:width, here] = flat.T
        grad_t[:, here] = grads.T
        out = jnp.zeros((block_rows, width), F32)
        back = jnp.zeros((block_rows, width), F32)
        for c in range(wide // chunk):
            cols = pl.ds(c * chunk, chunk)
            pre = nn(flat, up[:, cols]) + up_bias[:, cols]
            square = pre * pre
            half = 0.5 + 0.5 * jnp.tanh(pre * (first + third * square))
            value = pre * half
            low = value.astype(BF)
            slope = half + value * (1.0 - half) * (2.0 * first + (6.0 * third) * square)
            gpre = (nt(grads, down[cols]) * slope).astype(BF)
            hidden_at(c, i * block_rows, block_rows)[...] = low
            pre_at(c, i * block_rows, block_rows)[...] = gpre
            out += nn(low, down[cols])
            back += nt(gpre, up[:, cols])
        received[here] = (out + down_bias[...]).astype(BF)
        received_grad[here] = back.astype(BF)
        for n in range(per):
            offset = i * per + n

            @pl.when(offset > 0)
            def _():
                send(received_grad, returned_o, offset, back_send, back_recv).start()

        return bias + jnp.sum(grads.astype(F32), 0, keepdims=True)

    bias = lax.fori_loop(0, slot_rows // block_rows, block, jnp.zeros((1, width), F32))
    grad_down_bias[...] = bias.astype(BF)
    stores.append(
        pltpu.make_async_copy(part(received_grad, 0), part(returned_o, 0), out_sems.at[3])
    )
    stores.append(pltpu.make_async_copy(received, rows_out_o, out_sems.at[4]))
    stores[3].start()
    stores[4].start()

    def weights(c, _):
        cols = span(c, chunk)
        both = nn(flat_t[...], pre_at(c, 0, slot_rows)[...])
        grad_up[:, cols] = both[:width].astype(BF)
        grad_up_bias[:, cols] = both[width : width + 1].astype(BF)
        grad_down[cols] = nn(grad_t[...], hidden_at(c, 0, slot_rows)[...]).T.astype(BF)
        return 0

    lax.fori_loop(0, wide // chunk, weights, 0)
    stores.append(pltpu.make_async_copy(grad_up, grad_up_o, out_sems.at[5]))
    stores.append(pltpu.make_async_copy(grad_down, grad_down_o, out_sems.at[6]))
    stores[5].start()
    stores[6].start()
    sent(outbound, received, row_send, row_recv)
    sent(received_grad, returned_o, back_send, back_recv)

    def arrived(offset, _):
        send(received_grad, returned_o, offset, back_send, back_recv).wait_recv()
        return 0

    lax.fori_loop(1, size, arrived, 0)
    for store in stores[1:]:
        store.wait()


def back_kernel(
    size,
    group_rows,
    routes,
    x,
    memory,
    grad,
    self_gain,
    self_shift,
    self_project,
    self_output,
    cross_gain,
    cross_shift,
    cross_query,
    cross_memory,
    cross_output,
    moe_gain,
    moe_shift,
    saved,
    total1,
    hidden1,
    total2,
    hidden2,
    returned_grad,
    grad_input,
    grad_memory,
    grads,
    carried,
    carried_low,
    back_low,
    grad_q,
    grad_kv,
    grad_project,
    normed,
    sum_a,
    sum_b,
):
    rows, width = x.shape
    blocks = rows // ROWS
    zero = jnp.zeros((1, width), F32)
    per = ROWS // group_rows
    tail = grads.shape[0] - 16
    gains = []
    own = lax.axis_index("exp")
    q, k, v, attn, cross_q, mk, mv, cross, attn_t, cross_t = [
        saved.at[pl.ds(n * rows, rows)] for n in range(SAVED)
    ]

    def times(turned, right):
        half = 512
        return sum(
            nn(turned[n * width : (n + 1) * width], right[n * half : (n + 1) * half])
            for n in range(rows // half)
        )

    def block3(i, carry):
        here = span(i, ROWS)
        hat, scale = normalize(hidden2[here])
        gy = jnp.concatenate(
            [
                returned_grad[span(slot_of(routes, i * per + part, own, size), group_rows)]
                for part in range(per)
            ],
            0,
        ).astype(F32)
        total = grad[here].astype(F32) + normalize_back(hat, scale, gy, moe_gain[...])
        carried[here] = total
        low = total.astype(BF)
        carried_low[here] = low
        back_low[here] = nt(low, cross_output[...]).astype(BF)
        return (
            carry[0] + jnp.sum(gy * hat, 0, keepdims=True),
            carry[1] + jnp.sum(gy, 0, keepdims=True),
        )

    gains.append(lax.fori_loop(0, blocks, block3, (zero, zero)))
    grads[span(7, width)] = times(cross_t, carried_low).astype(BF)
    attend_back(
        (cross_q, 0),
        (mk, 0),
        (mv, 0),
        back_low,
        cross,
        total2,
        (grad_q, 0),
        (grad_kv, 0),
        (grad_kv, width),
        (sum_a, sum_b),
        False,
        256,
    )

    def block2(i, carry):
        here = span(i, ROWS)
        hat, scale = normalize(hidden1[here])
        normed[here] = (hat * cross_gain[...] + cross_shift[...]).astype(BF)
        gy = nt(grad_q[here], cross_query[...])
        total = carried[here] + normalize_back(hat, scale, gy, cross_gain[...])
        carried[here] = total
        low = total.astype(BF)
        carried_low[here] = low
        back_low[here] = nt(low, self_output[...]).astype(BF)
        grad_memory[here] = nt(grad_kv[here], cross_memory[...])
        return (
            carry[0] + jnp.sum(gy * hat, 0, keepdims=True),
            carry[1] + jnp.sum(gy, 0, keepdims=True),
        )

    gains.append(lax.fori_loop(0, blocks, block2, (zero, zero)))
    grads[span(4, width)] = tn(normed[...], grad_q[...]).astype(BF)
    grads[span(5, width)] = tn(memory[...], grad_kv[:, :width]).astype(BF)
    grads[span(6, width)] = tn(memory[...], grad_kv[:, width:]).astype(BF)
    grads[span(3, width)] = times(attn_t, carried_low).astype(BF)
    attend_back(
        (q, 0),
        (k, 0),
        (v, 0),
        back_low,
        attn,
        total1,
        (grad_project, 0),
        (grad_project, width),
        (grad_project, 2 * width),
        (sum_a, sum_b),
        True,
        256,
    )

    def block1(i, carry):
        here = span(i, ROWS)
        hat, scale = normalize(x[here].astype(F32))
        normed[here] = (hat * self_gain[...] + self_shift[...]).astype(BF)
        gy = nt(grad_project[here], self_project[...])
        grad_input[here] = carried[here] + normalize_back(hat, scale, gy, self_gain[...])
        return (
            carry[0] + jnp.sum(gy * hat, 0, keepdims=True),
            carry[1] + jnp.sum(gy, 0, keepdims=True),
        )

    gains.append(lax.fori_loop(0, blocks, block1, (zero, zero)))
    for part in range(3):
        grads[span(part, width)] = tn(
            normed[...], grad_project[:, part * width : (part + 1) * width]
        ).astype(BF)
    small = [gains[2][0], gains[2][1], gains[1][0], gains[1][1], gains[0][0], gains[0][1]]
    grads[tail:] = jnp.concatenate(small + [jnp.zeros((10, width), F32)], 0).astype(BF)


def output_kernel(size, group_rows, routes, hidden2, returned, out):
    own = lax.axis_index("exp")
    groups = out.shape[0] // group_rows

    def block(i, _):
        here = span(i, group_rows)
        moved = returned[span(slot_of(routes, i, own, size), group_rows)]
        out[here] = (hidden2[here] + moved.astype(F32)).astype(BF)
        return 0

    lax.fori_loop(0, groups, block, 0)


def call(kernel, inputs, outputs, scratch=(), scalars=0, flops=0):
    vmem = pl.BlockSpec(memory_space=pltpu.VMEM)
    smem = pl.BlockSpec(memory_space=pltpu.SMEM)
    return pl.pallas_call(
        kernel,
        out_shape=tuple(jax.ShapeDtypeStruct(shape, dtype) for shape, dtype in outputs),
        in_specs=[smem] * scalars + [vmem] * (len(inputs) - scalars),
        out_specs=tuple(vmem for _ in outputs),
        scratch_shapes=[pltpu.VMEM(shape, dtype) for shape, dtype in scratch],
        compiler_params=pltpu.CompilerParams(vmem_limit_bytes=60 << 20),
        cost_estimate=pl.CostEstimate(flops=flops, bytes_accessed=20 << 20, transcendentals=0),
    )(*inputs)


def body(
    layer_input,
    memory,
    routes,
    out_grad,
    self_gain,
    self_shift,
    self_project,
    self_output,
    cross_gain,
    cross_shift,
    cross_query,
    cross_memory,
    cross_output,
    moe_gain,
    moe_shift,
    expert_up,
    up_bias,
    expert_down,
    down_bias,
):
    x = layer_input[0]
    memory = memory[0]
    grad = out_grad[0]
    rows, width = x.shape
    wide = expert_up.shape[2]
    size = lax.axis_size("exp")
    groups = routes.shape[1]
    group_rows = rows // groups
    slot_rows = size * CAPACITY * group_rows
    route = routes.reshape(groups)
    gains = [v.reshape(1, width) for v in (self_gain, self_shift, cross_gain, cross_shift, moe_gain, moe_shift)]
    def array(shape, dtype):
        return jax.ShapeDtypeStruct(shape, dtype)

    vmem, smem, any_ = [pl.BlockSpec(memory_space=m) for m in (pltpu.VMEM, pltpu.SMEM, pl.ANY)]
    big = [
        x, memory, grad, self_project, self_output, cross_query, cross_memory, cross_output,
        expert_up[0], expert_down[0],
    ]
    sems = pltpu.SemaphoreType.DMA((size,))
    saved, hidden1, hidden2, rows_out, returned_grad, grad_up, grad_down, total1, total2, grad_up_bias, grad_down_bias = pl.pallas_call(
        functools.partial(forward_kernel, size, group_rows),
        out_shape=(
            array((SAVED * rows, width), BF),
            array((rows, width), F32),
            array((rows, width), F32),
            array((slot_rows, width), BF),
            array((slot_rows, width), BF),
            array((width, wide), BF),
            array((wide, width), BF),
            array((PAIRS, 8, rows), F32),
            array((PAIRS, 8, rows), F32),
            array((1, wide), BF),
            array((1, width), BF),
        ),
        in_specs=[smem] + [vmem] * 8 + [any_] * 10,
        out_specs=(any_,) * 7 + (vmem,) * 4,
        scratch_shapes=[pltpu.VMEM(v.shape, v.dtype) for v in big]
        + [
            pltpu.VMEM(shape, dtype)
            for shape, dtype in [
                ((2 * slot_rows * (wide // 512), 512), BF),
                ((rows, width), F32),
                ((rows, width), F32),
                ((rows, width), BF),
                ((slot_rows, width), BF),
                ((slot_rows, width), BF),
                ((slot_rows, width), BF),
                ((width + 16, slot_rows), BF),
                ((width, slot_rows), BF),
                ((width, wide), BF),
                ((wide, width), BF),
            ]
        ]
        + [pltpu.SemaphoreType.DMA((10,)), pltpu.SemaphoreType.DMA((7,))]
        + [sems] * 6,
        compiler_params=pltpu.CompilerParams(
            collective_id=0, has_side_effects=True, vmem_limit_bytes=62 << 20
        ),
        cost_estimate=pl.CostEstimate(flops=60 * 10**9, bytes_accessed=40 << 20, transcendentals=0),
    )(route, *gains, up_bias, down_bias, *big)
    shared_in = [
        route, x, memory, grad,
        gains[0], gains[1], self_project, self_output,
        gains[2], gains[3], cross_query, cross_memory, cross_output,
        gains[4], gains[5],
    ]
    saved = [saved, total1, hidden1, total2, hidden2]
    own = lax.axis_index("exp")
    order = jnp.stack([partner_of(own, jnp.int32(n), size) for n in range(size)])
    returned = lax.all_to_all(
        jnp.take(rows_out.reshape(size, slot_rows // size, width), order, 0), "exp", split_axis=0, concat_axis=0, tiled=True
    )
    returned = jnp.take(returned, order, 0).reshape(slot_rows, width)
    expert_sums = (
        lax.psum_scatter(grad_up, "batch", scatter_dimension=0, tiled=True).astype(F32),
        lax.psum_scatter(grad_up_bias, "batch", scatter_dimension=1, tiled=True).astype(F32),
        lax.psum_scatter(grad_down, "batch", scatter_dimension=0, tiled=True).astype(F32),
        lax.psum_scatter(grad_down_bias, "batch", scatter_dimension=1, tiled=True).astype(F32),
    )
    mats = 8
    grad_input, grad_memory, grads = call(
        functools.partial(back_kernel, size, group_rows),
        shared_in + saved + [returned_grad],
        [
            ((rows, width), F32),
            ((memory.shape[0], width), F32),
            ((mats * width + 16, width), BF),
        ],
        [
            ((rows, width), F32),
            ((rows, width), BF),
            ((rows, width), BF),
            ((rows, width), BF),
            ((memory.shape[0], 2 * width), BF),
            ((rows, 3 * width), BF),
            ((rows, width), BF),
            ((max(rows, memory.shape[0]), PAIR), F32),
            ((max(rows, memory.shape[0]), PAIR), F32),
        ],
        scalars=1,
        flops=60 * 10**9,
    )
    layer_output = call(
        functools.partial(output_kernel, size, group_rows),
        [route, hidden2, returned],
        [((rows, width), BF)],
        scalars=1,
        flops=10**6,
    )[0]
    grads = lax.psum(grads, ("batch", "exp")).astype(F32)
    mat = [grads[i * width : (i + 1) * width] for i in range(mats)]
    small = grads[mats * width :]
    return (
        layer_output[None],
        grad_input[None],
        grad_memory[None],
        small[0],
        small[1],
        jnp.concatenate(mat[0:3], 1),
        mat[3],
        small[2],
        small[3],
        mat[4],
        jnp.concatenate(mat[5:7], 1),
        mat[7],
        small[4],
        small[5],
        expert_sums[0][None],
        expert_sums[1],
        expert_sums[2][None],
        expert_sums[3],
    )


def solution(mesh):
    return jax.shard_map(
        body,
        mesh=mesh,
        in_specs=(
            P(("batch", "exp"), None, None),
            P(("batch", "exp"), None, None),
            P(("batch", "exp"), None, None),
            P(("batch", "exp"), None, None),
            P(),
            P(),
            P(),
            P(),
            P(),
            P(),
            P(),
            P(),
            P(),
            P(),
            P(),
            P("exp", None, None),
            P("exp", None),
            P("exp", None, None),
            P("exp", None),
        ),
        out_specs=(
            P(("batch", "exp"), None, None),
            P(("batch", "exp"), None, None),
            P(("batch", "exp"), None, None),
            P(),
            P(),
            P(),
            P(),
            P(),
            P(),
            P(),
            P(),
            P(),
            P(),
            P(),
            P("exp", "batch", None),
            P("exp", "batch"),
            P("exp", "batch", None),
            P("exp", "batch"),
        ),
        check_vma=False,
    )
```

```python
import functools
import math

import jax
import jax.numpy as jnp
from jax import lax
from jax.experimental import pallas as pl
from jax.experimental.pallas import tpu as pltpu
from jax.sharding import PartitionSpec as P

HEADS = 8
HEAD_DIM = 64
CAPACITY = 4
PAIR = 2 * HEAD_DIM
PAIRS = HEADS // 2
EPSILON = 1e-05
NEGATIVE = -1e30
SCALE = HEAD_DIM ** (-0.5)
SCALE2 = SCALE * math.log2(math.e)
BF = jnp.bfloat16
F32 = jnp.float32


def nn(left, right):
    return lax.dot_general(left, right, (((1,), (0,)), ((), ())), preferred_element_type=F32)


def nt(left, right):
    return lax.dot_general(left, right, (((1,), (1,)), ((), ())), preferred_element_type=F32)


def tn(left, right):
    return lax.dot_general(left, right, (((0,), (0,)), ((), ())), preferred_element_type=F32)


def span(index, size):
    return pl.ds(pl.multiple_of(index * size, size), size)


def normalize(values):
    center = values - jnp.mean(values, -1, keepdims=True)
    scale = lax.rsqrt(jnp.mean(center * center, -1, keepdims=True) + EPSILON)
    return center * scale, scale


def normalize_back(hat, scale, grad, gain):
    gained = grad * gain
    first = jnp.mean(gained, -1, keepdims=True)
    second = jnp.mean(gained * hat, -1, keepdims=True)
    return scale * (gained - first - hat * second)


def causal_mask(scores, block, causal):
    length = scores.shape[0]
    if not causal:
        return scores
    key = lax.broadcasted_iota(jnp.int32, (block, block), 0)
    row = lax.broadcasted_iota(jnp.int32, (block, block), 1)
    last = jnp.where(row >= key, scores[length - block :], NEGATIVE)
    if length == block:
        return last
    return jnp.concatenate([scores[: length - block], last], 0)


def own_head(values, head):
    lane = lax.broadcasted_iota(jnp.int32, values.shape, 1) < HEAD_DIM
    return jnp.where(lane if head == 0 else ~lane, values, jnp.zeros_like(values))


def attend(query, keys, values, out, out_t, total, causal, block=512):
    rows = out.shape[0]
    count = rows // block

    def pair(hp, _):
        def columns(column):
            return pl.ds(pl.multiple_of(column + hp * PAIR, PAIR), PAIR)

        two_keys = keys[0][:, columns(keys[1])]
        values_t = values[0][:, columns(values[1])].T
        results = {}

        def first(i, head):
            length = (i + 1) * block if causal else two_keys.shape[0]
            own = own_head(query[0][i * block : (i + 1) * block, columns(query[1])], head)
            return causal_mask(nt(two_keys[:length], own), block, causal)

        def second(i, head, scores):
            length = scores.shape[0]
            place = pl.ds(i * block, block)
            highest = jnp.max(scores, 0, keepdims=True)
            weights = jnp.exp2(scores * SCALE2 - highest * SCALE2).astype(BF)
            extended = jnp.concatenate(
                [
                    values_t[head * HEAD_DIM : (head + 1) * HEAD_DIM, :length],
                    jnp.ones((16, length), BF),
                ],
                0,
            )
            summed = nn(extended, weights)
            sums = summed[HEAD_DIM : HEAD_DIM + 1]
            total[hp, head : head + 1, place] = highest * SCALE2 + jnp.log2(sums)
            results[head] = summed[:HEAD_DIM] / sums
            if head == 1:
                both = jnp.concatenate([results[0], results[1]], 0).astype(BF)
                out_t[pl.ds(pl.multiple_of(i * HEADS * HEAD_DIM + hp * PAIR, PAIR), PAIR)] = both
                out[place, span(hp, PAIR)] = both.T

        before = None
        for i in range(count):
            for head in range(2):
                scores = first(i, head)
                if before is not None:
                    second(*before)
                before = (i, head, scores)
        second(*before)
        return 0

    lax.fori_loop(0, PAIRS, pair, 0)


def attend_back(
    query, keys, values, grad_out, out, total, grad_query, grad_keys, grad_values, sums, causal, block, hook=None
):
    rows = grad_out.shape[0]
    count = rows // block

    def pair(hp, _):
        def columns(column):
            return pl.ds(pl.multiple_of(column + hp * PAIR, PAIR), PAIR)

        two_keys = keys[0][:, columns(keys[1])]
        two_values = values[0][:, columns(values[1])]
        keys_t = two_keys.T
        here = span(hp, PAIR)
        product = grad_out[:, here].astype(F32) * out[:, here].astype(F32)
        high = product.astype(BF)
        low = (product - high.astype(F32)).astype(BF)
        pick = (
            lax.broadcasted_iota(jnp.int32, (8, PAIR), 1) // HEAD_DIM
            == lax.broadcasted_iota(jnp.int32, (8, PAIR), 0)
        ).astype(F32).astype(BF)
        dots = nt(pick, high) + nt(pick, low)
        kept = {}

        def first(i, head):
            length = (i + 1) * block if causal else two_keys.shape[0]
            place = pl.ds(i * block, block)
            own_query = own_head(query[0][place, columns(query[1])], head)
            own_grad = own_head(grad_out[place, here], head)
            return (
                nt(two_keys[:length], own_query),
                nt(two_values[:length], own_grad),
                own_query,
                own_grad,
            )

        def second(i, head, state):
            scores, grad_probs, own_query, own_grad = state
            length = scores.shape[0]
            place = pl.ds(i * block, block)
            shifted = scores * SCALE2 - total[hp, head : head + 1, place]
            probs = jnp.exp2(causal_mask(shifted, block, causal))
            dot = dots[head : head + 1, i * block : (i + 1) * block]
            grad_scores = (probs * (grad_probs - dot)).astype(BF)
            back = nn(keys_t[head * HEAD_DIM : (head + 1) * HEAD_DIM, :length], grad_scores)
            kept[head] = (probs.astype(BF), grad_scores, own_query, own_grad, back)
            if head == 1:
                probs2, scores2 = [
                    jnp.concatenate([kept[0][n], kept[1][n]], 1) for n in range(2)
                ]
                query2, grad2 = [
                    jnp.concatenate([kept[0][n], kept[1][n]], 0) for n in range(2, 4)
                ]
                new_values = nn(probs2, grad2)
                new_keys = nn(scores2, query2)
                if i == count - 1:
                    sums[0][...] = new_keys
                    sums[1][...] = new_values
                else:
                    sums[0][:length] += new_keys
                    sums[1][:length] += new_values
                grad_query[0][place, columns(grad_query[1])] = (
                    jnp.concatenate([kept[0][4], kept[1][4]], 0).T * SCALE
                ).astype(BF)

        before = None
        for i in reversed(range(count)):
            for head in range(2):
                state = first(i, head)
                if before is not None:
                    second(*before)
                before = (i, head, state)
        second(*before)
        grad_keys[0][:, columns(grad_keys[1])] = (sums[0][...] * SCALE).astype(BF)
        grad_values[0][:, columns(grad_values[1])] = sums[1][...].astype(BF)
        if hook is not None:
            hook(hp)
        return 0

    lax.fori_loop(0, PAIRS, pair, 0)


def slot_of(routes, group, device, size):
    own = routes[group]
    rank = lax.fori_loop(
        0, group, lambda j, c: c + jnp.where(routes[j] == own, 1, 0).astype(jnp.int32), jnp.int32(0)
    )
    return partner_of(device, own, size) * CAPACITY + rank


def weigh(values, weight):
    return values * jnp.full(values.shape, weight.astype(F32), F32).astype(BF)


def pick_group(routes, source, group_rows, expert, rank):
    count = jnp.int32(0)
    total = None
    for group in range(source.shape[0] // group_rows):
        same = jnp.where(routes[group] == expert, 1, 0).astype(jnp.int32)
        hit = same * jnp.where(count == rank, 1, 0).astype(jnp.int32)
        count = count + same
        term = weigh(source[group * group_rows : (group + 1) * group_rows], hit)
        total = term if total is None else total + term
    return total


def partner_of(own, offset, size):
    result, bit = 0, 1
    while bit < size:
        result = result + lax.rem(own // bit + offset // bit, 2) * bit
        bit *= 2
    return result


ROWS = 256
MESH = pl.DeviceIdType.MESH
Q, K, V, ATTN, CQ, MK, MV, CROSS, ATTN_T, CROSS_T = range(10)
SAVED = 10


def forward_kernel(
    size,
    group_rows,
    routes,
    self_gain,
    self_shift,
    cross_gain,
    cross_shift,
    moe_gain,
    moe_shift,
    up_bias,
    down_bias,
    *refs,
):
    (
        x_h, memory_h, grad_h, project_h, output_h, query_h, memory_w_h, cross_w_h, up_h, down_h,
        saved_o, hidden1_o, hidden2_o, rows_out_o, returned_o, half_own_o, half_other_o,
        total1, total2, biases,
        x, memory, grad, self_project, self_output, cross_query, cross_memory, cross_output, up, down,
        arena, hidden1, hidden2, normed3, outbound, received, received_grad, flat_t, grad_t, halves,
        in_sems, out_sems, core_sems, grad_send, grad_recv, row_send, row_recv, back_send, back_recv,
    ) = refs
    rows, width = x.shape
    wide = up.shape[1]
    blocks = rows // ROWS
    part_rows = CAPACITY * group_rows
    slot_rows = size * part_rows
    batch, own = lax.axis_index("batch"), lax.axis_index("exp")

    layers = lax.axis_size("batch") // 2
    half = halves.shape[0] // 2
    piece = half // layers
    core, other = lax.rem(batch, 2), 1 - lax.rem(batch, 2)
    twin = (batch + other - core, own)

    def partner(offset):
        return (batch, partner_of(own, offset, size))

    loads = [
        pltpu.make_async_copy(source, target, in_sems.at[n])
        for n, (source, target) in enumerate(
            [
                (grad_h, grad), (x_h, x), (project_h, self_project), (memory_h, memory),
                (memory_w_h, cross_memory), (output_h, self_output), (query_h, cross_query),
                (cross_w_h, cross_output), (up_h, up), (down_h, down),
            ]
        )
    ]
    for load in loads:
        load.start()
    barrier = pltpu.get_barrier_semaphore()
    for offset in range(1, size):
        pl.semaphore_signal(barrier, inc=1, device_id=partner(offset), device_id_type=MESH)
    pl.semaphore_signal(barrier, inc=1, device_id=twin, device_id_type=MESH)
    pl.semaphore_wait(barrier, size)

    def part(ref, offset):
        return ref.at[pl.ds(pl.multiple_of(offset * part_rows, part_rows), part_rows)]

    def send(source, target, offset, send_sems, recv_sems):
        return pltpu.make_async_remote_copy(
            src_ref=part(source, offset),
            dst_ref=part(target, offset),
            send_sem=send_sems.at[offset],
            recv_sem=recv_sems.at[offset],
            device_id=partner(offset),
            device_id_type=MESH,
        )

    def dispatch(source, target, offset):
        expert = partner_of(own, offset, size)

        def one(rank, _):
            values = pick_group(routes, source, group_rows, expert, rank)
            target[pl.ds(pl.multiple_of(offset * part_rows + rank * group_rows, group_rows), group_rows)] = values
            return 0

        lax.fori_loop(0, CAPACITY, one, 0)

    def to_all(source, target, send_sems, recv_sems):
        dispatch(source, target, 0)

        def one(offset, _):
            dispatch(source, outbound, offset)
            send(outbound, target, offset, send_sems, recv_sems).start()
            return 0

        lax.fori_loop(1, size, one, 0)

    loads[0].wait()
    to_all(grad, received_grad, grad_send, grad_recv)
    for load in loads[1:5]:
        load.wait()

    def place(which):
        return arena.at[pl.ds(which * rows, rows)]

    q, k, v, attn, cq, mk, mv, cross, attn_t, cross_t = [place(n) for n in range(SAVED)]

    def block1(i, _):
        here = span(i, ROWS)
        hat, _s = normalize(x[here].astype(F32))
        normed = (hat * self_gain[...] + self_shift[...]).astype(BF)
        for n, target in enumerate((q, k, v)):
            target[here] = nn(normed, self_project[:, n * width : (n + 1) * width]).astype(BF)
        for n, target in enumerate((mk, mv)):
            target[here] = nn(memory[here], cross_memory[:, n * width : (n + 1) * width]).astype(BF)
        return 0

    lax.fori_loop(0, blocks, block1, 0)
    attend((q, 0), (k, 0), (v, 0), attn, attn_t, total1, True)
    for load in loads[5:]:
        load.wait()

    def block2(i, _):
        here = span(i, ROWS)
        hidden = x[here].astype(F32) + nn(attn[here], self_output[...])
        hidden1[here] = hidden
        hat, _s = normalize(hidden)
        normed = (hat * cross_gain[...] + cross_shift[...]).astype(BF)
        cq[here] = nn(normed, cross_query[...]).astype(BF)
        return 0

    lax.fori_loop(0, blocks, block2, 0)
    attend((cq, 0), (mk, 0), (mv, 0), cross, cross_t, total2, False)
    stores = [
        pltpu.make_async_copy(arena.at[pl.ds(0, SAVED * rows)], saved_o, out_sems.at[0]),
        pltpu.make_async_copy(hidden1, hidden1_o, out_sems.at[1]),
        pltpu.make_async_copy(hidden2, hidden2_o, out_sems.at[2]),
    ]
    stores[0].start()
    stores[1].start()

    def block3(i, _):
        here = span(i, ROWS)
        hidden = hidden1[here] + nn(cross[here], cross_output[...])
        hidden2[here] = hidden
        hat, _s = normalize(hidden)
        normed3[here] = (hat * moe_gain[...] + moe_shift[...]).astype(BF)
        return 0

    lax.fori_loop(0, blocks, block3, 0)
    stores[2].start()

    def sent(source, target, send_sems, recv_sems):
        def one(offset, _):
            send(source, target, offset, send_sems, recv_sems).wait_send()
            return 0

        lax.fori_loop(1, size, one, 0)

    sent(outbound, received_grad, grad_send, grad_recv)
    to_all(normed3, received, row_send, row_recv)
    stores[0].wait()

    block_rows = max(512, part_rows)
    per = block_rows // part_rows
    chunk = 512
    first, third = math.sqrt(2.0 / math.pi), math.sqrt(2.0 / math.pi) * 0.044715
    flat_t[width:] = jnp.ones((flat_t.shape[0] - width, slot_rows), BF)

    def hidden_at(c, start, length):
        return arena.at[pl.ds(pl.multiple_of(c * slot_rows + start, block_rows), length)]

    def pre_at(c, start, length):
        return arena.at[
            pl.ds(pl.multiple_of((wide // chunk + c) * slot_rows + start, block_rows), length)
        ]

    def block(i, bias):
        for n in range(per):
            offset = i * per + n

            @pl.when(offset > 0)
            def _():
                send(outbound, received_grad, offset, grad_send, grad_recv).wait_recv()
                send(outbound, received, offset, row_send, row_recv).wait_recv()

        here = span(i, block_rows)
        flat = received[here]
        grads = received_grad[here]
        flat_t[:width, here] = flat.T
        grad_t[:, here] = grads.T
        out = jnp.zeros((block_rows, width), F32)
        back = jnp.zeros((block_rows, width), F32)
        for c in range(wide // chunk):
            cols = pl.ds(c * chunk, chunk)
            pre = nn(flat, up[:, cols]) + up_bias[:, cols]
            square = pre * pre
            half = 0.5 + 0.5 * jnp.tanh(pre * (first + third * square))
            value = pre * half
            low = value.astype(BF)
            slope = half + value * (1.0 - half) * (2.0 * first + (6.0 * third) * square)
            gpre = (nt(grads, down[cols]) * slope).astype(BF)
            hidden_at(c, i * block_rows, block_rows)[...] = low
            pre_at(c, i * block_rows, block_rows)[...] = gpre
            out += nn(low, down[cols])
            back += nt(gpre, up[:, cols])
        received[here] = (out + down_bias[...]).astype(BF)
        received_grad[here] = back.astype(BF)
        for n in range(per):
            offset = i * per + n

            @pl.when(offset > 0)
            def _():
                send(received_grad, returned_o, offset, back_send, back_recv).start()

        return bias + jnp.sum(grads.astype(F32), 0, keepdims=True)

    bias = lax.fori_loop(0, slot_rows // block_rows, block, jnp.zeros((1, width), F32))
    stores.append(
        pltpu.make_async_copy(part(received_grad, 0), part(returned_o, 0), out_sems.at[3])
    )
    stores.append(pltpu.make_async_copy(received, rows_out_o, out_sems.at[4]))
    stores[3].start()
    stores[4].start()
    up_rows, down_rows = width // (2 * layers), wide // (2 * layers)
    biases[...] = jnp.zeros_like(biases)
    per_chunk = chunk // down_rows

    def piece_at(number, start, length):
        row = lax.rem(number, 2) * half + number // 2 * piece + start
        return halves.at[pl.ds(pl.multiple_of(row, length), length)]

    def weights(c, _):
        cols = span(c, chunk)
        both = nn(flat_t[...], pre_at(c, 0, slot_rows)[...])
        for n in range(2 * layers):
            piece_at(jnp.int32(n), c * up_rows, up_rows)[...] = both[
                n * up_rows : (n + 1) * up_rows
            ].astype(BF)
        biases[pl.ds(c, 1)] = both[width : width + 1]
        down_t = nn(grad_t[...], hidden_at(c, 0, slot_rows)[...])
        for n in range(per_chunk):
            piece_at(c * per_chunk + n, wide // chunk * up_rows, down_rows)[...] = down_t[
                :, n * down_rows : (n + 1) * down_rows
            ].T.astype(BF)
        return 0

    lax.fori_loop(0, wide // chunk, weights, 0)
    biases[wide // chunk : wide // chunk + 1] = bias

    def half_at(which):
        return halves.at[pl.ds(pl.multiple_of(which * half, half), half)]

    to_twin = pltpu.make_async_remote_copy(
        src_ref=half_at(other),
        dst_ref=half_other_o,
        send_sem=core_sems.at[0],
        recv_sem=core_sems.at[1],
        device_id=twin,
        device_id_type=MESH,
    )
    to_twin.start()
    stores.append(pltpu.make_async_copy(half_at(core), half_own_o, out_sems.at[5]))
    stores[5].start()
    sent(outbound, received, row_send, row_recv)
    sent(received_grad, returned_o, back_send, back_recv)

    def arrived(offset, _):
        send(received_grad, returned_o, offset, back_send, back_recv).wait_recv()
        return 0

    lax.fori_loop(1, size, arrived, 0)
    to_twin.wait()
    for store in stores[1:]:
        store.wait()


MATS = 8


def back_kernel(
    size,
    layers,
    group_rows,
    routes,
    self_gain,
    self_shift,
    cross_gain,
    cross_shift,
    moe_gain,
    moe_shift,
    total1,
    total2,
    biases,
    *refs,
):
    (
        x_h, memory_h, grad_h, project_h, output_h, query_h, memory_w_h, cross_w_h,
        saved_h, hidden1_h, hidden2_h, returned_grad_h, rows_out_h, half_own_h, half_other_h,
        layer_o, grad_input_o, grad_memory_o, reduced_o, returned_o,
        small, up_o, down_o, bias_o,
        x, memory, grad, self_project, self_output, cross_query, cross_memory, cross_output,
        saved, hidden1, hidden2, returned,
        carried, carried_low, back_low, grad_q, grad_kv, grad_project, normed, sum_a, sum_b,
        grads, from_twin, from_exp, part, from_layer, shard,
        half, from_half, from_small, from_bias,
        in_sems, out_sems, ret_send, ret_recv, half_send, half_recv, bias_send, bias_recv,
        small_send, small_recv, sends, recvs,
    ) = refs
    rows, width = x.shape
    wide = up_o.shape[1]
    blocks = rows // ROWS
    per = ROWS // group_rows
    part_rows = CAPACITY * group_rows
    zero = jnp.zeros((1, width), F32)
    batch, own = lax.axis_index("batch"), lax.axis_index("exp")
    core, layer = lax.rem(batch, 2), batch // 2
    twin = (batch + 1 - 2 * core, own)

    def partner(offset):
        return (batch, partner_of(own, offset, size))

    def above(offset):
        return lax.rem(layer + offset, layers)

    def column(offset):
        return (above(offset) * 2 + core, own)

    pairs = [
        (hidden2_h, hidden2), (returned_grad_h, returned), (grad_h, grad), (cross_w_h, cross_output),
        (half_own_h, half), (half_other_h, grad_kv), (saved_h, saved), (hidden1_h, hidden1),
        (query_h, cross_query), (memory_w_h, cross_memory), (output_h, self_output), (memory_h, memory),
        (x_h, x), (project_h, self_project),
    ]
    loads = [pltpu.make_async_copy(*pair, in_sems.at[n]) for n, pair in enumerate(pairs)]
    for load in loads:
        load.start()
    barrier = pltpu.get_barrier_semaphore()
    greeted = (
        [twin] + [partner(n) for n in range(1, size)] + [column(n) for n in range(1, layers)]
    )
    for device in greeted:
        pl.semaphore_signal(barrier, inc=1, device_id=device, device_id_type=MESH)
    pl.semaphore_wait(barrier, len(greeted))

    def remote(source, target, device, send_sem, recv_sem):
        return pltpu.make_async_remote_copy(
            src_ref=source,
            dst_ref=target,
            send_sem=send_sem,
            recv_sem=recv_sem,
            device_id=device,
            device_id_type=MESH,
        )

    def start_all(copies):
        for copy in copies:
            copy.start()

    def wait_all(copies):
        for copy in copies:
            copy.wait()

    def slots(ref, offset):
        return ref.at[pl.ds(offset * part_rows, part_rows)]

    back_rows = [
        remote(slots(rows_out_h, n), slots(returned_o, n), partner(n), ret_send.at[n], ret_recv.at[n])
        for n in range(1, size)
    ]
    start_all(back_rows)
    own_rows = pltpu.make_async_copy(slots(rows_out_h, 0), slots(returned_o, 0), out_sems.at[0])
    own_rows.start()

    q, k, v, attn, cross_q, mk, mv, cross, attn_t, cross_t = [
        saved.at[pl.ds(n * rows, rows)] for n in range(SAVED)
    ]
    gq, gk, gv = [grad_project.at[pl.ds(n * rows, rows)] for n in range(3)]
    gmk, gmv = [grad_kv.at[pl.ds(n * rows, rows)] for n in range(2)]

    def mat(number):
        return slice(number * width, (number + 1) * width)

    def times(turned, right):
        count = 512
        return sum(
            nn(turned[n * width : (n + 1) * width], right[n * count : (n + 1) * count])
            for n in range(rows // count)
        )

    def gather(source, group, place):
        expert = partner_of(own, routes[group], size)
        rank = lax.fori_loop(
            0,
            group,
            lambda j, c: c + jnp.where(routes[j] == routes[group], 1, 0).astype(jnp.int32),
            jnp.int32(0),
        )
        slot = expert * CAPACITY + rank
        total = None
        for n in range(size * CAPACITY):
            hit = jnp.where(slot == n, 1, 0).astype(jnp.int32)
            term = weigh(source[n * group_rows : (n + 1) * group_rows], hit)
            total = term if total is None else total + term
        place[span(group, group_rows)] = total

    def gather_all(source, place):
        def one(group, _):
            gather(source, group, place)
            return 0

        lax.fori_loop(0, rows // group_rows, one, 0)

    tall = grads.shape[0]
    by_core = tall // 2
    by_exp = by_core // size
    split = layers if (by_exp // layers) % 16 == 0 else 1
    by_layer = by_exp // split
    counter = [0]

    def pair_of_sems():
        counter[0] += 1
        return sends.at[counter[0] - 1], recvs.at[counter[0] - 1]

    def reduction(first, last):
        cols = pl.ds(first, last - first)

        def lane(ref, start, length):
            return ref.at[pl.ds(pl.multiple_of(start, length), length), cols]

        mine = core * by_core
        core_copies = [
            remote(lane(grads, (1 - core) * by_core, by_core), from_twin.at[:, cols], twin, *pair_of_sems())
        ]
        exp_copies = [
            remote(
                lane(grads, mine + partner_of(own, n, size) * by_exp, by_exp),
                from_exp.at[n - 1, :, cols],
                partner(n),
                *pair_of_sems(),
            )
            for n in range(1, size)
        ]
        at_layer = layer * by_layer if split > 1 else 0
        layer_copies = [
            remote(
                lane(part, above(n) * by_layer if split > 1 else 0, by_layer),
                from_layer.at[n - 1, :, cols],
                column(n),
                *pair_of_sems(),
            )
            for n in range(1, layers)
        ]
        share_copies = [
            remote(
                lane(shard, at_layer, by_layer),
                lane(shard, at_layer, by_layer),
                column(n),
                *pair_of_sems(),
            )
            for n in range(1, layers)
        ] if split > 1 else []
        spot = mine + own * by_exp
        out_copies = [
            remote(shard.at[:, cols], lane(reduced_o, spot, by_exp), partner(n), *pair_of_sems())
            for n in range(1, size)
        ]
        local = pltpu.make_async_copy(shard.at[:, cols], lane(reduced_o, spot, by_exp), pair_of_sems()[0])
        half_copies = [
            remote(lane(reduced_o, mine, by_core), lane(reduced_o, mine, by_core), twin, *pair_of_sems())
        ]

        def stage(number):
            if number == 0:
                start_all(core_copies)
            if number == 1:
                wait_all(core_copies)

                def add(i, _):
                    here = pl.ds(pl.multiple_of(mine + i * 64, 64), 64)
                    grads[here, cols] = (
                        grads[here, cols].astype(F32) + from_twin[span(i, 64), cols].astype(F32)
                    ).astype(BF)
                    return 0

                lax.fori_loop(0, by_core // 64, add, 0)
                start_all(exp_copies)
            if number == 2:
                wait_all(exp_copies)
                here = pl.ds(pl.multiple_of(spot, by_exp), by_exp)
                total = grads[here, cols].astype(F32)
                for n in range(size - 1):
                    total = total + from_exp[n, :, cols].astype(F32)
                part[:, cols] = total.astype(BF)
                start_all(layer_copies)
            if number == 3:
                wait_all(layer_copies)
                here = pl.ds(pl.multiple_of(at_layer, by_layer), by_layer)
                total = part[here, cols].astype(F32)
                for n in range(layers - 1):
                    total = total + from_layer[n, :, cols].astype(F32)
                shard[here, cols] = total.astype(BF)
                start_all(share_copies)
            if number == 4:
                wait_all(share_copies)
                start_all(out_copies)
                local.start()
            if number == 5:
                wait_all(out_copies)
                local.wait()
                start_all(half_copies)
            if number == 6:
                wait_all(half_copies)

        return stage

    late = reduction(0, 3 * width)
    early = reduction(3 * width, MATS * width)

    for load in loads[:4]:
        load.wait()
    gather_all(returned, carried_low)

    def block3(i, carry):
        here = span(i, ROWS)
        hat, scale = normalize(hidden2[here])
        gy = carried_low[here].astype(F32)
        total = grad[here].astype(F32) + normalize_back(hat, scale, gy, moe_gain[...])
        carried[here] = total
        low = total.astype(BF)
        carried_low[here] = low
        back_low[here] = nt(low, cross_output[...]).astype(BF)
        return (
            carry[0] + jnp.sum(gy * hat, 0, keepdims=True),
            carry[1] + jnp.sum(gy, 0, keepdims=True),
        )

    gains3 = lax.fori_loop(0, blocks, block3, (zero, zero))

    for load in loads[4:6]:
        load.wait()

    def add_half(i, _):
        here = span(i, ROWS)
        half[here] = (half[here].astype(F32) + grad_kv[here].astype(F32)).astype(BF)
        return 0

    lax.fori_loop(0, half.shape[0] // ROWS, add_half, 0)
    piece = half.shape[0] // layers
    pieces = [
        remote(
            half.at[pl.ds(pl.multiple_of(above(n) * piece, piece), piece)],
            from_half.at[n - 1],
            column(n),
            half_send.at[n],
            half_recv.at[n],
        )
        for n in range(1, layers)
    ]
    start_all(pieces)
    bias_twin = [remote(biases, from_bias.at[0], twin, bias_send.at[0], bias_recv.at[0])]
    start_all(bias_twin)
    for load in loads[6:]:
        load.wait()
    grads[:, mat(7)] = times(cross_t, carried_low).astype(BF)
    attend_back(
        (cross_q, 0), (mk, 0), (mv, 0), back_low, cross, total2,
        (grad_q, 0), (gmk, 0), (gmv, 0), (sum_a, sum_b), False, 256,
    )

    def block2(i, carry):
        here = span(i, ROWS)
        hat, scale = normalize(hidden1[here])
        normed[here] = (hat * cross_gain[...] + cross_shift[...]).astype(BF)
        gy = nt(grad_q[here], cross_query[...])
        total = carried[here] + normalize_back(hat, scale, gy, cross_gain[...])
        carried[here] = total
        low = total.astype(BF)
        carried_low[here] = low
        back_low[here] = nt(low, self_output[...]).astype(BF)
        return (
            carry[0] + jnp.sum(gy * hat, 0, keepdims=True),
            carry[1] + jnp.sum(gy, 0, keepdims=True),
        )

    gains2 = lax.fori_loop(0, blocks, block2, (zero, zero))
    grads[:, mat(4)] = tn(normed[...], grad_q[...]).astype(BF)
    grads[:, mat(5)] = tn(memory[...], gmk[...]).astype(BF)
    grads[:, mat(6)] = tn(memory[...], gmv[...]).astype(BF)
    grads[:, mat(3)] = times(attn_t, carried_low).astype(BF)
    early(0)
    wait_all(bias_twin)
    biases[...] += from_bias[0]
    bias_layers = [
        remote(biases, from_bias.at[n], column(n), bias_send.at[n], bias_recv.at[n])
        for n in range(1, layers)
    ]
    start_all(bias_layers)

    def hook(hp):
        @pl.when(hp == 0)
        def _():
            early(1)

    attend_back(
        (q, 0), (k, 0), (v, 0), back_low, attn, total1,
        (gq, 0), (gk, 0), (gv, 0), (sum_a, sum_b), True, 256, hook,
    )
    early(2)

    def renormed(i, _):
        here = span(i, ROWS)
        hat, _s = normalize(x[here].astype(F32))
        normed[here] = (hat * self_gain[...] + self_shift[...]).astype(BF)
        return 0

    lax.fori_loop(0, blocks, renormed, 0)
    for n, ref in enumerate((gq, gk, gv)):
        grads[:, mat(n)] = tn(normed[...], ref[...]).astype(BF)
    late(0)
    early(3)

    def block1(i, carry):
        here = span(i, ROWS)
        hat, scale = normalize(x[here].astype(F32))
        gy = sum(
            nt(ref[here], self_project[:, mat(n)]) for n, ref in enumerate((gq, gk, gv))
        )
        carried[here] += normalize_back(hat, scale, gy, self_gain[...])
        return (
            carry[0] + jnp.sum(gy * hat, 0, keepdims=True),
            carry[1] + jnp.sum(gy, 0, keepdims=True),
        )

    gains1 = lax.fori_loop(0, blocks, block1, (zero, zero))
    stores = [pltpu.make_async_copy(carried, grad_input_o, out_sems.at[1])]
    stores[0].start()
    late(1)
    early(4)
    small[...] = jnp.concatenate([*gains1, *gains2, *gains3, zero, zero], 0)

    def share_small(number, devices):
        copies = [
            remote(small, from_small.at[number + n], device, small_send.at[number + n], small_recv.at[number + n])
            for n, device in enumerate(devices)
        ]
        start_all(copies)

        def finish():
            wait_all(copies)
            total = small[...]
            for n in range(len(devices)):
                total = total + from_small[number + n]
            small[...] = total

        return finish

    finish = share_small(0, [twin])

    wait_all(back_rows)
    own_rows.wait()
    fetch = pltpu.make_async_copy(returned_o, returned, out_sems.at[2])
    fetch.start()
    finish()
    finish = share_small(1, [partner(n) for n in range(1, size)])

    def memory_block(i, _):
        here = span(i, ROWS)
        hidden1[here] = nt(gmk[here], cross_memory[:, :width]) + nt(gmv[here], cross_memory[:, width:])
        return 0

    lax.fori_loop(0, rows // ROWS, memory_block, 0)
    stores.append(pltpu.make_async_copy(hidden1, grad_memory_o, out_sems.at[3]))
    stores[1].start()
    fetch.wait()
    gather_all(returned, normed)

    def output_block(i, _):
        here = span(i, ROWS)
        grad[here] = (hidden2[here] + normed[here].astype(F32)).astype(BF)
        return 0

    lax.fori_loop(0, blocks, output_block, 0)
    stores.append(pltpu.make_async_copy(grad, layer_o, out_sems.at[4]))
    stores[2].start()
    finish()
    finish = share_small(size, [column(n) for n in range(1, layers)])
    late(2)
    early(5)
    wait_all(pieces)
    up_rows = up_o.shape[0]
    base = layer * piece
    for c in range(wide // width):
        total = half[pl.ds(pl.multiple_of(base + c * up_rows, up_rows), up_rows)].astype(F32)
        for n in range(layers - 1):
            total = total + from_half[n, c * up_rows : (c + 1) * up_rows].astype(F32)
        up_o[:, c * width : (c + 1) * width] = total
    down_rows = down_o.shape[0]
    start = wide // width * up_rows
    total = half[pl.ds(pl.multiple_of(base + start, down_rows), down_rows)].astype(F32)
    for n in range(layers - 1):
        total = total + from_half[n, start : start + down_rows].astype(F32)
    down_o[...] = total
    wait_all(bias_layers)
    total = biases[...]
    for n in range(1, layers):
        total = total + from_bias[n]
    bias_o[...] = total
    late(3)
    early(6)
    finish()
    late(4)
    late(5)
    late(6)
    for store in stores:
        store.wait()


def finish_kernel(reduced, project, output, query, memory, cross):
    width = output.shape[1]
    column = 0
    for target in (project, output, query, memory, cross):
        size = target.shape[1]
        target[...] = reduced[:, column : column + size].astype(F32)
        column += size


def body(
    layer_input,
    memory,
    routes,
    out_grad,
    self_gain,
    self_shift,
    self_project,
    self_output,
    cross_gain,
    cross_shift,
    cross_query,
    cross_memory,
    cross_output,
    moe_gain,
    moe_shift,
    expert_up,
    up_bias,
    expert_down,
    down_bias,
):
    x = layer_input[0]
    memory = memory[0]
    grad = out_grad[0]
    rows, width = x.shape
    wide = expert_up.shape[2]
    size = lax.axis_size("exp")
    groups = routes.shape[1]
    group_rows = rows // groups
    slot_rows = size * CAPACITY * group_rows
    route = routes.reshape(groups)
    gains = [v.reshape(1, width) for v in (self_gain, self_shift, cross_gain, cross_shift, moe_gain, moe_shift)]
    def array(shape, dtype):
        return jax.ShapeDtypeStruct(shape, dtype)

    vmem, smem, any_ = [pl.BlockSpec(memory_space=m) for m in (pltpu.VMEM, pltpu.SMEM, pl.ANY)]
    big = [
        x, memory, grad, self_project, self_output, cross_query, cross_memory, cross_output,
        expert_up[0], expert_down[0],
    ]
    sems = pltpu.SemaphoreType.DMA((size,))
    saved, hidden1, hidden2, rows_out, returned_grad, half_own, half_other, total1, total2, biases = pl.pallas_call(
        functools.partial(forward_kernel, size, group_rows),
        out_shape=(
            array((SAVED * rows, width), BF),
            array((rows, width), F32),
            array((rows, width), F32),
            array((slot_rows, width), BF),
            array((slot_rows, width), BF),
            array((wide, width), BF),
            array((wide, width), BF),
            array((PAIRS, 8, rows), F32),
            array((PAIRS, 8, rows), F32),
            array((8, width), F32),
        ),
        in_specs=[smem] + [vmem] * 8 + [any_] * 10,
        out_specs=(any_,) * 7 + (vmem,) * 3,
        scratch_shapes=[pltpu.VMEM(v.shape, v.dtype) for v in big]
        + [
            pltpu.VMEM(shape, dtype)
            for shape, dtype in [
                ((2 * slot_rows * (wide // 512), 512), BF),
                ((rows, width), F32),
                ((rows, width), F32),
                ((rows, width), BF),
                ((slot_rows, width), BF),
                ((slot_rows, width), BF),
                ((slot_rows, width), BF),
                ((width + 16, slot_rows), BF),
                ((width, slot_rows), BF),
                ((2 * wide, width), BF),
            ]
        ]
        + [pltpu.SemaphoreType.DMA((10,)), pltpu.SemaphoreType.DMA((6,)), pltpu.SemaphoreType.DMA((2,))]
        + [sems] * 6,
        compiler_params=pltpu.CompilerParams(
            collective_id=0, has_side_effects=True, vmem_limit_bytes=62 << 20
        ),
        cost_estimate=pl.CostEstimate(flops=60 * 10**9, bytes_accessed=40 << 20, transcendentals=0),
    )(route, *gains, up_bias, down_bias, *big)
    layers = lax.axis_size("batch") // 2
    by_exp = width // 2 // size
    by_layer = by_exp // layers if (by_exp // layers) % 16 == 0 else by_exp
    piece = wide // layers
    back_in = [
        *big[:8], saved, hidden1, hidden2, returned_grad, rows_out, half_own, half_other,
    ]
    count = 2 * (4 + 2 * (size - 1) + 2 * (layers - 1))
    dma = pltpu.SemaphoreType.DMA
    (
        layer_output, grad_input, grad_memory, reduced, _returned, small, grad_up, grad_down, biases,
    ) = pl.pallas_call(
        functools.partial(back_kernel, size, layers, group_rows),
        out_shape=(
            array((rows, width), BF),
            array((rows, width), F32),
            array((rows, width), F32),
            array((width, MATS * width), BF),
            array((slot_rows, width), BF),
            array((8, width), F32),
            array((width // (2 * layers), wide), F32),
            array((wide // (2 * layers), width), F32),
            array((8, width), F32),
        ),
        in_specs=[smem] + [vmem] * 9 + [any_] * len(back_in),
        out_specs=(any_,) * 5 + (vmem,) * 4,
        scratch_shapes=[pltpu.VMEM(v.shape, v.dtype) for v in big[:8]]
        + [
            pltpu.VMEM(shape, dtype)
            for shape, dtype in [
                (saved.shape, BF),
                ((rows, width), F32),
                ((rows, width), F32),
                ((slot_rows, width), BF),
                ((rows, width), F32),
                ((rows, width), BF),
                ((rows, width), BF),
                ((rows, width), BF),
                ((2 * rows, width), BF),
                ((3 * rows, width), BF),
                ((rows, width), BF),
                ((rows, PAIR), F32),
                ((rows, PAIR), F32),
                ((width, MATS * width), BF),
                ((width // 2, MATS * width), BF),
                ((size - 1, by_exp, MATS * width), BF),
                ((by_exp, MATS * width), BF),
                ((layers - 1, by_layer, MATS * width), BF),
                ((by_exp, MATS * width), BF),
                ((wide, width), BF),
                ((layers - 1, piece, width), BF),
                ((size + layers - 1, 8, width), F32),
                ((layers, 8, width), F32),
            ]
        ]
        + [dma((14,)), dma((5,)), sems, sems]
        + [dma((layers,))] * 4
        + [dma((size + layers - 1,))] * 2
        + [dma((count,))] * 2,
        compiler_params=pltpu.CompilerParams(
            collective_id=1, has_side_effects=True, vmem_limit_bytes=63 << 20
        ),
        cost_estimate=pl.CostEstimate(flops=60 * 10**9, bytes_accessed=40 << 20, transcendentals=0),
    )(route, *gains, total1, total2, biases, *back_in)
    shapes = [(width, 3 * width), (width, width), (width, width), (width, 2 * width), (width, width)]
    steps = 4
    grad_self_project, grad_self_output, grad_cross_query, grad_cross_memory, grad_cross_output = pl.pallas_call(
        finish_kernel,
        grid=(steps,),
        out_shape=tuple(array(shape, F32) for shape in shapes),
        in_specs=[pl.BlockSpec((width // steps, MATS * width), lambda i: (i, 0))],
        out_specs=tuple(pl.BlockSpec((width // steps, shape[1]), lambda i: (i, 0)) for shape in shapes),
    )(reduced)
    index = lax.axis_index("batch")
    up_bias_sum = lax.dynamic_slice_in_dim(
        biases[: wide // width].reshape(1, wide), index * (wide // (2 * layers)), wide // (2 * layers), 1
    )
    down_bias_sum = lax.dynamic_slice_in_dim(
        biases[wide // width : wide // width + 1], index * (width // (2 * layers)), width // (2 * layers), 1
    )
    return (
        layer_output[None],
        grad_input[None],
        grad_memory[None],
        small[0],
        small[1],
        grad_self_project,
        grad_self_output,
        small[2],
        small[3],
        grad_cross_query,
        grad_cross_memory,
        grad_cross_output,
        small[4],
        small[5],
        grad_up[None],
        up_bias_sum,
        grad_down[None],
        down_bias_sum,
    )


def solution(mesh):
    return jax.shard_map(
        body,
        mesh=mesh,
        in_specs=(
            P(("batch", "exp"), None, None),
            P(("batch", "exp"), None, None),
            P(("batch", "exp"), None, None),
            P(("batch", "exp"), None, None),
            P(),
            P(),
            P(),
            P(),
            P(),
            P(),
            P(),
            P(),
            P(),
            P(),
            P(),
            P("exp", None, None),
            P("exp", None),
            P("exp", None, None),
            P("exp", None),
        ),
        out_specs=(
            P(("batch", "exp"), None, None),
            P(("batch", "exp"), None, None),
            P(("batch", "exp"), None, None),
            P(),
            P(),
            P(),
            P(),
            P(),
            P(),
            P(),
            P(),
            P(),
            P(),
            P(),
            P("exp", "batch", None),
            P("exp", "batch"),
            P("exp", "batch", None),
            P("exp", "batch"),
        ),
        check_vma=False,
    )
```

```python
import functools
import math

import jax
import jax.numpy as jnp
from jax import lax
from jax.experimental import pallas as pl
from jax.experimental.pallas import tpu as pltpu
from jax.sharding import PartitionSpec as P

HEADS = 8
HEAD_DIM = 64
CAPACITY = 4
PAIR = 2 * HEAD_DIM
PAIRS = HEADS // 2
EPSILON = 1e-05
NEGATIVE = -1e30
SCALE = HEAD_DIM ** (-0.5)
SCALE2 = SCALE * math.log2(math.e)
BF = jnp.bfloat16
F32 = jnp.float32


def nn(left, right):
    return lax.dot_general(left, right, (((1,), (0,)), ((), ())), preferred_element_type=F32)


def nt(left, right):
    return lax.dot_general(left, right, (((1,), (1,)), ((), ())), preferred_element_type=F32)


def tn(left, right):
    return lax.dot_general(left, right, (((0,), (0,)), ((), ())), preferred_element_type=F32)


def span(index, size):
    return pl.ds(pl.multiple_of(index * size, size), size)


def normalize(values):
    center = values - jnp.mean(values, -1, keepdims=True)
    scale = lax.rsqrt(jnp.mean(center * center, -1, keepdims=True) + EPSILON)
    return center * scale, scale


def normalize_back(hat, scale, grad, gain):
    gained = grad * gain
    first = jnp.mean(gained, -1, keepdims=True)
    second = jnp.mean(gained * hat, -1, keepdims=True)
    return scale * (gained - first - hat * second)


def causal_mask(scores, block, causal):
    length = scores.shape[0]
    if not causal:
        return scores
    key = lax.broadcasted_iota(jnp.int32, (block, block), 0)
    row = lax.broadcasted_iota(jnp.int32, (block, block), 1)
    last = jnp.where(row >= key, scores[length - block :], NEGATIVE)
    if length == block:
        return last
    return jnp.concatenate([scores[: length - block], last], 0)


def own_head(values, head):
    lane = lax.broadcasted_iota(jnp.int32, values.shape, 1) < HEAD_DIM
    return jnp.where(lane if head == 0 else ~lane, values, jnp.zeros_like(values))


def attend(query, keys, values, out, out_t, total, causal, block=512):
    rows = out.shape[0]
    count = rows // block

    def pair(hp, _):
        def columns(column):
            return pl.ds(pl.multiple_of(column + hp * PAIR, PAIR), PAIR)

        two_keys = keys[0][:, columns(keys[1])]
        values_t = values[0][:, columns(values[1])].T
        results = {}

        def first(i, head):
            length = (i + 1) * block if causal else two_keys.shape[0]
            own = own_head(query[0][i * block : (i + 1) * block, columns(query[1])], head)
            return causal_mask(nt(two_keys[:length], own), block, causal)

        def second(i, head, scores):
            length = scores.shape[0]
            place = pl.ds(i * block, block)
            highest = jnp.max(scores, 0, keepdims=True)
            weights = jnp.exp2(scores * SCALE2 - highest * SCALE2).astype(BF)
            extended = jnp.concatenate(
                [
                    values_t[head * HEAD_DIM : (head + 1) * HEAD_DIM, :length],
                    jnp.ones((16, length), BF),
                ],
                0,
            )
            summed = nn(extended, weights)
            sums = summed[HEAD_DIM : HEAD_DIM + 1]
            total[hp, head : head + 1, place] = highest * SCALE2 + jnp.log2(sums)
            results[head] = summed[:HEAD_DIM] / sums
            if head == 1:
                both = jnp.concatenate([results[0], results[1]], 0).astype(BF)
                out_t[pl.ds(pl.multiple_of(i * HEADS * HEAD_DIM + hp * PAIR, PAIR), PAIR)] = both
                out[place, span(hp, PAIR)] = both.T

        before = None
        for i in range(count):
            for head in range(2):
                scores = first(i, head)
                if before is not None:
                    second(*before)
                before = (i, head, scores)
        second(*before)
        return 0

    lax.fori_loop(0, PAIRS, pair, 0)


def attend_back(
    query, keys, values, grad_out, out, total, grad_query, grad_keys, grad_values, sums, causal, block, hook=None
):
    rows = grad_out.shape[0]
    count = rows // block

    def pair(hp, _):
        def columns(column):
            return pl.ds(pl.multiple_of(column + hp * PAIR, PAIR), PAIR)

        two_keys = keys[0][:, columns(keys[1])]
        two_values = values[0][:, columns(values[1])]
        keys_t = two_keys.T
        here = span(hp, PAIR)
        product = grad_out[:, here].astype(F32) * out[:, here].astype(F32)
        high = product.astype(BF)
        low = (product - high.astype(F32)).astype(BF)
        pick = (
            lax.broadcasted_iota(jnp.int32, (8, PAIR), 1) // HEAD_DIM
            == lax.broadcasted_iota(jnp.int32, (8, PAIR), 0)
        ).astype(F32).astype(BF)
        dots = nt(pick, high) + nt(pick, low)
        kept = {}

        def first(i, head):
            length = (i + 1) * block if causal else two_keys.shape[0]
            place = pl.ds(i * block, block)
            own_query = own_head(query[0][place, columns(query[1])], head)
            own_grad = own_head(grad_out[place, here], head)
            return (
                nt(two_keys[:length], own_query),
                nt(two_values[:length], own_grad),
                own_query,
                own_grad,
            )

        def second(i, head, state):
            scores, grad_probs, own_query, own_grad = state
            length = scores.shape[0]
            place = pl.ds(i * block, block)
            shifted = scores * SCALE2 - total[hp, head : head + 1, place]
            probs = jnp.exp2(causal_mask(shifted, block, causal))
            dot = dots[head : head + 1, i * block : (i + 1) * block]
            grad_scores = (probs * (grad_probs - dot)).astype(BF)
            back = nn(keys_t[head * HEAD_DIM : (head + 1) * HEAD_DIM, :length], grad_scores)
            kept[head] = (probs.astype(BF), grad_scores, own_query, own_grad, back)
            if head == 1:
                probs2, scores2 = [
                    jnp.concatenate([kept[0][n], kept[1][n]], 1) for n in range(2)
                ]
                query2, grad2 = [
                    jnp.concatenate([kept[0][n], kept[1][n]], 0) for n in range(2, 4)
                ]
                new_values = nn(probs2, grad2)
                new_keys = nn(scores2, query2)
                if i == count - 1:
                    sums[0][...] = new_keys
                    sums[1][...] = new_values
                else:
                    sums[0][:length] += new_keys
                    sums[1][:length] += new_values
                grad_query[0][place, columns(grad_query[1])] = (
                    jnp.concatenate([kept[0][4], kept[1][4]], 0).T * SCALE
                ).astype(BF)

        before = None
        for i in reversed(range(count)):
            for head in range(2):
                state = first(i, head)
                if before is not None:
                    second(*before)
                before = (i, head, state)
        second(*before)
        grad_keys[0][:, columns(grad_keys[1])] = (sums[0][...] * SCALE).astype(BF)
        grad_values[0][:, columns(grad_values[1])] = sums[1][...].astype(BF)
        if hook is not None:
            hook(hp)
        return 0

    lax.fori_loop(0, PAIRS, pair, 0)


def slot_of(routes, group, device, size):
    own = routes[group]
    rank = lax.fori_loop(
        0, group, lambda j, c: c + jnp.where(routes[j] == own, 1, 0).astype(jnp.int32), jnp.int32(0)
    )
    return partner_of(device, own, size) * CAPACITY + rank


def weigh(values, weight):
    return values * jnp.full(values.shape, weight.astype(F32), F32).astype(BF)


def pick_group(routes, source, group_rows, expert, rank):
    count = jnp.int32(0)
    total = None
    for group in range(source.shape[0] // group_rows):
        same = jnp.where(routes[group] == expert, 1, 0).astype(jnp.int32)
        hit = same * jnp.where(count == rank, 1, 0).astype(jnp.int32)
        count = count + same
        term = weigh(source[group * group_rows : (group + 1) * group_rows], hit)
        total = term if total is None else total + term
    return total


def partner_of(own, offset, size):
    result, bit = 0, 1
    while bit < size:
        result = result + lax.rem(own // bit + offset // bit, 2) * bit
        bit *= 2
    return result


ROWS = 256
MESH = pl.DeviceIdType.MESH
Q, K, V, ATTN, CQ, MK, MV, CROSS, ATTN_T, CROSS_T = range(10)
SAVED = 10


def forward_kernel(
    size,
    group_rows,
    routes,
    self_gain,
    self_shift,
    cross_gain,
    cross_shift,
    moe_gain,
    moe_shift,
    up_bias,
    down_bias,
    *refs,
):
    (
        x_h, memory_h, grad_h, project_h, output_h, query_h, memory_w_h, cross_w_h, up_h, down_h,
        saved_o, hidden1_o, hidden2_o, rows_out_o, returned_o, half_own_o, half_other_o,
        total1, total2, biases,
        x, memory, grad, self_project, self_output, cross_query, cross_memory, cross_output, up, down,
        arena, hidden1, hidden2, normed3, outbound, received, received_grad, flat_t, grad_t, halves,
        in_sems, out_sems, core_sems, grad_send, grad_recv, row_send, row_recv, back_send, back_recv,
    ) = refs
    rows, width = x.shape
    wide = up.shape[1]
    blocks = rows // ROWS
    part_rows = CAPACITY * group_rows
    slot_rows = size * part_rows
    batch, own = lax.axis_index("batch"), lax.axis_index("exp")

    layers = lax.axis_size("batch") // 2
    half = halves.shape[0] // 2
    piece = half // layers
    core, other = lax.rem(batch, 2), 1 - lax.rem(batch, 2)
    twin = (batch + other - core, own)

    def partner(offset):
        return (batch, partner_of(own, offset, size))

    loads = [
        pltpu.make_async_copy(source, target, in_sems.at[n])
        for n, (source, target) in enumerate(
            [
                (grad_h, grad), (x_h, x), (project_h, self_project), (memory_h, memory),
                (memory_w_h, cross_memory), (output_h, self_output), (query_h, cross_query),
                (cross_w_h, cross_output), (up_h, up), (down_h, down),
            ]
        )
    ]
    for load in loads:
        load.start()
    barrier = pltpu.get_barrier_semaphore()
    for offset in range(1, size):
        pl.semaphore_signal(barrier, inc=1, device_id=partner(offset), device_id_type=MESH)
    pl.semaphore_signal(barrier, inc=1, device_id=twin, device_id_type=MESH)
    pl.semaphore_wait(barrier, size)

    def part(ref, offset):
        return ref.at[pl.ds(pl.multiple_of(offset * part_rows, part_rows), part_rows)]

    def send(source, target, offset, send_sems, recv_sems):
        return pltpu.make_async_remote_copy(
            src_ref=part(source, offset),
            dst_ref=part(target, offset),
            send_sem=send_sems.at[offset],
            recv_sem=recv_sems.at[offset],
            device_id=partner(offset),
            device_id_type=MESH,
        )

    def dispatch(source, target, offset):
        expert = partner_of(own, offset, size)

        def one(rank, _):
            values = pick_group(routes, source, group_rows, expert, rank)
            target[pl.ds(pl.multiple_of(offset * part_rows + rank * group_rows, group_rows), group_rows)] = values
            return 0

        lax.fori_loop(0, CAPACITY, one, 0)

    def to_all(source, target, send_sems, recv_sems):
        dispatch(source, target, 0)

        def one(offset, _):
            dispatch(source, outbound, offset)
            send(outbound, target, offset, send_sems, recv_sems).start()
            return 0

        lax.fori_loop(1, size, one, 0)

    loads[0].wait()
    to_all(grad, received_grad, grad_send, grad_recv)
    for load in loads[1:5]:
        load.wait()

    def place(which):
        return arena.at[pl.ds(which * rows, rows)]

    q, k, v, attn, cq, mk, mv, cross, attn_t, cross_t = [place(n) for n in range(SAVED)]

    def block1(i, _):
        here = span(i, ROWS)
        hat, _s = normalize(x[here].astype(F32))
        normed = (hat * self_gain[...] + self_shift[...]).astype(BF)
        for n, target in enumerate((q, k, v)):
            target[here] = nn(normed, self_project[:, n * width : (n + 1) * width]).astype(BF)
        for n, target in enumerate((mk, mv)):
            target[here] = nn(memory[here], cross_memory[:, n * width : (n + 1) * width]).astype(BF)
        return 0

    lax.fori_loop(0, blocks, block1, 0)
    attend((q, 0), (k, 0), (v, 0), attn, attn_t, total1, True)
    for load in loads[5:]:
        load.wait()

    def block2(i, _):
        here = span(i, ROWS)
        hidden = x[here].astype(F32) + nn(attn[here], self_output[...])
        hidden1[here] = hidden
        hat, _s = normalize(hidden)
        normed = (hat * cross_gain[...] + cross_shift[...]).astype(BF)
        cq[here] = nn(normed, cross_query[...]).astype(BF)
        return 0

    lax.fori_loop(0, blocks, block2, 0)
    attend((cq, 0), (mk, 0), (mv, 0), cross, cross_t, total2, False)
    stores = [
        pltpu.make_async_copy(arena.at[pl.ds(0, SAVED * rows)], saved_o, out_sems.at[0]),
        pltpu.make_async_copy(hidden1, hidden1_o, out_sems.at[1]),
        pltpu.make_async_copy(hidden2, hidden2_o, out_sems.at[2]),
    ]
    stores[0].start()
    stores[1].start()

    def block3(i, _):
        here = span(i, ROWS)
        hidden = hidden1[here] + nn(cross[here], cross_output[...])
        hidden2[here] = hidden
        hat, _s = normalize(hidden)
        normed3[here] = (hat * moe_gain[...] + moe_shift[...]).astype(BF)
        return 0

    lax.fori_loop(0, blocks, block3, 0)
    stores[2].start()

    def sent(source, target, send_sems, recv_sems):
        def one(offset, _):
            send(source, target, offset, send_sems, recv_sems).wait_send()
            return 0

        lax.fori_loop(1, size, one, 0)

    sent(outbound, received_grad, grad_send, grad_recv)
    to_all(normed3, received, row_send, row_recv)
    stores[0].wait()

    block_rows = max(512, part_rows)
    per = block_rows // part_rows
    chunk = 512
    first, third = math.sqrt(2.0 / math.pi), math.sqrt(2.0 / math.pi) * 0.044715
    flat_t[width:] = jnp.ones((flat_t.shape[0] - width, slot_rows), BF)

    def hidden_at(c, start, length):
        return arena.at[pl.ds(pl.multiple_of(c * slot_rows + start, block_rows), length)]

    def pre_at(c, start, length):
        return arena.at[
            pl.ds(pl.multiple_of((wide // chunk + c) * slot_rows + start, block_rows), length)
        ]

    def block(i, bias):
        for n in range(per):
            offset = i * per + n

            @pl.when(offset > 0)
            def _():
                send(outbound, received_grad, offset, grad_send, grad_recv).wait_recv()
                send(outbound, received, offset, row_send, row_recv).wait_recv()

        here = span(i, block_rows)
        flat = received[here]
        grads = received_grad[here]
        flat_t[:width, here] = flat.T
        grad_t[:, here] = grads.T
        out = jnp.zeros((block_rows, width), F32)
        back = jnp.zeros((block_rows, width), F32)
        for c in range(wide // chunk):
            cols = pl.ds(c * chunk, chunk)
            pre = nn(flat, up[:, cols]) + up_bias[:, cols]
            square = pre * pre
            half = 0.5 + 0.5 * jnp.tanh(pre * (first + third * square))
            value = pre * half
            low = value.astype(BF)
            slope = half + value * (1.0 - half) * (2.0 * first + (6.0 * third) * square)
            gpre = (nt(grads, down[cols]) * slope).astype(BF)
            hidden_at(c, i * block_rows, block_rows)[...] = low
            pre_at(c, i * block_rows, block_rows)[...] = gpre
            out += nn(low, down[cols])
            back += nt(gpre, up[:, cols])
        received[here] = (out + down_bias[...]).astype(BF)
        received_grad[here] = back.astype(BF)
        for n in range(per):
            offset = i * per + n

            @pl.when(offset > 0)
            def _():
                send(received_grad, returned_o, offset, back_send, back_recv).start()

        return bias + jnp.sum(grads.astype(F32), 0, keepdims=True)

    bias = lax.fori_loop(0, slot_rows // block_rows, block, jnp.zeros((1, width), F32))
    stores.append(
        pltpu.make_async_copy(part(received_grad, 0), part(returned_o, 0), out_sems.at[3])
    )
    stores.append(pltpu.make_async_copy(received, rows_out_o, out_sems.at[4]))
    stores[3].start()
    stores[4].start()
    up_rows, down_rows = width // (2 * layers), wide // (2 * layers)
    biases[...] = jnp.zeros_like(biases)
    per_chunk = chunk // down_rows

    def piece_at(number, start, length):
        row = lax.rem(number, 2) * half + number // 2 * piece + start
        return halves.at[pl.ds(pl.multiple_of(row, length), length)]

    def weights(c, _):
        cols = span(c, chunk)
        both = nn(flat_t[...], pre_at(c, 0, slot_rows)[...])
        for n in range(2 * layers):
            piece_at(jnp.int32(n), c * up_rows, up_rows)[...] = both[
                n * up_rows : (n + 1) * up_rows
            ].astype(BF)
        biases[pl.ds(c, 1)] = both[width : width + 1]
        down_t = nn(grad_t[...], hidden_at(c, 0, slot_rows)[...])
        for n in range(per_chunk):
            piece_at(c * per_chunk + n, wide // chunk * up_rows, down_rows)[...] = down_t[
                :, n * down_rows : (n + 1) * down_rows
            ].T.astype(BF)
        return 0

    lax.fori_loop(0, wide // chunk, weights, 0)
    biases[wide // chunk : wide // chunk + 1] = bias

    def half_at(which):
        return halves.at[pl.ds(pl.multiple_of(which * half, half), half)]

    to_twin = pltpu.make_async_remote_copy(
        src_ref=half_at(other),
        dst_ref=half_other_o,
        send_sem=core_sems.at[0],
        recv_sem=core_sems.at[1],
        device_id=twin,
        device_id_type=MESH,
    )
    to_twin.start()
    stores.append(pltpu.make_async_copy(half_at(core), half_own_o, out_sems.at[5]))
    stores[5].start()
    sent(outbound, received, row_send, row_recv)
    sent(received_grad, returned_o, back_send, back_recv)

    def arrived(offset, _):
        send(received_grad, returned_o, offset, back_send, back_recv).wait_recv()
        return 0

    lax.fori_loop(1, size, arrived, 0)
    to_twin.wait()
    for store in stores[1:]:
        store.wait()


MATS = 8


def back_kernel(
    size,
    layers,
    group_rows,
    routes,
    self_gain,
    self_shift,
    cross_gain,
    cross_shift,
    moe_gain,
    moe_shift,
    total1,
    total2,
    biases,
    *refs,
):
    (
        x_h, memory_h, grad_h, project_h, output_h, query_h, memory_w_h, cross_w_h,
        saved_h, hidden1_h, hidden2_h, returned_grad_h, rows_out_h, half_own_h, half_other_h,
        layer_o, grad_input_o, grad_memory_o, reduced_o, returned_o,
        small, up_o, down_o, bias_o,
        x, memory, grad, self_project, self_output, cross_query, cross_memory, cross_output,
        saved, hidden1, hidden2, returned,
        carried, carried_low, back_low, grad_q, grad_kv, grad_project, normed, sum_a, sum_b,
        grads, from_twin, from_exp, part, from_layer, from_layer_whole, shard,
        half, from_half, from_small, from_bias,
        in_sems, out_sems, ret_send, ret_recv, half_send, half_recv, bias_send, bias_recv,
        small_send, small_recv, sends, recvs,
    ) = refs
    rows, width = x.shape
    wide = up_o.shape[1]
    blocks = rows // ROWS
    per = ROWS // group_rows
    part_rows = CAPACITY * group_rows
    zero = jnp.zeros((1, width), F32)
    batch, own = lax.axis_index("batch"), lax.axis_index("exp")
    core, layer = lax.rem(batch, 2), batch // 2
    twin = (batch + 1 - 2 * core, own)

    def partner(offset):
        return (batch, partner_of(own, offset, size))

    def above(offset):
        return lax.rem(layer + offset, layers)

    def column(offset):
        return (above(offset) * 2 + core, own)

    pairs = [
        (hidden2_h, hidden2), (returned_grad_h, returned), (grad_h, grad), (cross_w_h, cross_output),
        (half_own_h, half), (half_other_h, grad_kv), (saved_h, saved), (hidden1_h, hidden1),
        (query_h, cross_query), (memory_w_h, cross_memory), (output_h, self_output), (memory_h, memory),
        (x_h, x), (project_h, self_project),
    ]
    loads = [pltpu.make_async_copy(*pair, in_sems.at[n]) for n, pair in enumerate(pairs)]
    for load in loads:
        load.start()
    barrier = pltpu.get_barrier_semaphore()
    greeted = (
        [twin] + [partner(n) for n in range(1, size)] + [column(n) for n in range(1, layers)]
    )
    for device in greeted:
        pl.semaphore_signal(barrier, inc=1, device_id=device, device_id_type=MESH)
    pl.semaphore_wait(barrier, len(greeted))

    def remote(source, target, device, send_sem, recv_sem):
        return pltpu.make_async_remote_copy(
            src_ref=source,
            dst_ref=target,
            send_sem=send_sem,
            recv_sem=recv_sem,
            device_id=device,
            device_id_type=MESH,
        )

    def start_all(copies):
        for copy in copies:
            copy.start()

    def wait_all(copies):
        for copy in copies:
            copy.wait()

    def slots(ref, offset):
        return ref.at[pl.ds(offset * part_rows, part_rows)]

    back_rows = [
        remote(slots(rows_out_h, n), slots(returned_o, n), partner(n), ret_send.at[n], ret_recv.at[n])
        for n in range(1, size)
    ]
    start_all(back_rows)
    own_rows = pltpu.make_async_copy(slots(rows_out_h, 0), slots(returned_o, 0), out_sems.at[0])
    own_rows.start()

    q, k, v, attn, cross_q, mk, mv, cross, attn_t, cross_t = [
        saved.at[pl.ds(n * rows, rows)] for n in range(SAVED)
    ]
    gq, gk, gv = [grad_project.at[pl.ds(n * rows, rows)] for n in range(3)]
    gmk, gmv = [grad_kv.at[pl.ds(n * rows, rows)] for n in range(2)]

    def mat(number):
        return slice(number * width, (number + 1) * width)

    def times(turned, right):
        count = 512
        return sum(
            nn(turned[n * width : (n + 1) * width], right[n * count : (n + 1) * count])
            for n in range(rows // count)
        )

    def gather(source, group, place):
        expert = partner_of(own, routes[group], size)
        rank = lax.fori_loop(
            0,
            group,
            lambda j, c: c + jnp.where(routes[j] == routes[group], 1, 0).astype(jnp.int32),
            jnp.int32(0),
        )
        slot = expert * CAPACITY + rank
        total = None
        for n in range(size * CAPACITY):
            hit = jnp.where(slot == n, 1, 0).astype(jnp.int32)
            term = weigh(source[n * group_rows : (n + 1) * group_rows], hit)
            total = term if total is None else total + term
        place[span(group, group_rows)] = total

    def gather_all(source, place):
        def one(group, _):
            gather(source, group, place)
            return 0

        lax.fori_loop(0, rows // group_rows, one, 0)

    tall = grads.shape[0]
    by_core = tall // 2
    by_exp = by_core // size
    counter = [0]

    def pair_of_sems():
        counter[0] += 1
        return sends.at[counter[0] - 1], recvs.at[counter[0] - 1]

    def reduction(first, last, whole=False):
        split = layers if (by_exp // layers) % 16 == 0 and not whole else 1
        by_layer = by_exp // split
        landing = from_layer_whole if whole else from_layer
        shift = first if whole else 0
        cols = pl.ds(first, last - first)

        def lane(ref, start, length):
            return ref.at[pl.ds(pl.multiple_of(start, length), length), cols]

        mine = core * by_core
        core_copies = [
            remote(lane(grads, (1 - core) * by_core, by_core), from_twin.at[:, cols], twin, *pair_of_sems())
        ]
        exp_copies = [
            remote(
                lane(grads, mine + partner_of(own, n, size) * by_exp, by_exp),
                from_exp.at[n - 1, :, cols],
                partner(n),
                *pair_of_sems(),
            )
            for n in range(1, size)
        ]
        at_layer = layer * by_layer if split > 1 else 0
        layer_copies = [
            remote(
                lane(part, above(n) * by_layer if split > 1 else 0, by_layer),
                landing.at[n - 1, :, pl.ds(first - shift, last - first)],
                column(n),
                *pair_of_sems(),
            )
            for n in range(1, layers)
        ]
        share_copies = [
            remote(
                lane(shard, at_layer, by_layer),
                lane(shard, at_layer, by_layer),
                column(n),
                *pair_of_sems(),
            )
            for n in range(1, layers)
        ] if split > 1 else []
        spot = mine + own * by_exp
        out_copies = [
            remote(shard.at[:, cols], lane(reduced_o, spot, by_exp), partner(n), *pair_of_sems())
            for n in range(1, size)
        ]
        local = pltpu.make_async_copy(shard.at[:, cols], lane(reduced_o, spot, by_exp), pair_of_sems()[0])
        half_copies = [
            remote(lane(reduced_o, mine, by_core), lane(reduced_o, mine, by_core), twin, *pair_of_sems())
        ]

        def stage(number):
            if number == 0:
                start_all(core_copies)
            if number == 1:
                wait_all(core_copies)

                def add(i, _):
                    here = pl.ds(pl.multiple_of(mine + i * 64, 64), 64)
                    grads[here, cols] = (
                        grads[here, cols].astype(F32) + from_twin[span(i, 64), cols].astype(F32)
                    ).astype(BF)
                    return 0

                lax.fori_loop(0, by_core // 64, add, 0)
                start_all(exp_copies)
            if number == 2:
                wait_all(exp_copies)
                here = pl.ds(pl.multiple_of(spot, by_exp), by_exp)
                total = grads[here, cols].astype(F32)
                for n in range(size - 1):
                    total = total + from_exp[n, :, cols].astype(F32)
                part[:, cols] = total.astype(BF)
            if number == 3:
                start_all(layer_copies)
            if number == 4:
                wait_all(layer_copies)
                here = pl.ds(pl.multiple_of(at_layer, by_layer), by_layer)
                total = part[here, cols].astype(F32)
                for n in range(layers - 1):
                    total = total + landing[n, :, first - shift : last - shift].astype(F32)
                shard[here, cols] = total.astype(BF)
                start_all(share_copies)
            if number == 5:
                wait_all(share_copies)
                start_all(out_copies)
                local.start()
            if number == 6:
                wait_all(out_copies)
                local.wait()
                start_all(half_copies)
            if number == 7:
                wait_all(half_copies)

        return stage

    per_pair = 3 * PAIR
    part_a = reduction(7 * width, 8 * width)
    part_b = reduction(5 * width, 7 * width)
    first_sum = reduction(5 * width, 8 * width)
    second_sum = reduction(3 * width, 5 * width)
    third_sum = reduction(0, 3 * per_pair)
    last_sum = reduction(3 * per_pair, 4 * per_pair, True)

    for load in loads[:4]:
        load.wait()
    gather_all(returned, carried_low)

    def block3(i, carry):
        here = span(i, ROWS)
        hat, scale = normalize(hidden2[here])
        gy = carried_low[here].astype(F32)
        total = grad[here].astype(F32) + normalize_back(hat, scale, gy, moe_gain[...])
        carried[here] = total
        low = total.astype(BF)
        carried_low[here] = low
        back_low[here] = nt(low, cross_output[...]).astype(BF)
        return (
            carry[0] + jnp.sum(gy * hat, 0, keepdims=True),
            carry[1] + jnp.sum(gy, 0, keepdims=True),
        )

    gains3 = lax.fori_loop(0, blocks, block3, (zero, zero))

    for load in loads[4:6]:
        load.wait()

    def add_half(i, _):
        here = span(i, ROWS)
        half[here] = (half[here].astype(F32) + grad_kv[here].astype(F32)).astype(BF)
        return 0

    lax.fori_loop(0, half.shape[0] // ROWS, add_half, 0)
    piece = half.shape[0] // layers
    turns = 8
    turn_rows = piece // turns
    pieces = [
        [
            remote(
                half.at[pl.ds(pl.multiple_of(above(n) * piece + turn * turn_rows, turn_rows), turn_rows)],
                from_half.at[n - 1, pl.ds(turn * turn_rows, turn_rows)],
                column(n),
                half_send.at[(n - 1) * turns + turn],
                half_recv.at[(n - 1) * turns + turn],
            )
            for n in range(1, layers)
        ]
        for turn in range(turns)
    ]
    start_all(pieces[0])
    bias_twin = [remote(biases, from_bias.at[0], twin, bias_send.at[0], bias_recv.at[0])]
    start_all(bias_twin)
    for load in loads[6:]:
        load.wait()
    grads[:, mat(7)] = times(cross_t, carried_low).astype(BF)
    part_a(0)

    def cross_hook(hp):
        @pl.when(hp == 0)
        def _():
            part_a(1)
            start_all(pieces[1])

        @pl.when(hp == 1)
        def _():
            start_all(pieces[2])

        @pl.when(hp == 2)
        def _():
            start_all(pieces[3])

        @pl.when(hp == 3)
        def _():
            start_all(pieces[4])
            part_a(2)

    attend_back(
        (cross_q, 0), (mk, 0), (mv, 0), back_low, cross, total2,
        (grad_q, 0), (gmk, 0), (gmv, 0), (sum_a, sum_b), False, 256, cross_hook,
    )
    grads[:, mat(5)] = tn(memory[...], gmk[...]).astype(BF)
    grads[:, mat(6)] = tn(memory[...], gmv[...]).astype(BF)
    part_b(0)

    def block2(i, carry):
        here = span(i, ROWS)
        hat, scale = normalize(hidden1[here])
        normed[here] = (hat * cross_gain[...] + cross_shift[...]).astype(BF)
        gy = nt(grad_q[here], cross_query[...])
        total = carried[here] + normalize_back(hat, scale, gy, cross_gain[...])
        carried[here] = total
        low = total.astype(BF)
        carried_low[here] = low
        back_low[here] = nt(low, self_output[...]).astype(BF)
        return (
            carry[0] + jnp.sum(gy * hat, 0, keepdims=True),
            carry[1] + jnp.sum(gy, 0, keepdims=True),
        )

    gains2 = lax.fori_loop(0, blocks, block2, (zero, zero))
    part_b(1)
    start_all(pieces[5])
    grads[:, mat(4)] = tn(normed[...], grad_q[...]).astype(BF)
    grads[:, mat(3)] = times(attn_t, carried_low).astype(BF)
    second_sum(0)
    wait_all(bias_twin)
    biases[...] += from_bias[0]
    bias_layers = [
        remote(biases, from_bias.at[n], column(n), bias_send.at[n], bias_recv.at[n])
        for n in range(1, layers)
    ]
    start_all(bias_layers)
    for n in range(rows // 512):
        hat, _s = normalize(x[n * 512 : (n + 1) * 512].astype(F32))
        normed[n * width : (n + 1) * width] = (
            (hat * self_gain[...] + self_shift[...]).astype(BF).T
        )

    def self_hook(hp):
        cols = span(hp, PAIR)
        three = jnp.concatenate([gq[:, cols], gk[:, cols], gv[:, cols]], 1)
        grads[:, pl.ds(pl.multiple_of(hp * per_pair, PAIR), per_pair)] = times(normed, three).astype(BF)

        @pl.when(hp == 0)
        def _():
            second_sum(1)
            part_b(2)
            first_sum(3)

        @pl.when(hp == 1)
        def _():
            first_sum(4)
            start_all(pieces[6])

        @pl.when(hp == 2)
        def _():
            third_sum(0)
            second_sum(2)
            second_sum(3)
            first_sum(5)

        @pl.when(hp == 3)
        def _():
            third_sum(1)
            last_sum(0)
            second_sum(4)
            start_all(pieces[7])

    attend_back(
        (q, 0), (k, 0), (v, 0), back_low, attn, total1,
        (gq, 0), (gk, 0), (gv, 0), (sum_a, sum_b), True, 256, self_hook,
    )
    last_sum(1)

    def block1(i, carry):
        here = span(i, ROWS)
        hat, scale = normalize(x[here].astype(F32))
        gy = sum(
            nt(ref[here], self_project[:, mat(n)]) for n, ref in enumerate((gq, gk, gv))
        )
        carried[here] += normalize_back(hat, scale, gy, self_gain[...])
        return (
            carry[0] + jnp.sum(gy * hat, 0, keepdims=True),
            carry[1] + jnp.sum(gy, 0, keepdims=True),
        )

    gains1 = lax.fori_loop(0, blocks, block1, (zero, zero))
    stores = [pltpu.make_async_copy(carried, grad_input_o, out_sems.at[1])]
    stores[0].start()
    small[...] = jnp.concatenate([*gains1, *gains2, *gains3, zero, zero], 0)

    def share_small(number, devices):
        copies = [
            remote(small, from_small.at[number + n], device, small_send.at[number + n], small_recv.at[number + n])
            for n, device in enumerate(devices)
        ]
        start_all(copies)

        def finish():
            wait_all(copies)
            total = small[...]
            for n in range(len(devices)):
                total = total + from_small[number + n]
            small[...] = total

        return finish

    finish = share_small(0, [twin])
    second_sum(5)
    third_sum(2)
    third_sum(3)

    wait_all(back_rows)
    own_rows.wait()
    fetch = pltpu.make_async_copy(returned_o, returned, out_sems.at[2])
    fetch.start()
    finish()
    finish = share_small(1, [partner(n) for n in range(1, size)])

    def memory_block(i, _):
        here = span(i, ROWS)
        hidden1[here] = nt(gmk[here], cross_memory[:, :width]) + nt(gmv[here], cross_memory[:, width:])
        return 0

    lax.fori_loop(0, rows // ROWS, memory_block, 0)
    stores.append(pltpu.make_async_copy(hidden1, grad_memory_o, out_sems.at[3]))
    stores[1].start()
    last_sum(2)
    last_sum(3)
    first_sum(6)
    third_sum(4)
    fetch.wait()
    gather_all(returned, normed)

    def output_block(i, _):
        here = span(i, ROWS)
        grad[here] = (hidden2[here] + normed[here].astype(F32)).astype(BF)
        return 0

    lax.fori_loop(0, blocks, output_block, 0)
    stores.append(pltpu.make_async_copy(grad, layer_o, out_sems.at[4]))
    stores[2].start()
    last_sum(4)
    last_sum(5)
    finish()
    finish = share_small(size, [column(n) for n in range(1, layers)])
    third_sum(5)
    second_sum(6)
    for turn in range(turns):
        wait_all(pieces[turn])
    up_rows = up_o.shape[0]
    base = layer * piece
    for c in range(wide // width):
        total = half[pl.ds(pl.multiple_of(base + c * up_rows, up_rows), up_rows)].astype(F32)
        for n in range(layers - 1):
            total = total + from_half[n, c * up_rows : (c + 1) * up_rows].astype(F32)
        up_o[:, c * width : (c + 1) * width] = total
    down_rows = down_o.shape[0]
    start = wide // width * up_rows
    total = half[pl.ds(pl.multiple_of(base + start, down_rows), down_rows)].astype(F32)
    for n in range(layers - 1):
        total = total + from_half[n, start : start + down_rows].astype(F32)
    down_o[...] = total
    wait_all(bias_layers)
    total = biases[...]
    for n in range(1, layers):
        total = total + from_bias[n]
    bias_o[...] = total
    finish()
    last_sum(6)
    third_sum(6)
    first_sum(7)
    second_sum(7)
    last_sum(7)
    third_sum(7)
    for store in stores:
        store.wait()


def finish_kernel(reduced, *refs):
    plain, (project, output, query, memory, cross), moved = refs[:5], refs[5:10], refs[10:]
    width = output.shape[1]
    for pair in range(PAIRS):
        for n in range(3):
            column = (pair * 3 + n) * PAIR
            project[:, n * width + pair * PAIR : n * width + (pair + 1) * PAIR] = reduced[
                :, column : column + PAIR
            ].astype(F32)
    column = 3 * width
    for target in (output, query, memory, cross):
        size = target.shape[1]
        target[...] = reduced[:, column : column + size].astype(F32)
        column += size
    for source, target in zip(plain, moved):
        target[...] = source[...]


def body(
    layer_input,
    memory,
    routes,
    out_grad,
    self_gain,
    self_shift,
    self_project,
    self_output,
    cross_gain,
    cross_shift,
    cross_query,
    cross_memory,
    cross_output,
    moe_gain,
    moe_shift,
    expert_up,
    up_bias,
    expert_down,
    down_bias,
):
    x = layer_input[0]
    memory = memory[0]
    grad = out_grad[0]
    rows, width = x.shape
    wide = expert_up.shape[2]
    size = lax.axis_size("exp")
    groups = routes.shape[1]
    group_rows = rows // groups
    slot_rows = size * CAPACITY * group_rows
    route = routes.reshape(groups)
    gains = [v.reshape(1, width) for v in (self_gain, self_shift, cross_gain, cross_shift, moe_gain, moe_shift)]
    def array(shape, dtype):
        return jax.ShapeDtypeStruct(shape, dtype)

    vmem, smem, any_ = [pl.BlockSpec(memory_space=m) for m in (pltpu.VMEM, pltpu.SMEM, pl.ANY)]
    big = [
        x, memory, grad, self_project, self_output, cross_query, cross_memory, cross_output,
        expert_up[0], expert_down[0],
    ]
    sems = pltpu.SemaphoreType.DMA((size,))
    saved, hidden1, hidden2, rows_out, returned_grad, half_own, half_other, total1, total2, biases = pl.pallas_call(
        functools.partial(forward_kernel, size, group_rows),
        out_shape=(
            array((SAVED * rows, width), BF),
            array((rows, width), F32),
            array((rows, width), F32),
            array((slot_rows, width), BF),
            array((slot_rows, width), BF),
            array((wide, width), BF),
            array((wide, width), BF),
            array((PAIRS, 8, rows), F32),
            array((PAIRS, 8, rows), F32),
            array((8, width), F32),
        ),
        in_specs=[smem] + [vmem] * 8 + [any_] * 10,
        out_specs=(any_,) * 7 + (vmem,) * 3,
        scratch_shapes=[pltpu.VMEM(v.shape, v.dtype) for v in big]
        + [
            pltpu.VMEM(shape, dtype)
            for shape, dtype in [
                ((2 * slot_rows * (wide // 512), 512), BF),
                ((rows, width), F32),
                ((rows, width), F32),
                ((rows, width), BF),
                ((slot_rows, width), BF),
                ((slot_rows, width), BF),
                ((slot_rows, width), BF),
                ((width + 16, slot_rows), BF),
                ((width, slot_rows), BF),
                ((2 * wide, width), BF),
            ]
        ]
        + [pltpu.SemaphoreType.DMA((10,)), pltpu.SemaphoreType.DMA((6,)), pltpu.SemaphoreType.DMA((2,))]
        + [sems] * 6,
        compiler_params=pltpu.CompilerParams(
            collective_id=0, has_side_effects=True, vmem_limit_bytes=62 << 20
        ),
        cost_estimate=pl.CostEstimate(flops=60 * 10**9, bytes_accessed=40 << 20, transcendentals=0),
    )(route, *gains, up_bias, down_bias, *big)
    layers = lax.axis_size("batch") // 2
    by_exp = width // 2 // size
    by_layer = by_exp // layers if (by_exp // layers) % 16 == 0 else by_exp
    piece = wide // layers
    back_in = [
        *big[:8], saved, hidden1, hidden2, returned_grad, rows_out, half_own, half_other,
    ]
    count = 6 * (4 + 2 * (size - 1) + 2 * (layers - 1))
    dma = pltpu.SemaphoreType.DMA
    (
        layer_output, grad_input, grad_memory, reduced, _returned, small, grad_up, grad_down, biases,
    ) = pl.pallas_call(
        functools.partial(back_kernel, size, layers, group_rows),
        out_shape=(
            array((rows, width), BF),
            array((rows, width), F32),
            array((rows, width), F32),
            array((width, MATS * width), BF),
            array((slot_rows, width), BF),
            array((8, width), F32),
            array((width // (2 * layers), wide), F32),
            array((wide // (2 * layers), width), F32),
            array((8, width), F32),
        ),
        in_specs=[smem] + [vmem] * 9 + [any_] * len(back_in),
        out_specs=(any_,) * 5 + (vmem,) * 4,
        scratch_shapes=[pltpu.VMEM(v.shape, v.dtype) for v in big[:8]]
        + [
            pltpu.VMEM(shape, dtype)
            for shape, dtype in [
                (saved.shape, BF),
                ((rows, width), F32),
                ((rows, width), F32),
                ((slot_rows, width), BF),
                ((rows, width), F32),
                ((rows, width), BF),
                ((rows, width), BF),
                ((rows, width), BF),
                ((2 * rows, width), BF),
                ((3 * rows, width), BF),
                ((rows, width), BF),
                ((rows, PAIR), F32),
                ((rows, PAIR), F32),
                ((width, MATS * width), BF),
                ((width // 2, MATS * width), BF),
                ((size - 1, by_exp, MATS * width), BF),
                ((by_exp, MATS * width), BF),
                ((layers - 1, by_layer, MATS * width), BF),
                ((layers - 1, by_exp, 3 * PAIR), BF),
                ((by_exp, MATS * width), BF),
                ((wide, width), BF),
                ((layers - 1, piece, width), BF),
                ((size + layers - 1, 8, width), F32),
                ((layers, 8, width), F32),
            ]
        ]
        + [dma((14,)), dma((5,)), sems, sems]
        + [dma((8 * layers,))] * 2
        + [dma((layers,))] * 2
        + [dma((size + layers - 1,))] * 2
        + [dma((count,))] * 2,
        compiler_params=pltpu.CompilerParams(
            collective_id=1, has_side_effects=True, vmem_limit_bytes=63 << 20
        ),
        cost_estimate=pl.CostEstimate(flops=60 * 10**9, bytes_accessed=40 << 20, transcendentals=0),
    )(route, *gains, total1, total2, biases, *back_in)
    shapes = [(width, 3 * width), (width, width), (width, width), (width, 2 * width), (width, width)]
    steps = 4
    plain = [grad_input, grad_memory, layer_output, grad_up, grad_down]
    wanted = [array(shape, F32) for shape in shapes] + [array(v.shape, v.dtype) for v in plain]

    def in_steps(value):
        return pl.BlockSpec((value.shape[0] // steps, value.shape[1]), lambda i: (i, 0))

    (
        grad_self_project, grad_self_output, grad_cross_query, grad_cross_memory, grad_cross_output,
        grad_input, grad_memory, layer_output, grad_up, grad_down,
    ) = pl.pallas_call(
        finish_kernel,
        grid=(steps,),
        out_shape=tuple(wanted),
        in_specs=[in_steps(v) for v in (reduced, *plain)],
        out_specs=tuple(in_steps(v) for v in wanted),
        compiler_params=pltpu.CompilerParams(vmem_limit_bytes=62 << 20),
    )(reduced, *plain)
    index = lax.axis_index("batch")
    up_bias_sum = lax.dynamic_slice_in_dim(
        biases[: wide // width].reshape(1, wide), index * (wide // (2 * layers)), wide // (2 * layers), 1
    )
    down_bias_sum = lax.dynamic_slice_in_dim(
        biases[wide // width : wide // width + 1], index * (width // (2 * layers)), width // (2 * layers), 1
    )
    return (
        layer_output[None],
        grad_input[None],
        grad_memory[None],
        small[0],
        small[1],
        grad_self_project,
        grad_self_output,
        small[2],
        small[3],
        grad_cross_query,
        grad_cross_memory,
        grad_cross_output,
        small[4],
        small[5],
        grad_up[None],
        up_bias_sum,
        grad_down[None],
        down_bias_sum,
    )


def solution(mesh):
    return jax.shard_map(
        body,
        mesh=mesh,
        in_specs=(
            P(("batch", "exp"), None, None),
            P(("batch", "exp"), None, None),
            P(("batch", "exp"), None, None),
            P(("batch", "exp"), None, None),
            P(),
            P(),
            P(),
            P(),
            P(),
            P(),
            P(),
            P(),
            P(),
            P(),
            P(),
            P("exp", None, None),
            P("exp", None),
            P("exp", None, None),
            P("exp", None),
        ),
        out_specs=(
            P(("batch", "exp"), None, None),
            P(("batch", "exp"), None, None),
            P(("batch", "exp"), None, None),
            P(),
            P(),
            P(),
            P(),
            P(),
            P(),
            P(),
            P(),
            P(),
            P(),
            P(),
            P("exp", "batch", None),
            P("exp", "batch"),
            P("exp", "batch", None),
            P("exp", "batch"),
        ),
        check_vma=False,
    )
```

```python
import functools
import math

import jax
import jax.numpy as jnp
from jax import lax
from jax.experimental import pallas as pl
from jax.experimental.pallas import tpu as pltpu
from jax.sharding import PartitionSpec as P

HEADS = 8
HEAD_DIM = 64
CAPACITY = 4
PAIR = 2 * HEAD_DIM
PAIRS = HEADS // 2
EPSILON = 1e-05
NEGATIVE = -1e30
SCALE = HEAD_DIM ** (-0.5)
SCALE2 = SCALE * math.log2(math.e)
BF = jnp.bfloat16
F32 = jnp.float32


def nn(left, right):
    return lax.dot_general(left, right, (((1,), (0,)), ((), ())), preferred_element_type=F32)


def nt(left, right):
    return lax.dot_general(left, right, (((1,), (1,)), ((), ())), preferred_element_type=F32)


def tn(left, right):
    return lax.dot_general(left, right, (((0,), (0,)), ((), ())), preferred_element_type=F32)


def span(index, size):
    return pl.ds(pl.multiple_of(index * size, size), size)


def normalize(values):
    center = values - jnp.mean(values, -1, keepdims=True)
    scale = lax.rsqrt(jnp.mean(center * center, -1, keepdims=True) + EPSILON)
    return center * scale, scale


def normalize_back(hat, scale, grad, gain):
    gained = grad * gain
    first = jnp.mean(gained, -1, keepdims=True)
    second = jnp.mean(gained * hat, -1, keepdims=True)
    return scale * (gained - first - hat * second)


def causal_mask(scores, block, causal):
    length = scores.shape[0]
    if not causal:
        return scores
    key = lax.broadcasted_iota(jnp.int32, (block, block), 0)
    row = lax.broadcasted_iota(jnp.int32, (block, block), 1)
    last = jnp.where(row >= key, scores[length - block :], NEGATIVE)
    if length == block:
        return last
    return jnp.concatenate([scores[: length - block], last], 0)


def own_head(values, head):
    lane = lax.broadcasted_iota(jnp.int32, values.shape, 1) < HEAD_DIM
    return jnp.where(lane if head == 0 else ~lane, values, jnp.zeros_like(values))


def attend(query, keys, values, out, out_t, total, causal, block=512):
    rows = out.shape[0]
    count = rows // block

    def pair(hp, _):
        def columns(column):
            return pl.ds(pl.multiple_of(column + hp * PAIR, PAIR), PAIR)

        two_keys = keys[0][:, columns(keys[1])]
        values_t = values[0][:, columns(values[1])].T
        results = {}

        def first(i, head):
            length = (i + 1) * block if causal else two_keys.shape[0]
            own = own_head(query[0][i * block : (i + 1) * block, columns(query[1])], head)
            return causal_mask(nt(two_keys[:length], own), block, causal)

        def second(i, head, scores):
            length = scores.shape[0]
            place = pl.ds(i * block, block)
            highest = jnp.max(scores, 0, keepdims=True)
            weights = jnp.exp2(scores * SCALE2 - highest * SCALE2).astype(BF)
            extended = jnp.concatenate(
                [
                    values_t[head * HEAD_DIM : (head + 1) * HEAD_DIM, :length],
                    jnp.ones((16, length), BF),
                ],
                0,
            )
            summed = nn(extended, weights)
            sums = summed[HEAD_DIM : HEAD_DIM + 1]
            total[hp, head : head + 1, place] = highest * SCALE2 + jnp.log2(sums)
            results[head] = summed[:HEAD_DIM] / sums
            if head == 1:
                both = jnp.concatenate([results[0], results[1]], 0).astype(BF)
                out_t[pl.ds(pl.multiple_of(i * HEADS * HEAD_DIM + hp * PAIR, PAIR), PAIR)] = both
                out[place, span(hp, PAIR)] = both.T

        before = None
        for i in range(count):
            for head in range(2):
                scores = first(i, head)
                if before is not None:
                    second(*before)
                before = (i, head, scores)
        second(*before)
        return 0

    lax.fori_loop(0, PAIRS, pair, 0)


def attend_back(
    query, keys, values, grad_out, out, total, grad_query, grad_keys, grad_values, sums, causal, block, hook=None
):
    rows = grad_out.shape[0]
    count = rows // block

    def pair(hp, _):
        def columns(column):
            return pl.ds(pl.multiple_of(column + hp * PAIR, PAIR), PAIR)

        two_keys = keys[0][:, columns(keys[1])]
        two_values = values[0][:, columns(values[1])]
        keys_t = two_keys.T
        here = span(hp, PAIR)
        product = grad_out[:, here].astype(F32) * out[:, here].astype(F32)
        high = product.astype(BF)
        low = (product - high.astype(F32)).astype(BF)
        pick = (
            lax.broadcasted_iota(jnp.int32, (8, PAIR), 1) // HEAD_DIM
            == lax.broadcasted_iota(jnp.int32, (8, PAIR), 0)
        ).astype(F32).astype(BF)
        dots = nt(pick, high) + nt(pick, low)
        kept = {}

        def first(i, head):
            length = (i + 1) * block if causal else two_keys.shape[0]
            place = pl.ds(i * block, block)
            own_query = own_head(query[0][place, columns(query[1])], head)
            own_grad = own_head(grad_out[place, here], head)
            return (
                nt(two_keys[:length], own_query),
                nt(two_values[:length], own_grad),
                own_query,
                own_grad,
            )

        def second(i, head, state):
            scores, grad_probs, own_query, own_grad = state
            length = scores.shape[0]
            place = pl.ds(i * block, block)
            shifted = scores * SCALE2 - total[hp, head : head + 1, place]
            probs = jnp.exp2(causal_mask(shifted, block, causal))
            dot = dots[head : head + 1, i * block : (i + 1) * block]
            grad_scores = (probs * (grad_probs - dot)).astype(BF)
            back = nn(keys_t[head * HEAD_DIM : (head + 1) * HEAD_DIM, :length], grad_scores)
            kept[head] = (probs.astype(BF), grad_scores, own_query, own_grad, back)
            if head == 1:
                probs2, scores2 = [
                    jnp.concatenate([kept[0][n], kept[1][n]], 1) for n in range(2)
                ]
                query2, grad2 = [
                    jnp.concatenate([kept[0][n], kept[1][n]], 0) for n in range(2, 4)
                ]
                new_values = nn(probs2, grad2)
                new_keys = nn(scores2, query2)
                if i == count - 1:
                    sums[0][...] = new_keys
                    sums[1][...] = new_values
                else:
                    sums[0][:length] += new_keys
                    sums[1][:length] += new_values
                grad_query[0][place, columns(grad_query[1])] = (
                    jnp.concatenate([kept[0][4], kept[1][4]], 0).T * SCALE
                ).astype(BF)

        before = None
        for i in reversed(range(count)):
            for head in range(2):
                state = first(i, head)
                if before is not None:
                    second(*before)
                before = (i, head, state)
        second(*before)
        grad_keys[0][:, columns(grad_keys[1])] = (sums[0][...] * SCALE).astype(BF)
        grad_values[0][:, columns(grad_values[1])] = sums[1][...].astype(BF)
        if hook is not None:
            hook(hp)
        return 0

    lax.fori_loop(0, PAIRS, pair, 0)


def slot_of(routes, group, device, size):
    own = routes[group]
    rank = lax.fori_loop(
        0, group, lambda j, c: c + jnp.where(routes[j] == own, 1, 0).astype(jnp.int32), jnp.int32(0)
    )
    return partner_of(device, own, size) * CAPACITY + rank


def weigh(values, weight):
    return values * jnp.full(values.shape, weight.astype(F32), F32).astype(BF)


def pick_group(routes, source, group_rows, expert, rank):
    count = jnp.int32(0)
    total = None
    for group in range(source.shape[0] // group_rows):
        same = jnp.where(routes[group] == expert, 1, 0).astype(jnp.int32)
        hit = same * jnp.where(count == rank, 1, 0).astype(jnp.int32)
        count = count + same
        term = weigh(source[group * group_rows : (group + 1) * group_rows], hit)
        total = term if total is None else total + term
    return total


def partner_of(own, offset, size):
    result, bit = 0, 1
    while bit < size:
        result = result + lax.rem(own // bit + offset // bit, 2) * bit
        bit *= 2
    return result


ROWS = 512
MESH = pl.DeviceIdType.MESH
SAVED = 10


def forward_kernel(
    size,
    group_rows,
    routes,
    self_gain,
    self_shift,
    cross_gain,
    cross_shift,
    moe_gain,
    moe_shift,
    up_bias,
    down_bias,
    *refs,
):
    (
        x_h, memory_h, grad_h, project_h, output_h, query_h, memory_w_h, cross_w_h, up_h, down_h,
        saved_o, hidden1_o, hidden2_o, rows_out_o, returned_o, half_o,
        total1, total2, biases,
        x, memory, grad, self_project, self_output, cross_query, cross_memory, cross_output, up, down,
        arena, hidden1, hidden2, normed3, outbound, received, received_grad, flat_t, grad_t, halves,
        in_sems, out_sems, core_sems, free, grad_send, grad_recv, row_send, row_recv, back_send, back_recv,
    ) = refs
    rows, width = x.shape
    wide = up.shape[1]
    blocks = rows // ROWS
    part_rows = CAPACITY * group_rows
    slot_rows = size * part_rows
    batch, own = lax.axis_index("batch"), lax.axis_index("exp")

    layers = lax.axis_size("batch") // 2
    half = halves.shape[0] // 2
    piece = half // layers
    core, other = lax.rem(batch, 2), 1 - lax.rem(batch, 2)
    twin = (batch + other - core, own)

    def partner(offset):
        return (batch, partner_of(own, offset, size))

    loads = [
        pltpu.make_async_copy(source, target, in_sems.at[n])
        for n, (source, target) in enumerate(
            [
                (grad_h, grad), (x_h, x), (project_h, self_project), (memory_h, memory),
                (memory_w_h, cross_memory), (output_h, self_output), (query_h, cross_query),
                (cross_w_h, cross_output), (up_h, up), (down_h, down),
            ]
        )
    ]
    for load in loads:
        load.start()
    barrier = pltpu.get_barrier_semaphore()
    for offset in range(1, size):
        pl.semaphore_signal(barrier, inc=1, device_id=partner(offset), device_id_type=MESH)
    pl.semaphore_signal(barrier, inc=1, device_id=twin, device_id_type=MESH)
    pl.semaphore_wait(barrier, size)

    def part(ref, offset):
        return ref.at[pl.ds(pl.multiple_of(offset * part_rows, part_rows), part_rows)]

    def send(source, target, offset, send_sems, recv_sems):
        return pltpu.make_async_remote_copy(
            src_ref=part(source, offset),
            dst_ref=part(target, offset),
            send_sem=send_sems.at[offset],
            recv_sem=recv_sems.at[offset],
            device_id=partner(offset),
            device_id_type=MESH,
        )

    def dispatch(source, target, offset):
        expert = partner_of(own, offset, size)

        def one(rank, _):
            values = pick_group(routes, source, group_rows, expert, rank)
            target[pl.ds(pl.multiple_of(offset * part_rows + rank * group_rows, group_rows), group_rows)] = values
            return 0

        lax.fori_loop(0, CAPACITY, one, 0)

    near = [n for n in range(1, size) if bin(n).count("1") == 1]
    far = [n for n in range(1, size) if n not in near]

    def to_near(source, target, send_sems, recv_sems):
        for offset in near:
            dispatch(source, outbound, jnp.int32(offset))
            send(outbound, target, offset, send_sems, recv_sems).start()
        dispatch(source, target, jnp.int32(0))

        def one(offset, _):
            @pl.when(sum((offset // 2**n) % 2 for n in range(8)) != 1)
            def _():
                dispatch(source, outbound, offset)

            return 0

        lax.fori_loop(1, size, one, 0)

    def to_far(target, send_sems, recv_sems):
        for offset in far:
            send(outbound, target, offset, send_sems, recv_sems).start()

    loads[0].wait()
    to_near(grad, received_grad, grad_send, grad_recv)
    to_far(received_grad, grad_send, grad_recv)
    for load in loads[1:5]:
        load.wait()

    def place(which):
        return arena.at[pl.ds(which * rows, rows)]

    q, k, v, attn, attn_t, cq, mk, mv, cross, cross_t = [place(n) for n in range(SAVED)]

    def block1(i, _):
        here = span(i, ROWS)
        hat, _s = normalize(x[here].astype(F32))
        normed = (hat * self_gain[...] + self_shift[...]).astype(BF)
        for n, target in enumerate((q, k, v)):
            target[here] = nn(normed, self_project[:, n * width : (n + 1) * width]).astype(BF)
        for n, target in enumerate((mk, mv)):
            target[here] = nn(memory[here], cross_memory[:, n * width : (n + 1) * width]).astype(BF)
        return 0

    lax.fori_loop(0, blocks, block1, 0)
    attend((q, 0), (k, 0), (v, 0), attn, attn_t, total1, True)
    for load in loads[5:]:
        load.wait()

    def block2(i, _):
        here = span(i, ROWS)
        hidden = x[here].astype(F32) + nn(attn[here], self_output[...])
        hidden1[here] = hidden
        hat, _s = normalize(hidden)
        normed = (hat * cross_gain[...] + cross_shift[...]).astype(BF)
        cq[here] = nn(normed, cross_query[...]).astype(BF)
        return 0

    lax.fori_loop(0, blocks, block2, 0)
    ready = 8 * rows
    stores = [
        pltpu.make_async_copy(arena.at[pl.ds(0, ready)], saved_o.at[pl.ds(0, ready)], out_sems.at[0]),
        pltpu.make_async_copy(
            arena.at[pl.ds(ready, SAVED * rows - ready)],
            saved_o.at[pl.ds(ready, SAVED * rows - ready)],
            out_sems.at[1],
        ),
        pltpu.make_async_copy(hidden1, hidden1_o, out_sems.at[2]),
        pltpu.make_async_copy(hidden2, hidden2_o, out_sems.at[3]),
    ]
    stores[0].start()
    stores[2].start()
    attend((cq, 0), (mk, 0), (mv, 0), cross, cross_t, total2, False)
    stores[1].start()
    def block3(i, _):
        here = span(i, ROWS)
        hidden = hidden1[here] + nn(cross[here], cross_output[...])
        hidden2[here] = hidden
        hat, _s = normalize(hidden)
        normed3[here] = (hat * moe_gain[...] + moe_shift[...]).astype(BF)
        return 0

    lax.fori_loop(0, blocks, block3, 0)
    stores[3].start()

    def sent(source, target, send_sems, recv_sems):
        def one(offset, _):
            send(source, target, offset, send_sems, recv_sems).wait_send()
            return 0

        lax.fori_loop(1, size, one, 0)

    sent(outbound, received_grad, grad_send, grad_recv)
    to_near(normed3, received, row_send, row_recv)
    stores[0].wait()
    stores[1].wait()

    block_rows = max(512, part_rows)
    per = block_rows // part_rows
    chunk = 512
    first, third = math.sqrt(2.0 / math.pi), math.sqrt(2.0 / math.pi) * 0.044715
    flat_t[width:] = jnp.ones((flat_t.shape[0] - width, slot_rows), BF)

    def hidden_at(c, start, length):
        return arena.at[pl.ds(pl.multiple_of(c * slot_rows + start, block_rows), length)]

    def pre_at(c, start, length):
        return arena.at[
            pl.ds(pl.multiple_of((wide // chunk + c) * slot_rows + start, block_rows), length)
        ]

    def block(i, bias):
        for n in range(per):
            offset = i * per + n

            @pl.when(offset > 0)
            def _():
                send(outbound, received_grad, offset, grad_send, grad_recv).wait_recv()
                send(outbound, received, offset, row_send, row_recv).wait_recv()

        here = span(i, block_rows)
        flat = received[here]
        grads = received_grad[here]
        back = jnp.zeros((block_rows, width), F32)
        for c in range(wide // chunk):
            cols = pl.ds(c * chunk, chunk)
            pre = nn(flat, up[:, cols]) + up_bias[:, cols]
            square = pre * pre
            half = 0.5 + 0.5 * jnp.tanh(pre * (first + third * square))
            value = pre * half
            low = value.astype(BF)
            slope = half + value * (1.0 - half) * (2.0 * first + (6.0 * third) * square)
            gpre = (nt(grads, down[cols]) * slope).astype(BF)
            hidden_at(c, i * block_rows, block_rows)[...] = low
            pre_at(c, i * block_rows, block_rows)[...] = gpre
            back += nt(gpre, up[:, cols])
        received_grad[here] = back.astype(BF)
        for n in range(per):
            offset = i * per + n

            @pl.when(offset > 0)
            def _():
                send(received_grad, returned_o, offset, back_send, back_recv).start()

        @pl.when(i == 0)
        def _():
            to_far(received, row_send, row_recv)

        flat_t[:width, here] = flat.T
        grad_t[:, here] = grads.T
        return bias + jnp.sum(grads.astype(F32), 0, keepdims=True)

    bias = lax.fori_loop(0, slot_rows // block_rows, block, jnp.zeros((1, width), F32))
    sent(outbound, received, row_send, row_recv)
    pl.semaphore_signal(free, inc=1, device_id=twin, device_id_type=MESH)
    stores.append(
        pltpu.make_async_copy(part(received_grad, 0), part(returned_o, 0), out_sems.at[4])
    )
    stores[4].start()

    def rows_block(i, _):
        here = span(i, block_rows)
        out = down_bias[...]
        for c in range(wide // chunk):
            out = out + nn(hidden_at(c, i * block_rows, block_rows)[...], down[c * chunk : (c + 1) * chunk])
        received[here] = out.astype(BF)
        return 0

    up_rows, down_rows = width // (2 * layers), wide // (2 * layers)
    biases[...] = jnp.zeros_like(biases)
    per_chunk = chunk // down_rows

    def piece_at(number, start, length):
        row = lax.rem(number, 2) * half + number // 2 * piece + start
        return halves.at[pl.ds(pl.multiple_of(row, length), length)]

    def weights(c, _):
        cols = span(c, chunk)
        both = nn(flat_t[...], pre_at(c, 0, slot_rows)[...])
        for n in range(2 * layers):
            piece_at(jnp.int32(n), c * up_rows, up_rows)[...] = both[
                n * up_rows : (n + 1) * up_rows
            ].astype(BF)
        biases[pl.ds(c, 1)] = both[width : width + 1]
        down_t = nn(grad_t[...], hidden_at(c, 0, slot_rows)[...])
        for n in range(per_chunk):
            piece_at(c * per_chunk + n, wide // chunk * up_rows, down_rows)[...] = down_t[
                :, n * down_rows : (n + 1) * down_rows
            ].T.astype(BF)
        return 0

    lax.fori_loop(0, wide // chunk, weights, 0)
    biases[wide // chunk : wide // chunk + 1] = bias

    def half_at(which):
        return halves.at[pl.ds(pl.multiple_of(which * half, half), half)]

    to_twin = pltpu.make_async_remote_copy(
        src_ref=half_at(other),
        dst_ref=outbound,
        send_sem=core_sems.at[0],
        recv_sem=core_sems.at[1],
        device_id=twin,
        device_id_type=MESH,
    )
    pl.semaphore_wait(free, 1)
    to_twin.start()
    lax.fori_loop(0, slot_rows // block_rows, rows_block, 0)
    stores.append(pltpu.make_async_copy(received, rows_out_o, out_sems.at[5]))
    stores[5].start()
    to_twin.wait()

    def add_half(i, _):
        here = pl.ds(pl.multiple_of(core * half + i * ROWS, ROWS), ROWS)
        halves[here] = (halves[here].astype(F32) + outbound[span(i, ROWS)].astype(F32)).astype(BF)
        return 0

    lax.fori_loop(0, half // ROWS, add_half, 0)
    stores.append(pltpu.make_async_copy(half_at(core), half_o, out_sems.at[6]))
    stores[6].start()
    sent(received_grad, returned_o, back_send, back_recv)

    def arrived(offset, _):
        send(received_grad, returned_o, offset, back_send, back_recv).wait_recv()
        return 0

    lax.fori_loop(1, size, arrived, 0)
    for store in stores[2:]:
        store.wait()


MATS = 8


def back_kernel(
    size,
    layers,
    group_rows,
    routes,
    self_gain,
    self_shift,
    cross_gain,
    cross_shift,
    moe_gain,
    moe_shift,
    total1,
    total2,
    biases,
    *refs,
):
    (
        x_h, memory_h, grad_h, project_h, output_h, query_h, memory_w_h, cross_w_h,
        saved_h, hidden1_h, hidden2_h, returned_grad_h, rows_out_h, half_h,
        layer_o, grad_input_o, grad_memory_o, reduced_o, returned_o,
        small, up_o, down_o, bias_o,
        x, memory, grad, self_project, self_output, cross_query, cross_memory, cross_output,
        saved, hidden1, hidden2, returned,
        carried, carried_low, back_low, grad_q, grad_kv, grad_project, normed, sum_a, sum_b,
        grads, from_twin, from_exp, part, from_layer, from_layer_whole, shard,
        half, from_half, from_small, from_bias,
        in_sems, out_sems, ret_send, ret_recv, half_send, half_recv, bias_send, bias_recv,
        small_send, small_recv, sends, recvs,
    ) = refs
    rows, width = x.shape
    wide = up_o.shape[1]
    blocks = rows // ROWS
    per = ROWS // group_rows
    part_rows = CAPACITY * group_rows
    zero = jnp.zeros((1, width), F32)
    batch, own = lax.axis_index("batch"), lax.axis_index("exp")
    core, layer = lax.rem(batch, 2), batch // 2
    twin = (batch + 1 - 2 * core, own)

    def partner(offset):
        return (batch, partner_of(own, offset, size))

    def above(offset):
        return lax.rem(layer + offset, layers)

    def column(offset):
        return (above(offset) * 2 + core, own)

    pairs = [
        (hidden2_h, hidden2), (returned_grad_h, returned), (grad_h, grad), (cross_w_h, cross_output),
        (hidden1_h, hidden1), (memory_h, memory), (saved_h, saved),
        (query_h, cross_query), (memory_w_h, cross_memory), (output_h, self_output),
        (x_h, x), (project_h, self_project),
    ]
    piece = half_h.shape[0] // layers
    own_piece = half_h.at[pl.ds(pl.multiple_of(layer * piece, piece), piece)]
    pairs.append((own_piece, half))
    loads = [pltpu.make_async_copy(*pair, in_sems.at[n]) for n, pair in enumerate(pairs)]
    for load in loads:
        load.start()
    barrier = pltpu.get_barrier_semaphore()
    greeted = (
        [twin] + [partner(n) for n in range(1, size)] + [column(n) for n in range(1, layers)]
    )
    for device in greeted:
        pl.semaphore_signal(barrier, inc=1, device_id=device, device_id_type=MESH)
    pl.semaphore_wait(barrier, len(greeted))

    def remote(source, target, device, send_sem, recv_sem):
        return pltpu.make_async_remote_copy(
            src_ref=source,
            dst_ref=target,
            send_sem=send_sem,
            recv_sem=recv_sem,
            device_id=device,
            device_id_type=MESH,
        )

    def start_all(copies):
        for copy in copies:
            copy.start()

    def wait_all(copies):
        for copy in copies:
            copy.wait()

    def slots(ref, offset):
        return ref.at[pl.ds(offset * part_rows, part_rows)]

    back_rows = [
        remote(slots(rows_out_h, n), slots(returned_o, n), partner(n), ret_send.at[n], ret_recv.at[n])
        for n in range(1, size)
    ]
    start_all(back_rows)
    own_rows = pltpu.make_async_copy(slots(rows_out_h, 0), slots(returned_o, 0), out_sems.at[0])
    own_rows.start()

    turns = 8
    turn_rows = piece // turns
    pieces = [
        [
            remote(
                half_h.at[pl.ds(pl.multiple_of(above(n) * piece + turn * turn_rows, turn_rows), turn_rows)],
                from_half.at[n - 1, pl.ds(turn * turn_rows, turn_rows)],
                column(n),
                half_send.at[(n - 1) * turns + turn],
                half_recv.at[(n - 1) * turns + turn],
            )
            for n in range(1, layers)
        ]
        for turn in range(turns)
    ]
    start_all(pieces[0])
    start_all(pieces[1])
    start_all(pieces[3])
    start_all(pieces[4])
    start_all(pieces[5])

    q, k, v, attn, attn_t, cross_q, mk, mv, cross, cross_t = [
        saved.at[pl.ds(n * rows, rows)] for n in range(SAVED)
    ]
    gq, gk, gv = [grad_project.at[pl.ds(n * rows, rows)] for n in range(3)]
    gmk, gmv = [grad_kv.at[pl.ds(n * rows, rows)] for n in range(2)]

    def mat(number):
        return slice(number * width, (number + 1) * width)

    def times(turned, right):
        count = 512
        return sum(
            nn(turned[n * width : (n + 1) * width], right[n * count : (n + 1) * count])
            for n in range(rows // count)
        )

    def gather(source, group, place):
        expert = partner_of(own, routes[group], size)
        rank = lax.fori_loop(
            0,
            group,
            lambda j, c: c + jnp.where(routes[j] == routes[group], 1, 0).astype(jnp.int32),
            jnp.int32(0),
        )
        slot = expert * CAPACITY + rank
        total = None
        for n in range(size * CAPACITY):
            hit = jnp.where(slot == n, 1, 0).astype(jnp.int32)
            term = weigh(source[n * group_rows : (n + 1) * group_rows], hit)
            total = term if total is None else total + term
        place[span(group, group_rows)] = total

    def gather_all(source, place):
        def one(group, _):
            gather(source, group, place)
            return 0

        lax.fori_loop(0, rows // group_rows, one, 0)

    tall = grads.shape[0]
    by_core = tall // 2
    by_exp = by_core // size
    counter = [0]

    def pair_of_sems():
        counter[0] += 1
        return sends.at[counter[0] - 1], recvs.at[counter[0] - 1]

    def reduction(first, last, whole=False):
        split = layers if (by_exp // layers) % 16 == 0 and not whole else 1
        by_layer = by_exp // split
        landing = from_layer_whole if whole else from_layer
        shift = first if whole else 0
        cols = pl.ds(first, last - first)

        def lane(ref, start, length):
            return ref.at[pl.ds(pl.multiple_of(start, length), length), cols]

        mine = core * by_core
        core_copies = [
            remote(lane(grads, (1 - core) * by_core, by_core), from_twin.at[:, cols], twin, *pair_of_sems())
        ]
        exp_copies = [
            remote(
                lane(grads, mine + partner_of(own, n, size) * by_exp, by_exp),
                from_exp.at[n - 1, :, cols],
                partner(n),
                *pair_of_sems(),
            )
            for n in range(1, size)
        ]
        at_layer = layer * by_layer if split > 1 else 0
        layer_copies = [
            remote(
                lane(part, above(n) * by_layer if split > 1 else 0, by_layer),
                landing.at[n - 1, :, pl.ds(first - shift, last - first)],
                column(n),
                *pair_of_sems(),
            )
            for n in range(1, layers)
        ]
        share_copies = [
            remote(
                lane(shard, at_layer, by_layer),
                lane(shard, at_layer, by_layer),
                column(n),
                *pair_of_sems(),
            )
            for n in range(1, layers)
        ] if split > 1 else []
        spot = mine + own * by_exp
        out_copies = [
            remote(shard.at[:, cols], lane(reduced_o, spot, by_exp), partner(n), *pair_of_sems())
            for n in range(1, size)
        ]
        local = pltpu.make_async_copy(shard.at[:, cols], lane(reduced_o, spot, by_exp), pair_of_sems()[0])
        half_copies = [
            remote(lane(reduced_o, mine, by_core), lane(reduced_o, mine, by_core), twin, *pair_of_sems())
        ]

        def stage(number):
            if number == 0:
                start_all(core_copies)
            if number == 1:
                wait_all(core_copies)

                def add(i, _):
                    here = pl.ds(pl.multiple_of(mine + i * 64, 64), 64)
                    grads[here, cols] = (
                        grads[here, cols].astype(F32) + from_twin[span(i, 64), cols].astype(F32)
                    ).astype(BF)
                    return 0

                lax.fori_loop(0, by_core // 64, add, 0)
                start_all(exp_copies)
            if number == 2:
                wait_all(exp_copies)
                here = pl.ds(pl.multiple_of(spot, by_exp), by_exp)
                total = grads[here, cols].astype(F32)
                for n in range(size - 1):
                    total = total + from_exp[n, :, cols].astype(F32)
                part[:, cols] = total.astype(BF)
            if number == 3:
                start_all(layer_copies)
            if number == 4:
                wait_all(layer_copies)
                here = pl.ds(pl.multiple_of(at_layer, by_layer), by_layer)
                total = part[here, cols].astype(F32)
                for n in range(layers - 1):
                    total = total + landing[n, :, first - shift : last - shift].astype(F32)
                shard[here, cols] = total.astype(BF)
                start_all(share_copies)
            if number == 5:
                wait_all(share_copies)
                start_all(out_copies)
                local.start()
            if number == 6:
                wait_all(out_copies)
                local.wait()
                start_all(half_copies)
            if number == 7:
                wait_all(half_copies)

        return stage

    per_pair = 3 * PAIR
    two_pairs = 6 * PAIR
    part_a = reduction(7 * width, 8 * width)
    part_b = reduction(4 * width + two_pairs, 7 * width)
    first_sum = reduction(4 * width + two_pairs, 8 * width)
    cross_sum = reduction(4 * width, 4 * width + two_pairs)
    second_sum = reduction(3 * width, 4 * width)
    third_sum = reduction(0, two_pairs)
    fourth_sum = reduction(two_pairs, two_pairs + per_pair)
    last_sum = reduction(two_pairs + per_pair, 2 * two_pairs, True)

    for load in loads[:4]:
        load.wait()
    gather_all(returned, carried_low)

    def block3(i, carry):
        here = span(i, ROWS)
        hat, scale = normalize(hidden2[here])
        gy = carried_low[here].astype(F32)
        total = grad[here].astype(F32) + normalize_back(hat, scale, gy, moe_gain[...])
        carried[here] = total
        low = total.astype(BF)
        carried_low[here] = low
        back_low[here] = nt(low, cross_output[...]).astype(BF)
        return (
            carry[0] + jnp.sum(gy * hat, 0, keepdims=True),
            carry[1] + jnp.sum(gy, 0, keepdims=True),
        )

    gains3 = lax.fori_loop(0, blocks, block3, (zero, zero))

    bias_twin = [remote(biases, from_bias.at[0], twin, bias_send.at[0], bias_recv.at[0])]
    start_all(bias_twin)
    for load in loads[4:]:
        load.wait()
    grads[:, mat(7)] = times(cross_t, carried_low).astype(BF)
    part_a(0)
    start_all(pieces[2])
    for n in range(rows // 512):
        here = slice(n * 512, (n + 1) * 512)
        hat, _s = normalize(hidden1[here])
        normed[n * width : (n + 1) * width] = (
            (hat * cross_gain[...] + cross_shift[...]).astype(BF).T
        )
        memory[here] = memory[here].T

    def cross_grads(number):
        here = slice(2 * number * PAIR, 2 * (number + 1) * PAIR)
        base = 4 * width + (1 - number) * two_pairs
        two = jnp.concatenate([gmk[:, here], gmv[:, here]], 1)
        grads[:, base : base + 2 * PAIR] = times(normed, grad_q[:, here]).astype(BF)
        grads[:, base + 2 * PAIR : base + two_pairs] = times(memory, two).astype(BF)

    def cross_hook(hp):
        @pl.when(hp == 0)
        def _():
            part_a(1)
            pass

        @pl.when(hp == 1)
        def _():
            cross_grads(0)
            part_b(0)
            pass

        @pl.when(hp == 2)
        def _():
            part_b(1)

        @pl.when(hp == 3)
        def _():
            cross_grads(1)
            cross_sum(0)
            pass

    attend_back(
        (cross_q, 0), (mk, 0), (mv, 0), back_low, cross, total2,
        (grad_q, 0), (gmk, 0), (gmv, 0), (sum_a, sum_b), False, 256, cross_hook,
    )

    def block2(i, carry):
        here = span(i, ROWS)
        hat, scale = normalize(hidden1[here])
        gy = nt(grad_q[here], cross_query[...])
        total = carried[here] + normalize_back(hat, scale, gy, cross_gain[...])
        carried[here] = total
        low = total.astype(BF)
        carried_low[here] = low
        back_low[here] = nt(low, self_output[...]).astype(BF)
        return (
            carry[0] + jnp.sum(gy * hat, 0, keepdims=True),
            carry[1] + jnp.sum(gy, 0, keepdims=True),
        )

    gains2 = lax.fori_loop(0, blocks, block2, (zero, zero))
    cross_sum(1)
    part_a(2)
    part_b(2)
    first_sum(3)
    grads[:, mat(3)] = times(attn_t, carried_low).astype(BF)
    second_sum(0)
    wait_all(bias_twin)
    biases[...] += from_bias[0]
    bias_layers = [
        remote(biases, from_bias.at[n], column(n), bias_send.at[n], bias_recv.at[n])
        for n in range(1, layers)
    ]
    start_all(bias_layers)
    for n in range(rows // 512):
        hat, _s = normalize(x[n * 512 : (n + 1) * 512].astype(F32))
        normed[n * width : (n + 1) * width] = (
            (hat * self_gain[...] + self_shift[...]).astype(BF).T
        )

    def self_grads(first, pairs, base):
        here = slice(first * PAIR, (first + pairs) * PAIR)
        three = jnp.concatenate([gq[:, here], gk[:, here], gv[:, here]], 1)
        grads[:, base : base + 3 * pairs * PAIR] = times(normed, three).astype(BF)

    def self_hook(hp):
        @pl.when(hp == 0)
        def _():
            second_sum(1)
            first_sum(4)
            cross_sum(2)
            cross_sum(3)

        @pl.when(hp == 1)
        def _():
            self_grads(0, 2, 0)
            third_sum(0)

        @pl.when(hp == 2)
        def _():
            self_grads(2, 1, two_pairs)
            fourth_sum(0)
            third_sum(1)
            first_sum(5)
            second_sum(2)

        @pl.when(hp == 3)
        def _():
            self_grads(3, 1, two_pairs + per_pair)
            last_sum(0)
            fourth_sum(1)
            cross_sum(4)
            second_sum(3)

    attend_back(
        (q, 0), (k, 0), (v, 0), back_low, attn, total1,
        (gq, 0), (gk, 0), (gv, 0), (sum_a, sum_b), True, 256, self_hook,
    )
    last_sum(1)
    start_all(pieces[6])

    def block1(i, carry):
        here = span(i, ROWS)
        hat, scale = normalize(x[here].astype(F32))
        gy = sum(
            nt(ref[here], self_project[:, mat(n)]) for n, ref in enumerate((gq, gk, gv))
        )
        carried[here] += normalize_back(hat, scale, gy, self_gain[...])
        return (
            carry[0] + jnp.sum(gy * hat, 0, keepdims=True),
            carry[1] + jnp.sum(gy, 0, keepdims=True),
        )

    gains1 = lax.fori_loop(0, blocks, block1, (zero, zero))
    stores = [pltpu.make_async_copy(carried, grad_input_o, out_sems.at[1])]
    stores[0].start()
    small[...] = jnp.concatenate([*gains1, *gains2, *gains3, zero, zero], 0)

    def share_small(number, devices):
        copies = [
            remote(small, from_small.at[number + n], device, small_send.at[number + n], small_recv.at[number + n])
            for n, device in enumerate(devices)
        ]
        start_all(copies)

        def finish():
            wait_all(copies)
            total = small[...]
            for n in range(len(devices)):
                total = total + from_small[number + n]
            small[...] = total

        return finish

    finish = share_small(0, [twin])
    third_sum(2)
    third_sum(3)
    cross_sum(5)
    second_sum(4)
    second_sum(5)
    fourth_sum(2)
    fourth_sum(3)

    wait_all(back_rows)
    own_rows.wait()
    fetch = pltpu.make_async_copy(returned_o, returned, out_sems.at[2])
    fetch.start()
    finish()
    finish = share_small(1, [partner(n) for n in range(1, size)])
    third_sum(4)
    last_sum(2)
    last_sum(3)
    first_sum(6)

    def memory_block(i, _):
        here = span(i, ROWS)
        hidden1[here] = nt(gmk[here], cross_memory[:, :width]) + nt(gmv[here], cross_memory[:, width:])
        return 0

    lax.fori_loop(0, rows // ROWS, memory_block, 0)
    stores.append(pltpu.make_async_copy(hidden1, grad_memory_o, out_sems.at[3]))
    stores[1].start()
    third_sum(5)
    fourth_sum(4)
    start_all(pieces[7])
    fetch.wait()
    gather_all(returned, normed)

    def output_block(i, _):
        here = span(i, ROWS)
        grad[here] = (hidden2[here] + normed[here].astype(F32)).astype(BF)
        return 0

    lax.fori_loop(0, blocks, output_block, 0)
    stores.append(pltpu.make_async_copy(grad, layer_o, out_sems.at[4]))
    stores[2].start()
    fourth_sum(5)
    last_sum(4)
    last_sum(5)
    finish()
    finish = share_small(size, [column(n) for n in range(1, layers)])
    cross_sum(6)
    second_sum(6)
    third_sum(6)
    for turn in range(turns):
        wait_all(pieces[turn])
    up_rows = up_o.shape[0]
    for c in range(wide // width):
        total = half[pl.ds(c * up_rows, up_rows)].astype(F32)
        for n in range(layers - 1):
            total = total + from_half[n, c * up_rows : (c + 1) * up_rows].astype(F32)
        up_o[:, c * width : (c + 1) * width] = total
    down_rows = down_o.shape[0]
    start = wide // width * up_rows
    total = half[pl.ds(start, down_rows)].astype(F32)
    for n in range(layers - 1):
        total = total + from_half[n, start : start + down_rows].astype(F32)
    down_o[...] = total
    wait_all(bias_layers)
    total = biases[...]
    for n in range(1, layers):
        total = total + from_bias[n]
    bias_o[...] = total
    fourth_sum(6)
    finish()
    last_sum(6)
    for total in (first_sum, cross_sum, second_sum, third_sum, fourth_sum, last_sum):
        total(7)
    for store in stores:
        store.wait()


def finish_kernel(reduced, *refs):
    plain, (project, output, query, memory, cross), moved = refs[:5], refs[5:10], refs[10:]
    width = output.shape[1]
    spans = [(0, 2, 0), (2, 1, 6 * PAIR), (3, 1, 9 * PAIR)]
    crossed = [(2, 2, 4 * width), (0, 2, 4 * width + 6 * PAIR)]

    def widen(target, part, first, pairs, column):
        place = part * width + first * PAIR
        target[:, place : place + pairs * PAIR] = reduced[:, column : column + pairs * PAIR].astype(F32)

    for first, pairs, column in spans:
        for n in range(3):
            widen(project, n, first, pairs, column + n * pairs * PAIR)
    for first, pairs, column in crossed:
        widen(query, 0, first, pairs, column)
        for n in range(2):
            widen(memory, n, first, pairs, column + (n + 1) * pairs * PAIR)
    output[...] = reduced[:, 3 * width : 4 * width].astype(F32)
    cross[...] = reduced[:, 7 * width :].astype(F32)
    for source, target in zip(plain, moved):
        target[...] = source[...]


def body(
    layer_input,
    memory,
    routes,
    out_grad,
    self_gain,
    self_shift,
    self_project,
    self_output,
    cross_gain,
    cross_shift,
    cross_query,
    cross_memory,
    cross_output,
    moe_gain,
    moe_shift,
    expert_up,
    up_bias,
    expert_down,
    down_bias,
):
    x = layer_input[0]
    memory = memory[0]
    grad = out_grad[0]
    rows, width = x.shape
    wide = expert_up.shape[2]
    size = lax.axis_size("exp")
    groups = routes.shape[1]
    group_rows = rows // groups
    slot_rows = size * CAPACITY * group_rows
    route = routes.reshape(groups)
    gains = [v.reshape(1, width) for v in (self_gain, self_shift, cross_gain, cross_shift, moe_gain, moe_shift)]
    def array(shape, dtype):
        return jax.ShapeDtypeStruct(shape, dtype)

    vmem, smem, any_ = [pl.BlockSpec(memory_space=m) for m in (pltpu.VMEM, pltpu.SMEM, pl.ANY)]
    big = [
        x, memory, grad, self_project, self_output, cross_query, cross_memory, cross_output,
        expert_up[0], expert_down[0],
    ]
    sems = pltpu.SemaphoreType.DMA((size,))
    saved, hidden1, hidden2, rows_out, returned_grad, half, total1, total2, biases = pl.pallas_call(
        functools.partial(forward_kernel, size, group_rows),
        out_shape=(
            array((SAVED * rows, width), BF),
            array((rows, width), F32),
            array((rows, width), F32),
            array((slot_rows, width), BF),
            array((slot_rows, width), BF),
            array((wide, width), BF),
            array((PAIRS, 8, rows), F32),
            array((PAIRS, 8, rows), F32),
            array((8, width), F32),
        ),
        in_specs=[smem] + [vmem] * 8 + [any_] * 10,
        out_specs=(any_,) * 6 + (vmem,) * 3,
        scratch_shapes=[pltpu.VMEM(v.shape, v.dtype) for v in big]
        + [
            pltpu.VMEM(shape, dtype)
            for shape, dtype in [
                ((2 * slot_rows * (wide // 512), 512), BF),
                ((rows, width), F32),
                ((rows, width), F32),
                ((rows, width), BF),
                ((slot_rows, width), BF),
                ((slot_rows, width), BF),
                ((slot_rows, width), BF),
                ((width + 16, slot_rows), BF),
                ((width, slot_rows), BF),
                ((2 * wide, width), BF),
            ]
        ]
        + [pltpu.SemaphoreType.DMA((10,)), pltpu.SemaphoreType.DMA((7,)), pltpu.SemaphoreType.DMA((2,)), pltpu.SemaphoreType.REGULAR]
        + [sems] * 6,
        compiler_params=pltpu.CompilerParams(
            collective_id=0, has_side_effects=True, vmem_limit_bytes=62 << 20
        ),
        cost_estimate=pl.CostEstimate(flops=60 * 10**9, bytes_accessed=40 << 20, transcendentals=0),
    )(route, *gains, up_bias, down_bias, *big)
    layers = lax.axis_size("batch") // 2
    by_exp = width // 2 // size
    by_layer = by_exp // layers if (by_exp // layers) % 16 == 0 else by_exp
    piece = wide // layers
    back_in = [
        *big[:8], saved, hidden1, hidden2, returned_grad, rows_out, half,
    ]
    count = 8 * (4 + 2 * (size - 1) + 2 * (layers - 1))
    dma = pltpu.SemaphoreType.DMA
    (
        layer_output, grad_input, grad_memory, reduced, _returned, small, grad_up, grad_down, biases,
    ) = pl.pallas_call(
        functools.partial(back_kernel, size, layers, group_rows),
        out_shape=(
            array((rows, width), BF),
            array((rows, width), F32),
            array((rows, width), F32),
            array((width, MATS * width), BF),
            array((slot_rows, width), BF),
            array((8, width), F32),
            array((width // (2 * layers), wide), F32),
            array((wide // (2 * layers), width), F32),
            array((8, width), F32),
        ),
        in_specs=[smem] + [vmem] * 9 + [any_] * len(back_in),
        out_specs=(any_,) * 5 + (vmem,) * 4,
        scratch_shapes=[pltpu.VMEM(v.shape, v.dtype) for v in big[:8]]
        + [
            pltpu.VMEM(shape, dtype)
            for shape, dtype in [
                (saved.shape, BF),
                ((rows, width), F32),
                ((rows, width), F32),
                ((slot_rows, width), BF),
                ((rows, width), F32),
                ((rows, width), BF),
                ((rows, width), BF),
                ((rows, width), BF),
                ((2 * rows, width), BF),
                ((3 * rows, width), BF),
                ((rows, width), BF),
                ((rows, PAIR), F32),
                ((rows, PAIR), F32),
                ((width, MATS * width), BF),
                ((width // 2, MATS * width), BF),
                ((size - 1, by_exp, MATS * width), BF),
                ((by_exp, MATS * width), BF),
                ((layers - 1, by_layer, MATS * width), BF),
                ((layers - 1, by_exp, 3 * PAIR), BF),
                ((by_exp, MATS * width), BF),
                ((piece, width), BF),
                ((layers - 1, piece, width), BF),
                ((size + layers - 1, 8, width), F32),
                ((layers, 8, width), F32),
            ]
        ]
        + [dma((13,)), dma((5,)), sems, sems]
        + [dma((8 * layers,))] * 2
        + [dma((layers,))] * 2
        + [dma((size + layers - 1,))] * 2
        + [dma((count,))] * 2,
        compiler_params=pltpu.CompilerParams(
            collective_id=1, has_side_effects=True, vmem_limit_bytes=63 << 20
        ),
        cost_estimate=pl.CostEstimate(flops=60 * 10**9, bytes_accessed=40 << 20, transcendentals=0),
    )(route, *gains, total1, total2, biases, *back_in)
    shapes = [(width, 3 * width), (width, width), (width, width), (width, 2 * width), (width, width)]
    steps = 4
    plain = [grad_input, grad_memory, layer_output, grad_up, grad_down]
    wanted = [array(shape, F32) for shape in shapes] + [array(v.shape, v.dtype) for v in plain]

    def in_steps(value):
        return pl.BlockSpec((value.shape[0] // steps, value.shape[1]), lambda i: (i, 0))

    (
        grad_self_project, grad_self_output, grad_cross_query, grad_cross_memory, grad_cross_output,
        grad_input, grad_memory, layer_output, grad_up, grad_down,
    ) = pl.pallas_call(
        finish_kernel,
        grid=(steps,),
        out_shape=tuple(wanted),
        in_specs=[in_steps(v) for v in (reduced, *plain)],
        out_specs=tuple(in_steps(v) for v in wanted),
        compiler_params=pltpu.CompilerParams(vmem_limit_bytes=62 << 20),
    )(reduced, *plain)
    index = lax.axis_index("batch")
    up_bias_sum = lax.dynamic_slice_in_dim(
        biases[: wide // width].reshape(1, wide), index * (wide // (2 * layers)), wide // (2 * layers), 1
    )
    down_bias_sum = lax.dynamic_slice_in_dim(
        biases[wide // width : wide // width + 1], index * (width // (2 * layers)), width // (2 * layers), 1
    )
    return (
        layer_output[None],
        grad_input[None],
        grad_memory[None],
        small[0],
        small[1],
        grad_self_project,
        grad_self_output,
        small[2],
        small[3],
        grad_cross_query,
        grad_cross_memory,
        grad_cross_output,
        small[4],
        small[5],
        grad_up[None],
        up_bias_sum,
        grad_down[None],
        down_bias_sum,
    )


def solution(mesh):
    return jax.shard_map(
        body,
        mesh=mesh,
        in_specs=(
            P(("batch", "exp"), None, None),
            P(("batch", "exp"), None, None),
            P(("batch", "exp"), None, None),
            P(("batch", "exp"), None, None),
            P(),
            P(),
            P(),
            P(),
            P(),
            P(),
            P(),
            P(),
            P(),
            P(),
            P(),
            P("exp", None, None),
            P("exp", None),
            P("exp", None, None),
            P("exp", None),
        ),
        out_specs=(
            P(("batch", "exp"), None, None),
            P(("batch", "exp"), None, None),
            P(("batch", "exp"), None, None),
            P(),
            P(),
            P(),
            P(),
            P(),
            P(),
            P(),
            P(),
            P(),
            P(),
            P(),
            P("exp", "batch", None),
            P("exp", "batch"),
            P("exp", "batch", None),
            P("exp", "batch"),
        ),
        check_vma=False,
    )
```

```python
import functools
import math

import jax
import jax.numpy as jnp
from jax import lax
from jax.experimental import pallas as pl
from jax.experimental.pallas import tpu as pltpu
from jax.sharding import PartitionSpec as P

HEADS = 8
HEAD_DIM = 64
CAPACITY = 4
PAIR = 2 * HEAD_DIM
PAIRS = HEADS // 2
EPSILON = 1e-05
NEGATIVE = -1e30
SCALE = HEAD_DIM ** (-0.5)
SCALE2 = SCALE * math.log2(math.e)
BF = jnp.bfloat16
F32 = jnp.float32


def nn(left, right):
    return lax.dot_general(left, right, (((1,), (0,)), ((), ())), preferred_element_type=F32)


def nt(left, right):
    return lax.dot_general(left, right, (((1,), (1,)), ((), ())), preferred_element_type=F32)


def tn(left, right):
    return lax.dot_general(left, right, (((0,), (0,)), ((), ())), preferred_element_type=F32)


def span(index, size):
    return pl.ds(pl.multiple_of(index * size, size), size)


def normalize(values):
    center = values - jnp.mean(values, -1, keepdims=True)
    scale = lax.rsqrt(jnp.mean(center * center, -1, keepdims=True) + EPSILON)
    return center * scale, scale


def normalize_back(hat, scale, grad, gain):
    gained = grad * gain
    first = jnp.mean(gained, -1, keepdims=True)
    second = jnp.mean(gained * hat, -1, keepdims=True)
    return scale * (gained - first - hat * second)


def causal_mask(scores, block, causal):
    length = scores.shape[0]
    if not causal:
        return scores
    key = lax.broadcasted_iota(jnp.int32, (block, block), 0)
    row = lax.broadcasted_iota(jnp.int32, (block, block), 1)
    last = jnp.where(row >= key, scores[length - block :], NEGATIVE)
    if length == block:
        return last
    return jnp.concatenate([scores[: length - block], last], 0)


def own_head(values, head):
    lane = lax.broadcasted_iota(jnp.int32, values.shape, 1) < HEAD_DIM
    return jnp.where(lane if head == 0 else ~lane, values, jnp.zeros_like(values))


def attend(query, keys, values, out, out_t, total, causal, block=512):
    rows = out.shape[0]
    count = rows // block

    def pair(hp, _):
        def columns(column):
            return pl.ds(pl.multiple_of(column + hp * PAIR, PAIR), PAIR)

        two_keys = keys[0][:, columns(keys[1])]
        values_t = values[0][:, columns(values[1])].T
        results = {}

        def first(i, head):
            length = (i + 1) * block if causal else two_keys.shape[0]
            own = own_head(query[0][i * block : (i + 1) * block, columns(query[1])], head)
            return causal_mask(nt(two_keys[:length], own), block, causal)

        def second(i, head, scores):
            length = scores.shape[0]
            place = pl.ds(i * block, block)
            highest = jnp.max(scores, 0, keepdims=True)
            weights = jnp.exp2(scores * SCALE2 - highest * SCALE2).astype(BF)
            extended = jnp.concatenate(
                [
                    values_t[head * HEAD_DIM : (head + 1) * HEAD_DIM, :length],
                    jnp.ones((16, length), BF),
                ],
                0,
            )
            summed = nn(extended, weights)
            sums = summed[HEAD_DIM : HEAD_DIM + 1]
            total[hp, head : head + 1, place] = highest * SCALE2 + jnp.log2(sums)
            results[head] = summed[:HEAD_DIM] / sums
            if head == 1:
                both = jnp.concatenate([results[0], results[1]], 0).astype(BF)
                out_t[pl.ds(pl.multiple_of(i * HEADS * HEAD_DIM + hp * PAIR, PAIR), PAIR)] = both
                out[place, span(hp, PAIR)] = both.T

        before = None
        for i in range(count):
            for head in range(2):
                scores = first(i, head)
                if before is not None:
                    second(*before)
                before = (i, head, scores)
        second(*before)
        return 0

    lax.fori_loop(0, PAIRS, pair, 0)


def attend_back(
    query, keys, values, grad_out, out, total, grad_query, grad_keys, grad_values, sums, causal, block, hook=None
):
    rows = grad_out.shape[0]
    count = rows // block

    def pair(hp, _):
        def columns(column):
            return pl.ds(pl.multiple_of(column + hp * PAIR, PAIR), PAIR)

        two_keys = keys[0][:, columns(keys[1])]
        two_values = values[0][:, columns(values[1])]
        keys_t = two_keys.T
        here = span(hp, PAIR)
        product = grad_out[:, here].astype(F32) * out[:, here].astype(F32)
        high = product.astype(BF)
        low = (product - high.astype(F32)).astype(BF)
        pick = (
            lax.broadcasted_iota(jnp.int32, (8, PAIR), 1) // HEAD_DIM
            == lax.broadcasted_iota(jnp.int32, (8, PAIR), 0)
        ).astype(F32).astype(BF)
        dots = nt(pick, high) + nt(pick, low)
        kept = {}

        def first(i, head):
            length = (i + 1) * block if causal else two_keys.shape[0]
            place = pl.ds(i * block, block)
            own_query = own_head(query[0][place, columns(query[1])], head)
            own_grad = own_head(grad_out[place, here], head)
            return (
                nt(two_keys[:length], own_query),
                nt(two_values[:length], own_grad),
                own_query,
                own_grad,
            )

        def second(i, head, state):
            scores, grad_probs, own_query, own_grad = state
            length = scores.shape[0]
            place = pl.ds(i * block, block)
            shifted = scores * SCALE2 - total[hp, head : head + 1, place]
            probs = jnp.exp2(causal_mask(shifted, block, causal))
            dot = dots[head : head + 1, i * block : (i + 1) * block]
            grad_scores = (probs * (grad_probs - dot)).astype(BF)
            back = nn(keys_t[head * HEAD_DIM : (head + 1) * HEAD_DIM, :length], grad_scores)
            kept[head] = (probs.astype(BF), grad_scores, own_query, own_grad, back)
            if head == 1:
                probs2, scores2 = [
                    jnp.concatenate([kept[0][n], kept[1][n]], 1) for n in range(2)
                ]
                query2, grad2 = [
                    jnp.concatenate([kept[0][n], kept[1][n]], 0) for n in range(2, 4)
                ]
                new_values = nn(probs2, grad2)
                new_keys = nn(scores2, query2)
                if i == count - 1:
                    sums[0][...] = new_keys
                    sums[1][...] = new_values
                else:
                    sums[0][:length] += new_keys
                    sums[1][:length] += new_values
                grad_query[0][place, columns(grad_query[1])] = (
                    jnp.concatenate([kept[0][4], kept[1][4]], 0).T * SCALE
                ).astype(BF)

        before = None
        for i in reversed(range(count)):
            for head in range(2):
                state = first(i, head)
                if before is not None:
                    second(*before)
                before = (i, head, state)
        second(*before)
        grad_keys[0][:, columns(grad_keys[1])] = (sums[0][...] * SCALE).astype(BF)
        grad_values[0][:, columns(grad_values[1])] = sums[1][...].astype(BF)
        if hook is not None:
            hook(hp)
        return 0

    lax.fori_loop(0, PAIRS, pair, 0)


def slot_of(routes, group, device, size):
    own = routes[group]
    rank = lax.fori_loop(
        0, group, lambda j, c: c + jnp.where(routes[j] == own, 1, 0).astype(jnp.int32), jnp.int32(0)
    )
    return partner_of(device, own, size) * CAPACITY + rank


def weigh(values, weight):
    return values * jnp.full(values.shape, weight.astype(F32), F32).astype(BF)


def pick_group(routes, source, group_rows, expert, rank):
    count = jnp.int32(0)
    total = None
    for group in range(source.shape[0] // group_rows):
        same = jnp.where(routes[group] == expert, 1, 0).astype(jnp.int32)
        hit = same * jnp.where(count == rank, 1, 0).astype(jnp.int32)
        count = count + same
        term = weigh(source[group * group_rows : (group + 1) * group_rows], hit)
        total = term if total is None else total + term
    return total


def partner_of(own, offset, size):
    result, bit = 0, 1
    while bit < size:
        result = result + lax.rem(own // bit + offset // bit, 2) * bit
        bit *= 2
    return result


ROWS = 512
MESH = pl.DeviceIdType.MESH
SAVED = 10


def forward_kernel(
    size,
    group_rows,
    routes,
    self_gain,
    self_shift,
    cross_gain,
    cross_shift,
    moe_gain,
    moe_shift,
    up_bias,
    down_bias,
    *refs,
):
    (
        x_h, memory_h, grad_h, project_h, output_h, query_h, memory_w_h, cross_w_h, up_h, down_h,
        saved_o, hidden1_o, hidden2_o, rows_out_o, returned_o, half_o,
        total1, total2, biases,
        x, memory, grad, self_project, self_output, cross_query, cross_memory, cross_output, up, down,
        arena, hidden1, hidden2, normed3, outbound, received, received_grad, flat_t, grad_t, halves,
        in_sems, out_sems, core_sems, free, grad_send, grad_recv, row_send, row_recv, back_send, back_recv,
    ) = refs
    rows, width = x.shape
    wide = up.shape[1]
    blocks = rows // ROWS
    part_rows = CAPACITY * group_rows
    slot_rows = size * part_rows
    batch, own = lax.axis_index("batch"), lax.axis_index("exp")

    layers = lax.axis_size("batch") // 2
    half = halves.shape[0] // 2
    piece = half // layers
    core, other = lax.rem(batch, 2), 1 - lax.rem(batch, 2)
    twin = (batch + other - core, own)

    def partner(offset):
        return (batch, partner_of(own, offset, size))

    loads = [
        pltpu.make_async_copy(source, target, in_sems.at[n])
        for n, (source, target) in enumerate(
            [
                (grad_h, grad), (x_h, x), (project_h, self_project), (memory_h, memory),
                (memory_w_h, cross_memory), (output_h, self_output), (query_h, cross_query),
                (cross_w_h, cross_output), (up_h, up), (down_h, down),
            ]
        )
    ]
    for load in loads:
        load.start()
    barrier = pltpu.get_barrier_semaphore()
    for offset in range(1, size):
        pl.semaphore_signal(barrier, inc=1, device_id=partner(offset), device_id_type=MESH)
    pl.semaphore_signal(barrier, inc=1, device_id=twin, device_id_type=MESH)
    pl.semaphore_wait(barrier, size)

    def part(ref, offset):
        return ref.at[pl.ds(pl.multiple_of(offset * part_rows, part_rows), part_rows)]

    def send(source, target, offset, send_sems, recv_sems):
        return pltpu.make_async_remote_copy(
            src_ref=part(source, offset),
            dst_ref=part(target, offset),
            send_sem=send_sems.at[offset],
            recv_sem=recv_sems.at[offset],
            device_id=partner(offset),
            device_id_type=MESH,
        )

    def dispatch(source, target, offset):
        expert = partner_of(own, offset, size)

        def one(rank, _):
            values = pick_group(routes, source, group_rows, expert, rank)
            target[pl.ds(pl.multiple_of(offset * part_rows + rank * group_rows, group_rows), group_rows)] = values
            return 0

        lax.fori_loop(0, CAPACITY, one, 0)

    near = [n for n in range(1, size) if bin(n).count("1") == 1]
    far = [n for n in range(1, size) if n not in near]

    def to_near(source, target, send_sems, recv_sems):
        for offset in near:
            dispatch(source, outbound, jnp.int32(offset))
            send(outbound, target, offset, send_sems, recv_sems).start()
        dispatch(source, target, jnp.int32(0))

        def one(offset, _):
            @pl.when(sum((offset // 2**n) % 2 for n in range(8)) != 1)
            def _():
                dispatch(source, outbound, offset)

            return 0

        lax.fori_loop(1, size, one, 0)

    def to_far(target, send_sems, recv_sems):
        for offset in far:
            send(outbound, target, offset, send_sems, recv_sems).start()

    loads[0].wait()
    to_near(grad, received_grad, grad_send, grad_recv)
    to_far(received_grad, grad_send, grad_recv)
    for load in loads[1:5]:
        load.wait()

    def place(which):
        return arena.at[pl.ds(which * rows, rows)]

    q, k, v, attn, attn_t, cq, mk, mv, cross, cross_t = [place(n) for n in range(SAVED)]

    def block1(i, _):
        here = span(i, ROWS)
        hat, _s = normalize(x[here].astype(F32))
        normed = (hat * self_gain[...] + self_shift[...]).astype(BF)
        for n, target in enumerate((q, k, v)):
            target[here] = nn(normed, self_project[:, n * width : (n + 1) * width]).astype(BF)
        for n, target in enumerate((mk, mv)):
            target[here] = nn(memory[here], cross_memory[:, n * width : (n + 1) * width]).astype(BF)
        return 0

    lax.fori_loop(0, blocks, block1, 0)
    attend((q, 0), (k, 0), (v, 0), attn, attn_t, total1, True)
    for load in loads[5:]:
        load.wait()

    def block2(i, _):
        here = span(i, ROWS)
        hidden = x[here].astype(F32) + nn(attn[here], self_output[...])
        hidden1[here] = hidden
        hat, _s = normalize(hidden)
        normed = (hat * cross_gain[...] + cross_shift[...]).astype(BF)
        cq[here] = nn(normed, cross_query[...]).astype(BF)
        return 0

    lax.fori_loop(0, blocks, block2, 0)
    ready = 8 * rows
    stores = [
        pltpu.make_async_copy(arena.at[pl.ds(0, ready)], saved_o.at[pl.ds(0, ready)], out_sems.at[0]),
        pltpu.make_async_copy(
            arena.at[pl.ds(ready, SAVED * rows - ready)],
            saved_o.at[pl.ds(ready, SAVED * rows - ready)],
            out_sems.at[1],
        ),
        pltpu.make_async_copy(hidden1, hidden1_o, out_sems.at[2]),
        pltpu.make_async_copy(hidden2, hidden2_o, out_sems.at[3]),
    ]
    stores[0].start()
    stores[2].start()
    attend((cq, 0), (mk, 0), (mv, 0), cross, cross_t, total2, False)
    stores[1].start()
    def block3(i, _):
        here = span(i, ROWS)
        hidden = hidden1[here] + nn(cross[here], cross_output[...])
        hidden2[here] = hidden
        hat, _s = normalize(hidden)
        normed3[here] = (hat * moe_gain[...] + moe_shift[...]).astype(BF)
        return 0

    lax.fori_loop(0, blocks, block3, 0)
    stores[3].start()

    def sent(source, target, send_sems, recv_sems):
        def one(offset, _):
            send(source, target, offset, send_sems, recv_sems).wait_send()
            return 0

        lax.fori_loop(1, size, one, 0)

    sent(outbound, received_grad, grad_send, grad_recv)
    to_near(normed3, received, row_send, row_recv)
    stores[0].wait()
    stores[1].wait()

    block_rows = max(512, part_rows)
    per = block_rows // part_rows
    chunk = 512
    first, third = math.sqrt(2.0 / math.pi), math.sqrt(2.0 / math.pi) * 0.044715
    flat_t[width:] = jnp.ones((flat_t.shape[0] - width, slot_rows), BF)

    def hidden_at(c, start, length):
        return arena.at[pl.ds(pl.multiple_of(c * slot_rows + start, block_rows), length)]

    def pre_at(c, start, length):
        return arena.at[
            pl.ds(pl.multiple_of((wide // chunk + c) * slot_rows + start, block_rows), length)
        ]

    def block(i, bias):
        for n in range(per):
            offset = i * per + n

            @pl.when(offset > 0)
            def _():
                send(outbound, received_grad, offset, grad_send, grad_recv).wait_recv()
                send(outbound, received, offset, row_send, row_recv).wait_recv()

        here = span(i, block_rows)
        flat = received[here]
        grads = received_grad[here]
        back = jnp.zeros((block_rows, width), F32)
        for c in range(wide // chunk):
            cols = pl.ds(c * chunk, chunk)
            pre = nn(flat, up[:, cols]) + up_bias[:, cols]
            square = pre * pre
            half = 0.5 + 0.5 * jnp.tanh(pre * (first + third * square))
            value = pre * half
            low = value.astype(BF)
            slope = half + value * (1.0 - half) * (2.0 * first + (6.0 * third) * square)
            gpre = (nt(grads, down[cols]) * slope).astype(BF)
            hidden_at(c, i * block_rows, block_rows)[...] = low
            pre_at(c, i * block_rows, block_rows)[...] = gpre
            back += nt(gpre, up[:, cols])
        received_grad[here] = back.astype(BF)
        for n in range(per):
            offset = i * per + n

            @pl.when(offset > 0)
            def _():
                send(received_grad, returned_o, offset, back_send, back_recv).start()

        @pl.when(i == 0)
        def _():
            to_far(received, row_send, row_recv)

        flat_t[:width, here] = flat.T
        grad_t[:, here] = grads.T
        return bias + jnp.sum(grads.astype(F32), 0, keepdims=True)

    bias = lax.fori_loop(0, slot_rows // block_rows, block, jnp.zeros((1, width), F32))
    sent(outbound, received, row_send, row_recv)
    pl.semaphore_signal(free, inc=1, device_id=twin, device_id_type=MESH)
    stores.append(
        pltpu.make_async_copy(part(received_grad, 0), part(returned_o, 0), out_sems.at[4])
    )
    stores[4].start()

    def rows_block(i, _):
        here = span(i, block_rows)
        out = down_bias[...]
        for c in range(wide // chunk):
            out = out + nn(hidden_at(c, i * block_rows, block_rows)[...], down[c * chunk : (c + 1) * chunk])
        received[here] = out.astype(BF)
        return 0

    up_rows, down_rows = width // (2 * layers), wide // (2 * layers)
    biases[...] = jnp.zeros_like(biases)
    per_chunk = chunk // down_rows

    def piece_at(number, start, length):
        row = lax.rem(number, 2) * half + number // 2 * piece + start
        return halves.at[pl.ds(pl.multiple_of(row, length), length)]

    def weights(c, _):
        cols = span(c, chunk)
        both = nn(flat_t[...], pre_at(c, 0, slot_rows)[...])
        for n in range(2 * layers):
            piece_at(jnp.int32(n), c * up_rows, up_rows)[...] = both[
                n * up_rows : (n + 1) * up_rows
            ].astype(BF)
        biases[pl.ds(c, 1)] = both[width : width + 1]
        down_t = nn(grad_t[...], hidden_at(c, 0, slot_rows)[...])
        for n in range(per_chunk):
            piece_at(c * per_chunk + n, wide // chunk * up_rows, down_rows)[...] = down_t[
                :, n * down_rows : (n + 1) * down_rows
            ].T.astype(BF)
        return 0

    lax.fori_loop(0, wide // chunk, weights, 0)
    biases[wide // chunk : wide // chunk + 1] = bias

    def half_at(which):
        return halves.at[pl.ds(pl.multiple_of(which * half, half), half)]

    to_twin = pltpu.make_async_remote_copy(
        src_ref=half_at(other),
        dst_ref=outbound,
        send_sem=core_sems.at[0],
        recv_sem=core_sems.at[1],
        device_id=twin,
        device_id_type=MESH,
    )
    pl.semaphore_wait(free, 1)
    to_twin.start()
    lax.fori_loop(0, slot_rows // block_rows, rows_block, 0)
    stores.append(pltpu.make_async_copy(received, rows_out_o, out_sems.at[5]))
    stores[5].start()
    to_twin.wait()

    def add_half(i, _):
        here = pl.ds(pl.multiple_of(core * half + i * ROWS, ROWS), ROWS)
        halves[here] = (halves[here].astype(F32) + outbound[span(i, ROWS)].astype(F32)).astype(BF)
        return 0

    lax.fori_loop(0, half // ROWS, add_half, 0)
    stores.append(pltpu.make_async_copy(half_at(core), half_o, out_sems.at[6]))
    stores[6].start()
    sent(received_grad, returned_o, back_send, back_recv)

    def arrived(offset, _):
        send(received_grad, returned_o, offset, back_send, back_recv).wait_recv()
        return 0

    lax.fori_loop(1, size, arrived, 0)
    for store in stores[2:]:
        store.wait()


MATS = 8


def back_kernel(
    size,
    layers,
    group_rows,
    routes,
    self_gain,
    self_shift,
    cross_gain,
    cross_shift,
    moe_gain,
    moe_shift,
    total1,
    total2,
    biases,
    *refs,
):
    (
        x_h, memory_h, grad_h, project_h, output_h, query_h, memory_w_h, cross_w_h,
        saved_h, hidden1_h, hidden2_h, returned_grad_h, rows_out_h, half_h,
        layer_o, grad_input_o, grad_memory_o, reduced_o, returned_o,
        small, up_o, down_o, bias_o,
        x, memory, grad, self_project, self_output, cross_query, cross_memory, cross_output,
        saved, hidden1, hidden2, returned,
        carried, carried_low, back_low, grad_q, grad_kv, grad_project, normed, sum_a, sum_b,
        grads, from_twin, from_exp, part, from_layer, from_layer_whole, shard,
        half, from_half, from_small, from_bias,
        in_sems, out_sems, ret_send, ret_recv, half_send, half_recv, bias_send, bias_recv,
        small_send, small_recv, sends, recvs,
    ) = refs
    rows, width = x.shape
    wide = up_o.shape[1]
    blocks = rows // ROWS
    per = ROWS // group_rows
    part_rows = CAPACITY * group_rows
    zero = jnp.zeros((1, width), F32)
    batch, own = lax.axis_index("batch"), lax.axis_index("exp")
    core, layer = lax.rem(batch, 2), batch // 2
    twin = (batch + 1 - 2 * core, own)

    def partner(offset):
        return (batch, partner_of(own, offset, size))

    def above(offset):
        return lax.rem(layer + offset, layers)

    def column(offset):
        return (above(offset) * 2 + core, own)

    pairs = [
        (hidden2_h, hidden2), (returned_grad_h, returned), (grad_h, grad), (cross_w_h, cross_output),
        (hidden1_h, hidden1), (memory_h, memory), (saved_h, saved),
        (query_h, cross_query), (memory_w_h, cross_memory), (output_h, self_output),
        (x_h, x), (project_h, self_project),
    ]
    piece = half_h.shape[0] // layers
    own_piece = half_h.at[pl.ds(pl.multiple_of(layer * piece, piece), piece)]
    pairs.append((own_piece, half))
    loads = [pltpu.make_async_copy(*pair, in_sems.at[n]) for n, pair in enumerate(pairs)]
    for load in loads:
        load.start()
    barrier = pltpu.get_barrier_semaphore()
    greeted = (
        [twin] + [partner(n) for n in range(1, size)] + [column(n) for n in range(1, layers)]
    )
    for device in greeted:
        pl.semaphore_signal(barrier, inc=1, device_id=device, device_id_type=MESH)
    pl.semaphore_wait(barrier, len(greeted))

    def remote(source, target, device, send_sem, recv_sem):
        return pltpu.make_async_remote_copy(
            src_ref=source,
            dst_ref=target,
            send_sem=send_sem,
            recv_sem=recv_sem,
            device_id=device,
            device_id_type=MESH,
        )

    def start_all(copies):
        for copy in copies:
            copy.start()

    def wait_all(copies):
        for copy in copies:
            copy.wait()

    def slots(ref, offset):
        return ref.at[pl.ds(offset * part_rows, part_rows)]

    back_rows = [
        remote(slots(rows_out_h, n), slots(returned_o, n), partner(n), ret_send.at[n], ret_recv.at[n])
        for n in range(1, size)
    ]
    start_all(back_rows)
    own_rows = pltpu.make_async_copy(slots(rows_out_h, 0), slots(returned_o, 0), out_sems.at[0])
    own_rows.start()

    turns = 8
    turn_rows = piece // turns
    pieces = [
        [
            remote(
                half_h.at[pl.ds(pl.multiple_of(above(n) * piece + turn * turn_rows, turn_rows), turn_rows)],
                from_half.at[n - 1, pl.ds(turn * turn_rows, turn_rows)],
                column(n),
                half_send.at[(n - 1) * turns + turn],
                half_recv.at[(n - 1) * turns + turn],
            )
            for n in range(1, layers)
        ]
        for turn in range(turns)
    ]
    start_all(pieces[0])
    for turn in (1, 3, 4, 5):
        start_all(pieces[turn])

    q, k, v, attn, attn_t, cross_q, mk, mv, cross, cross_t = [
        saved.at[pl.ds(n * rows, rows)] for n in range(SAVED)
    ]
    gq, gk, gv = [grad_project.at[pl.ds(n * rows, rows)] for n in range(3)]
    gmk, gmv = [grad_kv.at[pl.ds(n * rows, rows)] for n in range(2)]

    def mat(number):
        return slice(number * width, (number + 1) * width)

    def times(turned, right):
        count = 512
        return sum(
            nn(turned[n * width : (n + 1) * width], right[n * count : (n + 1) * count])
            for n in range(rows // count)
        )

    def gather(source, group, place):
        expert = partner_of(own, routes[group], size)
        rank = lax.fori_loop(
            0,
            group,
            lambda j, c: c + jnp.where(routes[j] == routes[group], 1, 0).astype(jnp.int32),
            jnp.int32(0),
        )
        slot = expert * CAPACITY + rank
        total = None
        for n in range(size * CAPACITY):
            hit = jnp.where(slot == n, 1, 0).astype(jnp.int32)
            term = weigh(source[n * group_rows : (n + 1) * group_rows], hit)
            total = term if total is None else total + term
        place[span(group, group_rows)] = total

    def gather_all(source, place):
        def one(group, _):
            gather(source, group, place)
            return 0

        lax.fori_loop(0, rows // group_rows, one, 0)

    tall = grads.shape[0]
    by_core = tall // 2
    by_exp = by_core // size
    counter = [0]

    def pair_of_sems():
        counter[0] += 1
        return sends.at[counter[0] - 1], recvs.at[counter[0] - 1]

    def reduction(first, last, whole=False):
        split = layers if (by_exp // layers) % 16 == 0 and not whole else 1
        by_layer = by_exp // split
        landing = from_layer_whole if whole else from_layer
        shift = first if whole else 0
        cols = pl.ds(first, last - first)

        def lane(ref, start, length):
            return ref.at[pl.ds(pl.multiple_of(start, length), length), cols]

        mine = core * by_core
        core_copies = [
            remote(lane(grads, (1 - core) * by_core, by_core), from_twin.at[:, cols], twin, *pair_of_sems())
        ]
        exp_copies = [
            remote(
                lane(grads, mine + partner_of(own, n, size) * by_exp, by_exp),
                from_exp.at[n - 1, :, cols],
                partner(n),
                *pair_of_sems(),
            )
            for n in range(1, size)
        ]
        at_layer = layer * by_layer if split > 1 else 0
        layer_copies = [
            remote(
                lane(part, above(n) * by_layer if split > 1 else 0, by_layer),
                landing.at[n - 1, :, pl.ds(first - shift, last - first)],
                column(n),
                *pair_of_sems(),
            )
            for n in range(1, layers)
        ]
        share_copies = [
            remote(
                lane(shard, at_layer, by_layer),
                lane(shard, at_layer, by_layer),
                column(n),
                *pair_of_sems(),
            )
            for n in range(1, layers)
        ] if split > 1 else []
        spot = mine + own * by_exp
        out_copies = [
            remote(shard.at[:, cols], lane(reduced_o, spot, by_exp), partner(n), *pair_of_sems())
            for n in range(1, size)
        ]
        local = pltpu.make_async_copy(shard.at[:, cols], lane(reduced_o, spot, by_exp), pair_of_sems()[0])
        half_copies = [
            remote(lane(reduced_o, mine, by_core), lane(reduced_o, mine, by_core), twin, *pair_of_sems())
        ]

        def stage(number):
            if number == 0:
                start_all(core_copies)
            if number == 1:
                wait_all(core_copies)

                def add(i, _):
                    here = pl.ds(pl.multiple_of(mine + i * 64, 64), 64)
                    grads[here, cols] = (
                        grads[here, cols].astype(F32) + from_twin[span(i, 64), cols].astype(F32)
                    ).astype(BF)
                    return 0

                lax.fori_loop(0, by_core // 64, add, 0)
                start_all(exp_copies)
            if number == 2:
                wait_all(exp_copies)
                here = pl.ds(pl.multiple_of(spot, by_exp), by_exp)
                total = grads[here, cols].astype(F32)
                for n in range(size - 1):
                    total = total + from_exp[n, :, cols].astype(F32)
                part[:, cols] = total.astype(BF)
            if number == 3:
                start_all(layer_copies)
            if number == 4:
                wait_all(layer_copies)
                here = pl.ds(pl.multiple_of(at_layer, by_layer), by_layer)
                total = part[here, cols].astype(F32)
                for n in range(layers - 1):
                    total = total + landing[n, :, first - shift : last - shift].astype(F32)
                shard[here, cols] = total.astype(BF)
                start_all(share_copies)
            if number == 5:
                wait_all(share_copies)
                start_all(out_copies)
                local.start()
            if number == 6:
                wait_all(out_copies)
                local.wait()
                start_all(half_copies)
            if number == 7:
                wait_all(half_copies)

        return stage

    per_pair = 3 * PAIR
    two_pairs = 6 * PAIR
    part_a = reduction(7 * width, 8 * width)
    part_b = reduction(4 * width + two_pairs, 7 * width)
    first_sum = reduction(4 * width + two_pairs, 8 * width)
    cross_sum = reduction(4 * width, 4 * width + two_pairs)
    second_sum = reduction(3 * width, 4 * width)
    third_sum = reduction(0, two_pairs)
    fourth_sum = reduction(two_pairs, two_pairs + per_pair)
    last_sum = reduction(two_pairs + per_pair, 2 * two_pairs, True)

    for load in loads[:4]:
        load.wait()
    gather_all(returned, carried_low)

    def block3(i, carry):
        here = span(i, ROWS)
        hat, scale = normalize(hidden2[here])
        gy = carried_low[here].astype(F32)
        total = grad[here].astype(F32) + normalize_back(hat, scale, gy, moe_gain[...])
        carried[here] = total
        low = total.astype(BF)
        carried_low[here] = low
        back_low[here] = nt(low, cross_output[...]).astype(BF)
        return (
            carry[0] + jnp.sum(gy * hat, 0, keepdims=True),
            carry[1] + jnp.sum(gy, 0, keepdims=True),
        )

    gains3 = lax.fori_loop(0, blocks, block3, (zero, zero))

    bias_twin = [remote(biases, from_bias.at[0], twin, bias_send.at[0], bias_recv.at[0])]
    start_all(bias_twin)
    for load in loads[4:]:
        load.wait()
    grads[:, mat(7)] = times(cross_t, carried_low).astype(BF)
    part_a(0)
    start_all(pieces[2])
    for n in range(rows // 512):
        here = slice(n * 512, (n + 1) * 512)
        hat, _s = normalize(hidden1[here])
        normed[n * width : (n + 1) * width] = (
            (hat * cross_gain[...] + cross_shift[...]).astype(BF).T
        )
        memory[here] = memory[here].T

    def cross_grads(number):
        here = slice(2 * number * PAIR, 2 * (number + 1) * PAIR)
        base = 4 * width + (1 - number) * two_pairs
        two = jnp.concatenate([gmk[:, here], gmv[:, here]], 1)
        grads[:, base : base + 2 * PAIR] = times(normed, grad_q[:, here]).astype(BF)
        grads[:, base + 2 * PAIR : base + two_pairs] = times(memory, two).astype(BF)

    def cross_hook(hp):
        @pl.when(hp == 0)
        def _():
            part_a(1)

        @pl.when(hp == 1)
        def _():
            cross_grads(0)
            part_b(0)

        @pl.when(hp == 2)
        def _():
            part_b(1)

        @pl.when(hp == 3)
        def _():
            cross_grads(1)
            cross_sum(0)

    attend_back(
        (cross_q, 0), (mk, 0), (mv, 0), back_low, cross, total2,
        (grad_q, 0), (gmk, 0), (gmv, 0), (sum_a, sum_b), False, 256, cross_hook,
    )

    def block2(i, carry):
        here = span(i, ROWS)
        hat, scale = normalize(hidden1[here])
        gy = nt(grad_q[here], cross_query[...])
        total = carried[here] + normalize_back(hat, scale, gy, cross_gain[...])
        carried[here] = total
        low = total.astype(BF)
        carried_low[here] = low
        back_low[here] = nt(low, self_output[...]).astype(BF)
        return (
            carry[0] + jnp.sum(gy * hat, 0, keepdims=True),
            carry[1] + jnp.sum(gy, 0, keepdims=True),
        )

    gains2 = lax.fori_loop(0, blocks, block2, (zero, zero))
    cross_sum(1)
    part_a(2)
    part_b(2)
    first_sum(3)
    grads[:, mat(3)] = times(attn_t, carried_low).astype(BF)
    second_sum(0)
    wait_all(bias_twin)
    biases[...] += from_bias[0]
    bias_layers = [
        remote(biases, from_bias.at[n], column(n), bias_send.at[n], bias_recv.at[n])
        for n in range(1, layers)
    ]
    start_all(bias_layers)
    for n in range(rows // 512):
        hat, _s = normalize(x[n * 512 : (n + 1) * 512].astype(F32))
        normed[n * width : (n + 1) * width] = (
            (hat * self_gain[...] + self_shift[...]).astype(BF).T
        )

    def self_grads(first, pairs, base):
        here = slice(first * PAIR, (first + pairs) * PAIR)
        three = jnp.concatenate([gq[:, here], gk[:, here], gv[:, here]], 1)
        grads[:, base : base + 3 * pairs * PAIR] = times(normed, three).astype(BF)

    def self_hook(hp):
        @pl.when(hp == 0)
        def _():
            second_sum(1)
            first_sum(4)
            cross_sum(2)
            cross_sum(3)

        @pl.when(hp == 1)
        def _():
            self_grads(0, 2, 0)
            third_sum(0)

        @pl.when(hp == 2)
        def _():
            self_grads(2, 1, two_pairs)
            fourth_sum(0)
            third_sum(1)
            first_sum(5)
            second_sum(2)

        @pl.when(hp == 3)
        def _():
            self_grads(3, 1, two_pairs + per_pair)
            last_sum(0)
            fourth_sum(1)
            cross_sum(4)
            second_sum(3)

    attend_back(
        (q, 0), (k, 0), (v, 0), back_low, attn, total1,
        (gq, 0), (gk, 0), (gv, 0), (sum_a, sum_b), True, 256, self_hook,
    )
    start_all(pieces[6])

    def block1(i, carry):
        here = span(i, ROWS)
        hat, scale = normalize(x[here].astype(F32))
        gy = sum(
            nt(ref[here], self_project[:, mat(n)]) for n, ref in enumerate((gq, gk, gv))
        )
        carried[here] += normalize_back(hat, scale, gy, self_gain[...])
        return (
            carry[0] + jnp.sum(gy * hat, 0, keepdims=True),
            carry[1] + jnp.sum(gy, 0, keepdims=True),
        )

    gains1 = lax.fori_loop(0, blocks, block1, (zero, zero))
    stores = [pltpu.make_async_copy(carried, grad_input_o, out_sems.at[1])]
    stores[0].start()
    small[...] = jnp.concatenate([*gains1, *gains2, *gains3, zero, zero], 0)

    def share_small(number, devices):
        copies = [
            remote(small, from_small.at[number + n], device, small_send.at[number + n], small_recv.at[number + n])
            for n, device in enumerate(devices)
        ]
        start_all(copies)

        def finish():
            wait_all(copies)
            total = small[...]
            for n in range(len(devices)):
                total = total + from_small[number + n]
            small[...] = total

        return finish

    finish = share_small(0, [twin])
    last_sum(1)
    third_sum(2)
    third_sum(3)
    cross_sum(5)
    second_sum(4)
    second_sum(5)
    fourth_sum(2)
    fourth_sum(3)

    wait_all(back_rows)
    own_rows.wait()
    fetch = pltpu.make_async_copy(returned_o, returned, out_sems.at[2])
    fetch.start()
    finish()
    finish = share_small(1, [partner(n) for n in range(1, size)])
    third_sum(4)
    last_sum(2)
    last_sum(3)
    first_sum(6)

    def memory_block(i, _):
        here = span(i, ROWS)
        hidden1[here] = nt(gmk[here], cross_memory[:, :width]) + nt(gmv[here], cross_memory[:, width:])
        return 0

    lax.fori_loop(0, rows // ROWS, memory_block, 0)
    stores.append(pltpu.make_async_copy(hidden1, grad_memory_o, out_sems.at[3]))
    stores[1].start()
    third_sum(5)
    fourth_sum(4)
    start_all(pieces[7])
    fetch.wait()
    gather_all(returned, normed)

    def output_block(i, _):
        here = span(i, ROWS)
        grad[here] = (hidden2[here] + normed[here].astype(F32)).astype(BF)
        return 0

    lax.fori_loop(0, blocks, output_block, 0)
    stores.append(pltpu.make_async_copy(grad, layer_o, out_sems.at[4]))
    stores[2].start()
    fourth_sum(5)
    last_sum(4)
    last_sum(5)
    finish()
    finish = share_small(size, [column(n) for n in range(1, layers)])
    cross_sum(6)
    second_sum(6)
    third_sum(6)
    for turn in range(turns):
        wait_all(pieces[turn])
    up_rows = up_o.shape[0]
    for c in range(wide // width):
        total = half[pl.ds(c * up_rows, up_rows)].astype(F32)
        for n in range(layers - 1):
            total = total + from_half[n, c * up_rows : (c + 1) * up_rows].astype(F32)
        up_o[:, c * width : (c + 1) * width] = total
    down_rows = down_o.shape[0]
    start = wide // width * up_rows
    total = half[pl.ds(start, down_rows)].astype(F32)
    for n in range(layers - 1):
        total = total + from_half[n, start : start + down_rows].astype(F32)
    down_o[...] = total
    wait_all(bias_layers)
    total = biases[...]
    for n in range(1, layers):
        total = total + from_bias[n]
    bias_o[...] = total
    fourth_sum(6)
    finish()
    last_sum(6)
    for total in (first_sum, cross_sum, second_sum, third_sum, fourth_sum, last_sum):
        total(7)
    for store in stores:
        store.wait()


def finish_kernel(reduced, *refs):
    plain, (project, output, query, memory, cross), moved = refs[:5], refs[5:10], refs[10:]
    width = output.shape[1]
    spans = [(0, 2, 0), (2, 1, 6 * PAIR), (3, 1, 9 * PAIR)]
    crossed = [(2, 2, 4 * width), (0, 2, 4 * width + 6 * PAIR)]

    def widen(target, part, first, pairs, column):
        place = part * width + first * PAIR
        target[:, place : place + pairs * PAIR] = reduced[:, column : column + pairs * PAIR].astype(F32)

    for first, pairs, column in spans:
        for n in range(3):
            widen(project, n, first, pairs, column + n * pairs * PAIR)
    for first, pairs, column in crossed:
        widen(query, 0, first, pairs, column)
        for n in range(2):
            widen(memory, n, first, pairs, column + (n + 1) * pairs * PAIR)
    output[...] = reduced[:, 3 * width : 4 * width].astype(F32)
    cross[...] = reduced[:, 7 * width :].astype(F32)
    for source, target in zip(plain, moved):
        target[...] = source[...]


def body(
    layer_input,
    memory,
    routes,
    out_grad,
    self_gain,
    self_shift,
    self_project,
    self_output,
    cross_gain,
    cross_shift,
    cross_query,
    cross_memory,
    cross_output,
    moe_gain,
    moe_shift,
    expert_up,
    up_bias,
    expert_down,
    down_bias,
):
    x = layer_input[0]
    memory = memory[0]
    grad = out_grad[0]
    rows, width = x.shape
    wide = expert_up.shape[2]
    size = lax.axis_size("exp")
    groups = routes.shape[1]
    group_rows = rows // groups
    slot_rows = size * CAPACITY * group_rows
    route = routes.reshape(groups)
    gains = [v.reshape(1, width) for v in (self_gain, self_shift, cross_gain, cross_shift, moe_gain, moe_shift)]
    def array(shape, dtype):
        return jax.ShapeDtypeStruct(shape, dtype)

    vmem, smem, any_ = [pl.BlockSpec(memory_space=m) for m in (pltpu.VMEM, pltpu.SMEM, pl.ANY)]
    big = [
        x, memory, grad, self_project, self_output, cross_query, cross_memory, cross_output,
        expert_up[0], expert_down[0],
    ]
    sems = pltpu.SemaphoreType.DMA((size,))
    saved, hidden1, hidden2, rows_out, returned_grad, half, total1, total2, biases = pl.pallas_call(
        functools.partial(forward_kernel, size, group_rows),
        out_shape=(
            array((SAVED * rows, width), BF),
            array((rows, width), F32),
            array((rows, width), F32),
            array((slot_rows, width), BF),
            array((slot_rows, width), BF),
            array((wide, width), BF),
            array((PAIRS, 8, rows), F32),
            array((PAIRS, 8, rows), F32),
            array((8, width), F32),
        ),
        in_specs=[smem] + [vmem] * 8 + [any_] * 10,
        out_specs=(any_,) * 6 + (vmem,) * 3,
        scratch_shapes=[pltpu.VMEM(v.shape, v.dtype) for v in big]
        + [
            pltpu.VMEM(shape, dtype)
            for shape, dtype in [
                ((2 * slot_rows * (wide // 512), 512), BF),
                ((rows, width), F32),
                ((rows, width), F32),
                ((rows, width), BF),
                ((slot_rows, width), BF),
                ((slot_rows, width), BF),
                ((slot_rows, width), BF),
                ((width + 16, slot_rows), BF),
                ((width, slot_rows), BF),
                ((2 * wide, width), BF),
            ]
        ]
        + [pltpu.SemaphoreType.DMA((10,)), pltpu.SemaphoreType.DMA((7,)), pltpu.SemaphoreType.DMA((2,)), pltpu.SemaphoreType.REGULAR]
        + [sems] * 6,
        compiler_params=pltpu.CompilerParams(
            collective_id=0, has_side_effects=True, vmem_limit_bytes=62 << 20
        ),
        cost_estimate=pl.CostEstimate(flops=60 * 10**9, bytes_accessed=40 << 20, transcendentals=0),
    )(route, *gains, up_bias, down_bias, *big)
    layers = lax.axis_size("batch") // 2
    by_exp = width // 2 // size
    by_layer = by_exp // layers if (by_exp // layers) % 16 == 0 else by_exp
    piece = wide // layers
    back_in = [
        *big[:8], saved, hidden1, hidden2, returned_grad, rows_out, half,
    ]
    count = 8 * (4 + 2 * (size - 1) + 2 * (layers - 1))
    dma = pltpu.SemaphoreType.DMA
    (
        layer_output, grad_input, grad_memory, reduced, _returned, small, grad_up, grad_down, biases,
    ) = pl.pallas_call(
        functools.partial(back_kernel, size, layers, group_rows),
        out_shape=(
            array((rows, width), BF),
            array((rows, width), F32),
            array((rows, width), F32),
            array((width, MATS * width), BF),
            array((slot_rows, width), BF),
            array((8, width), F32),
            array((width // (2 * layers), wide), F32),
            array((wide // (2 * layers), width), F32),
            array((8, width), F32),
        ),
        in_specs=[smem] + [vmem] * 9 + [any_] * len(back_in),
        out_specs=(any_,) * 5 + (vmem,) * 4,
        scratch_shapes=[pltpu.VMEM(v.shape, v.dtype) for v in big[:8]]
        + [
            pltpu.VMEM(shape, dtype)
            for shape, dtype in [
                (saved.shape, BF),
                ((rows, width), F32),
                ((rows, width), F32),
                ((slot_rows, width), BF),
                ((rows, width), F32),
                ((rows, width), BF),
                ((rows, width), BF),
                ((rows, width), BF),
                ((2 * rows, width), BF),
                ((3 * rows, width), BF),
                ((rows, width), BF),
                ((rows, PAIR), F32),
                ((rows, PAIR), F32),
                ((width, MATS * width), BF),
                ((width // 2, MATS * width), BF),
                ((size - 1, by_exp, MATS * width), BF),
                ((by_exp, MATS * width), BF),
                ((layers - 1, by_layer, MATS * width), BF),
                ((layers - 1, by_exp, 3 * PAIR), BF),
                ((by_exp, MATS * width), BF),
                ((piece, width), BF),
                ((layers - 1, piece, width), BF),
                ((size + layers - 1, 8, width), F32),
                ((layers, 8, width), F32),
            ]
        ]
        + [dma((13,)), dma((5,)), sems, sems]
        + [dma((8 * layers,))] * 2
        + [dma((layers,))] * 2
        + [dma((size + layers - 1,))] * 2
        + [dma((count,))] * 2,
        compiler_params=pltpu.CompilerParams(
            collective_id=1, has_side_effects=True, vmem_limit_bytes=63 << 20
        ),
        cost_estimate=pl.CostEstimate(flops=60 * 10**9, bytes_accessed=40 << 20, transcendentals=0),
    )(route, *gains, total1, total2, biases, *back_in)
    shapes = [(width, 3 * width), (width, width), (width, width), (width, 2 * width), (width, width)]
    steps = 4
    plain = [grad_input, grad_memory, layer_output, grad_up, grad_down]
    wanted = [array(shape, F32) for shape in shapes] + [array(v.shape, v.dtype) for v in plain]

    def in_steps(value):
        return pl.BlockSpec((value.shape[0] // steps, value.shape[1]), lambda i: (i, 0))

    (
        grad_self_project, grad_self_output, grad_cross_query, grad_cross_memory, grad_cross_output,
        grad_input, grad_memory, layer_output, grad_up, grad_down,
    ) = pl.pallas_call(
        finish_kernel,
        grid=(steps,),
        out_shape=tuple(wanted),
        in_specs=[in_steps(v) for v in (reduced, *plain)],
        out_specs=tuple(in_steps(v) for v in wanted),
        compiler_params=pltpu.CompilerParams(vmem_limit_bytes=62 << 20),
    )(reduced, *plain)
    index = lax.axis_index("batch")
    up_bias_sum = lax.dynamic_slice_in_dim(
        biases[: wide // width].reshape(1, wide), index * (wide // (2 * layers)), wide // (2 * layers), 1
    )
    down_bias_sum = lax.dynamic_slice_in_dim(
        biases[wide // width : wide // width + 1], index * (width // (2 * layers)), width // (2 * layers), 1
    )
    return (
        layer_output[None],
        grad_input[None],
        grad_memory[None],
        small[0],
        small[1],
        grad_self_project,
        grad_self_output,
        small[2],
        small[3],
        grad_cross_query,
        grad_cross_memory,
        grad_cross_output,
        small[4],
        small[5],
        grad_up[None],
        up_bias_sum,
        grad_down[None],
        down_bias_sum,
    )


def solution(mesh):
    return jax.shard_map(
        body,
        mesh=mesh,
        in_specs=(
            P(("batch", "exp"), None, None),
            P(("batch", "exp"), None, None),
            P(("batch", "exp"), None, None),
            P(("batch", "exp"), None, None),
            P(),
            P(),
            P(),
            P(),
            P(),
            P(),
            P(),
            P(),
            P(),
            P(),
            P(),
            P("exp", None, None),
            P("exp", None),
            P("exp", None, None),
            P("exp", None),
        ),
        out_specs=(
            P(("batch", "exp"), None, None),
            P(("batch", "exp"), None, None),
            P(("batch", "exp"), None, None),
            P(),
            P(),
            P(),
            P(),
            P(),
            P(),
            P(),
            P(),
            P(),
            P(),
            P(),
            P("exp", "batch", None),
            P("exp", "batch"),
            P("exp", "batch", None),
            P("exp", "batch"),
        ),
        check_vma=False,
    )
```
